32 devices in a mesh: groups: 2 (over x), band: 16 (over z, y, core).
Axes of the slice: x: 2, y: 2, z: 4, core: 2. Of those that a mesh axis runs over, the one named last changes fastest.
Arguments:
- orbitals: float32 [32, 96, 9216], P(('groups', 'band')), parts along dimension 0, may hold values from -6 to 6
Outputs:
- exchange_term: float32 [32, 96, 9216], P(('groups', 'band')), parts along dimension 0
The draws below stay inside these ranges and needn't reach their ends.
There are 2 independent parts, one for each index of `groups`. The reference program is written for one: setup_inputs(seed, part) draws one part's arguments, and reference() takes and returns one part's arrays. A program takes and returns all parts, laid end to end along the dimension named above; each array names one. Nothing has to cross between parts.
All inputs are finite; a program needn't handle non-finite values.
Results may differ from the reference program's by a relative error of at most 0.0003.
Values sent between devices are 32-bit elements; how exact they have to be, the bound alone decides.
No kernel may reach another device: no remote copies, remote signals or barrier semaphores. Data moves between devices by JAX's collectives and lax.ppermute only.
A program may use at most 128 MiB of HBM per device.

```python
import math
import jax
import jax.numpy as jnp
from jax import lax

NG = 96
B_DEV = 1
OFFSET = 5
NBANDS = 16
N_BAND = 16


def steps_of(own_key, dims, cuts, least, high):
    gain = 1.0
    for dim, shards_of in cuts:
        draws = jax.random.uniform(jax.random.fold_in(jax.random.fold_in(own_key, 6), dim), (shards_of,), jnp.float32, least / len(cuts), high / len(cuts))
        gain = gain * jnp.repeat(jnp.exp(draws), dims[dim] // shards_of).reshape((-1,) + (1,) * (len(dims) - 1 - dim))
    return gain


def bell_draw(key, shape, width, limit, pieces=(), kind=jnp.bfloat16):
    drawn = width * jax.random.normal(key, shape, jnp.float32)
    if pieces:
        drawn = drawn * steps_of(key, shape, pieces, -0.22, 0.18)
    return jnp.clip(drawn, -limit, limit).astype(kind)


def setup_inputs(seed: int = 0, part: int = 0) -> dict:
    key_list = jax.random.split(jax.random.key(seed), 2)
    part_splits = jax.random.split(jax.random.fold_in(key_list[1], part), 2)
    return {
        "orbitals": bell_draw(part_splits[0], (NBANDS, NG, NG * NG), 0.45, 6.0, ((0, 16),), jnp.float32),
    }


screening = 5.44


def screened_kernel(points):
    signed = jnp.arange(points, dtype=jnp.int32)
    signed = jnp.where(signed >= points // 2, signed - points, signed)
    wavenumber = signed.astype(jnp.float32) * (2.0 * math.pi / points)
    squared = wavenumber[:, None, None] ** 2 + wavenumber[None, :, None] ** 2 + wavenumber[None, None, :] ** 2
    screen_rate = screening / points
    finite = jnp.where(squared > 0.0, squared, 1.0)
    screened = 4.0 * math.pi / finite * (-jnp.expm1(-finite / (4.0 * screen_rate * screen_rate)))
    return jnp.where(squared > 0.0, screened, math.pi / (screen_rate * screen_rate))


def reference(orbitals):
    kernel = screened_kernel(NG)
    blocks = orbitals.reshape(N_BAND, B_DEV, NG, NG, NG)

    def one_device(device):
        resident = blocks[device]
        lower_block = blocks[(device - OFFSET) % N_BAND]
        upper_block = blocks[(device + OFFSET) % N_BAND]
        visitors = jnp.concatenate([lower_block, upper_block], 0)

        def one_visitor(visitor):
            density = resident * visitor[None]
            spectrum = jnp.fft.fftn(density, axes=(1, 2, 3))
            potential = jnp.real(jnp.fft.ifftn(spectrum * kernel, axes=(1, 2, 3)))
            return visitor[None] * potential

        return -jnp.sum(lax.map(one_visitor, visitors), 0)

    result = lax.map(one_device, jnp.arange(N_BAND, dtype=jnp.int32))
    return result.reshape(NBANDS, NG, NG * NG)
```

```python
import functools
import math

import jax
import jax.numpy as jnp
import numpy as np
from jax import lax
from jax.experimental import pallas as pl
from jax.experimental.pallas import tpu as pltpu
from jax.sharding import PartitionSpec as P

OFFSET = 5
screening = 5.44
LANES = 128
X_STEPS = 6
PLANE_STEPS = 6


def from_behind(value, axis, by):
    count = lax.axis_size(axis)
    return lax.ppermute(value, axis, [(i, (i + by) % count) for i in range(count)])


def screened_kernel(points):
    signed = jnp.arange(points, dtype=jnp.int32)
    signed = jnp.where(signed >= points // 2, signed - points, signed)
    wavenumber = signed.astype(jnp.float32) * (2.0 * math.pi / points)
    squared = (
        wavenumber[:, None, None] ** 2
        + wavenumber[None, :, None] ** 2
        + wavenumber[None, None, :] ** 2
    )
    screen_rate = screening / points
    finite = jnp.where(squared > 0.0, squared, 1.0)
    screened = 4.0 * math.pi / finite * -jnp.expm1(-finite / (4.0 * screen_rate * screen_rate))
    kernel = jnp.where(squared > 0.0, screened, math.pi / (screen_rate * screen_rate))
    kernel = kernel / float(points * points * points)
    return jnp.pad(kernel, ((0, 0), (0, 0), (0, LANES - points)))


def hartley_tables(points):
    counter = np.arange(points)
    angles = 2.0 * np.pi * (counter[:, None] * counter[None, :] % points) / points
    table = np.cos(angles) + np.sin(angles)
    high = table.astype(jnp.bfloat16)
    low = (table - high.astype(np.float64)).astype(jnp.bfloat16)
    left = np.zeros((2 * points, 2 * points), jnp.bfloat16)
    left[:points, :points] = high
    left[:points, points:] = high
    left[points:, :points] = low
    right = np.zeros((2 * LANES, 2 * LANES), jnp.bfloat16)
    right[:points, :points] = high
    right[:points, LANES:LANES + points] = low
    right[LANES:LANES + points, :points] = high
    return jnp.asarray(left), jnp.asarray(right)


def two_terms(value, axis):
    high = value.astype(jnp.bfloat16)
    low = (value - high.astype(jnp.float32)).astype(jnp.bfloat16)
    return jnp.concatenate([high, low], axis)


def from_left(left, value):
    half = value.shape[0]
    out = jnp.dot(left, two_terms(value, 0), preferred_element_type=jnp.float32)
    return out[:half] + out[half:]


def from_right(value, right):
    out = jnp.dot(two_terms(value, 1), right, preferred_element_type=jnp.float32)
    return out[:, :LANES] + out[:, LANES:]


def pair_body(points, have_sum, both, *refs):
    refs = list(refs)
    a_ref, b_ref, kernel_ref, left_ref, right_ref = refs[:5]
    refs = refs[5:]
    sum_ref = refs.pop(0) if have_sum else None
    for_a_ref = refs.pop(0)
    for_b_ref = refs.pop(0) if both else None
    (held,) = refs
    step = pl.program_id(0)
    group = 4 * points
    columns = a_ref.shape[1]
    groups = columns // group
    rows_of = columns // points

    @pl.when(step < X_STEPS)
    def forward_x():
        left = left_ref[...]
        for part in range(groups):
            span = pl.ds(part * group, group)
            density = a_ref[:, span] * b_ref[:, span]
            spectrum = from_left(left, density)
            for q in range(4):
                row = step * rows_of + part * 4 + q
                piece = spectrum[:, q * points:(q + 1) * points]
                piece = jnp.concatenate([piece, jnp.zeros((points, LANES - points), jnp.float32)], 1)
                held[pl.ds(row, points, stride=points), :] = piece

    @pl.when((step >= X_STEPS) & (step < X_STEPS + PLANE_STEPS))
    def planes():
        left = left_ref[...]
        right = right_ref[...]
        per_step = points // PLANE_STEPS
        first = (step - X_STEPS) * per_step

        def two_planes(index, carry):
            start = pl.multiple_of((first + 2 * index) * points, points)
            block = held[pl.ds(start, 2 * points), :]
            block = from_right(block, right)
            wide = jnp.concatenate([block[:points], block[points:]], 1)
            wide = from_left(left, wide)
            scale = kernel_ref[pl.ds(2 * index, 2)]
            wide = wide * jnp.concatenate([scale[0], scale[1]], 1)
            wide = from_left(left, wide)
            block = jnp.concatenate([wide[:, :LANES], wide[:, LANES:]], 0)
            held[pl.ds(start, 2 * points), :] = from_right(block, right)
            return carry

        lax.fori_loop(0, per_step // 2, two_planes, 0, unroll=2)

    @pl.when(step >= X_STEPS + PLANE_STEPS)
    def inverse_x():
        left = left_ref[...]
        for part in range(groups):
            span = pl.ds(part * group, group)
            pieces = []
            for q in range(4):
                row = (step - X_STEPS - PLANE_STEPS) * rows_of + part * 4 + q
                pieces.append(held[pl.ds(row, points, stride=points), :][:, :points])
            potential = from_left(left, jnp.concatenate(pieces, 1))
            for_a = -b_ref[:, span] * potential
            if have_sum:
                for_a = for_a + sum_ref[:, span]
            for_a_ref[:, span] = for_a
            if both:
                for_b_ref[:, span] = -a_ref[:, span] * potential


def pair_terms(a, b, kernel, tables, running=None, both=False):
    points, plane = a.shape
    columns = plane // X_STEPS
    late = X_STEPS + PLANE_STEPS

    def ends(i):
        return (0, jnp.where(i < X_STEPS, i, jnp.where(i < late, X_STEPS - 1, i - late)))

    def tail(i):
        return (0, jnp.maximum(i - late, 0))

    def middle(i):
        return (jnp.clip(i - X_STEPS, 0, PLANE_STEPS - 1), 0, 0)

    wide = pl.BlockSpec((points, columns), ends)
    in_specs = [
        wide,
        wide,
        pl.BlockSpec((points // PLANE_STEPS, points, LANES), middle),
        pl.BlockSpec(tables[0].shape, lambda i: (0, 0)),
        pl.BlockSpec(tables[1].shape, lambda i: (0, 0)),
    ]
    operands = [a, b, kernel, *tables]
    if running is not None:
        in_specs.append(pl.BlockSpec((points, columns), tail))
        operands.append(running)
    n_out = 2 if both else 1
    out = pl.pallas_call(
        functools.partial(pair_body, points, running is not None, both),
        grid=(2 * X_STEPS + PLANE_STEPS,),
        in_specs=in_specs,
        out_specs=[pl.BlockSpec((points, columns), tail)] * n_out,
        out_shape=[jax.ShapeDtypeStruct((points, plane), jnp.float32)] * n_out,
        scratch_shapes=[pltpu.VMEM((points * points, LANES), jnp.float32)],
        compiler_params=pltpu.CompilerParams(vmem_limit_bytes=40 * 2**20),
        cost_estimate=pl.CostEstimate(
            flops=40_000_000_000, bytes_accessed=20_000_000, transcendentals=0
        ),
        name="pair_terms",
    )(*operands)
    return out if both else out[0]


def local(orbitals):
    bands, points, plane = orbitals.shape
    resident = orbitals[0]
    lower = from_behind(orbitals, "band", OFFSET)[0]
    upper = from_behind(orbitals, "band", -OFFSET)[0]
    tables = hartley_tables(points)
    kernel = screened_kernel(points)
    total = pair_terms(resident, lower, kernel, tables)
    total = pair_terms(resident, upper, kernel, tables, running=total)
    return total[None]


def solution(mesh):
    return jax.shard_map(
        local,
        mesh=mesh,
        in_specs=(P(("groups", "band"), None, None),),
        out_specs=P(("groups", "band"), None, None),
        check_vma=False,
    )
```

```python
import functools
import math

import jax
import jax.numpy as jnp
import numpy as np
from jax import lax
from jax.experimental import pallas as pl
from jax.experimental.pallas import tpu as pltpu
from jax.sharding import PartitionSpec as P

OFFSET = 5
screening = 5.44
LANES = 128
X_STEPS = 6
PLANE_STEPS = 6


def from_behind(value, axis, by):
    count = lax.axis_size(axis)
    return lax.ppermute(value, axis, [(i, (i + by) % count) for i in range(count)])


def screened_kernel(points):
    signed = jnp.arange(points, dtype=jnp.int32)
    signed = jnp.where(signed >= points // 2, signed - points, signed)
    wavenumber = signed.astype(jnp.float32) * (2.0 * math.pi / points)
    squared = (
        wavenumber[:, None, None] ** 2
        + wavenumber[None, :, None] ** 2
        + wavenumber[None, None, :] ** 2
    )
    screen_rate = screening / points
    finite = jnp.where(squared > 0.0, squared, 1.0)
    screened = 4.0 * math.pi / finite * -jnp.expm1(-finite / (4.0 * screen_rate * screen_rate))
    kernel = jnp.where(squared > 0.0, screened, math.pi / (screen_rate * screen_rate))
    kernel = kernel / float(points * points * points)
    return jnp.pad(kernel, ((0, 0), (0, 0), (0, LANES - points)))


def hartley_tables(points):
    counter = np.arange(points)
    angles = 2.0 * np.pi * (counter[:, None] * counter[None, :] % points) / points
    table = np.cos(angles) + np.sin(angles)
    high = table.astype(jnp.bfloat16)
    low = (table - high.astype(np.float64)).astype(jnp.bfloat16)
    left = np.zeros((2 * points, 2 * points), jnp.bfloat16)
    left[:points, :points] = high
    left[:points, points:] = high
    left[points:, :points] = low
    right = np.zeros((2 * LANES, 2 * LANES), jnp.bfloat16)
    right[:points, :points] = high
    right[:points, LANES:LANES + points] = low
    right[LANES:LANES + points, :points] = high
    return jnp.asarray(left), jnp.asarray(right)


def two_terms(value, axis):
    high = value.astype(jnp.bfloat16)
    low = (value - high.astype(jnp.float32)).astype(jnp.bfloat16)
    return jnp.concatenate([high, low], axis)


def from_left(left, value):
    half = value.shape[0]
    out = jnp.dot(left, two_terms(value, 0), preferred_element_type=jnp.float32)
    return out[:half] + out[half:]


def from_right(value, right):
    out = jnp.dot(two_terms(value, 1), right, preferred_element_type=jnp.float32)
    return out[:, :LANES] + out[:, LANES:]


def pair_body(points, have_sum, both, *refs):
    refs = list(refs)
    a_ref, b_ref, kernel_ref, left_ref, right_ref = refs[:5]
    refs = refs[5:]
    sum_ref = refs.pop(0) if have_sum else None
    for_a_ref = refs.pop(0)
    for_b_ref = refs.pop(0) if both else None
    (held,) = refs
    step = pl.program_id(0)
    ys = a_ref.shape[1] // points
    per_step = points // PLANE_STEPS

    def lanes_apart(block):
        gap = jnp.zeros((points, LANES - points), jnp.float32)
        rows = [
            jnp.concatenate([block[:, q * points:(q + 1) * points], gap], 1) for q in range(ys)
        ]
        return jnp.swapaxes(jnp.stack(rows, 0), 0, 1)

    def lanes_together(block):
        block = jnp.swapaxes(block, 0, 1)
        return jnp.concatenate([block[q][:, :points] for q in range(ys)], 1)

    def side_by_side(block):
        return jnp.concatenate([block[i] for i in range(per_step)], 1)

    @pl.when(step < X_STEPS)
    def forward_x():
        spectrum = from_left(left_ref[...], a_ref[...] * b_ref[...])
        start = pl.multiple_of(step * ys, ys)
        held[:, pl.ds(start, ys), :] = lanes_apart(spectrum)

    @pl.when((step >= X_STEPS) & (step < X_STEPS + PLANE_STEPS))
    def planes():
        left = left_ref[...]
        right = right_ref[...]
        first = (step - X_STEPS) * per_step
        block = held[pl.ds(first, per_step)].reshape(per_step * points, LANES)
        block = from_right(block, right).reshape(per_step, points, LANES)
        wide = from_left(left, side_by_side(block))
        wide = from_left(left, wide * side_by_side(kernel_ref[...]))
        block = jnp.concatenate(
            [wide[:, i * LANES:(i + 1) * LANES] for i in range(per_step)], 0
        )
        block = from_right(block, right)
        held[pl.ds(first, per_step)] = block.reshape(per_step, points, LANES)

    @pl.when(step >= X_STEPS + PLANE_STEPS)
    def inverse_x():
        start = pl.multiple_of((step - X_STEPS - PLANE_STEPS) * ys, ys)
        block = lanes_together(held[:, pl.ds(start, ys), :])
        potential = from_left(left_ref[...], block)
        for_a = -b_ref[...] * potential
        if have_sum:
            for_a = for_a + sum_ref[...]
        for_a_ref[...] = for_a
        if both:
            for_b_ref[...] = -a_ref[...] * potential


def pair_terms(a, b, kernel, tables, running=None, both=False):
    points, plane = a.shape
    columns = plane // X_STEPS
    late = X_STEPS + PLANE_STEPS

    def ends(i):
        return (0, jnp.where(i < X_STEPS, i, jnp.where(i < late, X_STEPS - 1, i - late)))

    def tail(i):
        return (0, jnp.maximum(i - late, 0))

    def middle(i):
        return (jnp.clip(i - X_STEPS, 0, PLANE_STEPS - 1), 0, 0)

    wide = pl.BlockSpec((points, columns), ends)
    in_specs = [
        wide,
        wide,
        pl.BlockSpec((points // PLANE_STEPS, points, LANES), middle),
        pl.BlockSpec(tables[0].shape, lambda i: (0, 0)),
        pl.BlockSpec(tables[1].shape, lambda i: (0, 0)),
    ]
    operands = [a, b, kernel, *tables]
    if running is not None:
        in_specs.append(pl.BlockSpec((points, columns), tail))
        operands.append(running)
    n_out = 2 if both else 1
    out = pl.pallas_call(
        functools.partial(pair_body, points, running is not None, both),
        grid=(2 * X_STEPS + PLANE_STEPS,),
        in_specs=in_specs,
        out_specs=[pl.BlockSpec((points, columns), tail)] * n_out,
        out_shape=[jax.ShapeDtypeStruct((points, plane), jnp.float32)] * n_out,
        scratch_shapes=[pltpu.VMEM((points, points, LANES), jnp.float32)],
        compiler_params=pltpu.CompilerParams(vmem_limit_bytes=40 * 2**20),
        cost_estimate=pl.CostEstimate(
            flops=40_000_000_000, bytes_accessed=20_000_000, transcendentals=0
        ),
        name="pair_terms",
    )(*operands)
    return out if both else out[0]


def local(orbitals):
    bands, points, plane = orbitals.shape
    resident = orbitals[0]
    lower = from_behind(orbitals, "band", OFFSET)[0]
    upper = from_behind(orbitals, "band", -OFFSET)[0]
    tables = hartley_tables(points)
    kernel = screened_kernel(points)
    total = pair_terms(resident, lower, kernel, tables)
    total = pair_terms(resident, upper, kernel, tables, running=total)
    return total[None]


def solution(mesh):
    return jax.shard_map(
        local,
        mesh=mesh,
        in_specs=(P(("groups", "band"), None, None),),
        out_specs=P(("groups", "band"), None, None),
        check_vma=False,
    )
```

```python
import functools
import math

import jax
import jax.numpy as jnp
import numpy as np
from jax import lax
from jax.experimental import pallas as pl
from jax.experimental.pallas import tpu as pltpu
from jax.sharding import PartitionSpec as P

OFFSET = 5
screening = 5.44
LANES = 128
X_STEPS = 6
PLANE_STEPS = 6


def from_behind(value, axis, by):
    count = lax.axis_size(axis)
    return lax.ppermute(value, axis, [(i, (i + by) % count) for i in range(count)])


def screened_kernel(points):
    signed = jnp.arange(points, dtype=jnp.int32)
    signed = jnp.where(signed >= points // 2, signed - points, signed)
    wavenumber = signed.astype(jnp.float32) * (2.0 * math.pi / points)
    squared = (
        wavenumber[:, None, None] ** 2
        + wavenumber[None, :, None] ** 2
        + wavenumber[None, None, :] ** 2
    )
    screen_rate = screening / points
    finite = jnp.where(squared > 0.0, squared, 1.0)
    screened = 4.0 * math.pi / finite * -jnp.expm1(-finite / (4.0 * screen_rate * screen_rate))
    kernel = jnp.where(squared > 0.0, screened, math.pi / (screen_rate * screen_rate))
    kernel = kernel / float(points * points * points)
    return jnp.pad(kernel, ((0, 0), (0, 0), (0, LANES - points)))


def hartley_tables(points):
    counter = np.arange(points)
    angles = 2.0 * np.pi * (counter[:, None] * counter[None, :] % points) / points
    table = np.cos(angles) + np.sin(angles)
    high = table.astype(jnp.bfloat16)
    low = (table - high.astype(np.float64)).astype(jnp.bfloat16)
    left = np.zeros((2 * points, 2 * points), jnp.bfloat16)
    left[:points, :points] = high
    left[:points, points:] = high
    left[points:, :points] = low
    right = np.zeros((2 * LANES, 2 * LANES), jnp.bfloat16)
    right[:points, :points] = high
    right[:points, LANES:LANES + points] = low
    right[LANES:LANES + points, :points] = high
    return jnp.asarray(left), jnp.asarray(right)


def two_terms(value, axis):
    high = value.astype(jnp.bfloat16)
    low = (value - high.astype(jnp.float32)).astype(jnp.bfloat16)
    return jnp.concatenate([high, low], axis)


def from_left(left, value):
    half = value.shape[0]
    out = jnp.dot(left, two_terms(value, 0), preferred_element_type=jnp.float32)
    return out[:half] + out[half:]


def from_right(value, right):
    out = jnp.dot(two_terms(value, 1), right, preferred_element_type=jnp.float32)
    return out[:, :LANES] + out[:, LANES:]


def pair_body(points, has, *refs):
    refs = list(refs)
    a_ref, b_ref = refs.pop(0), refs.pop(0)
    more_ref = refs.pop(0) if "more" in has else None
    kernel_ref, left_ref, right_ref = refs.pop(0), refs.pop(0), refs.pop(0)
    sum_a_ref = refs.pop(0) if "sum_a" in has else None
    sum_b_ref = refs.pop(0) if "sum_b" in has else None
    for_a_ref = refs.pop(0)
    for_b_ref = refs.pop(0) if "for_b" in has else None
    (held,) = refs
    step = pl.program_id(0)
    ys = a_ref.shape[1] // points
    per_step = points // PLANE_STEPS

    def visitor():
        return b_ref[...] if more_ref is None else b_ref[...] + more_ref[...]

    def lanes_apart(block):
        gap = jnp.zeros((points, LANES - points), jnp.float32)
        rows = [
            jnp.concatenate([block[:, q * points:(q + 1) * points], gap], 1) for q in range(ys)
        ]
        return jnp.swapaxes(jnp.stack(rows, 0), 0, 1)

    def lanes_together(block):
        block = jnp.swapaxes(block, 0, 1)
        return jnp.concatenate([block[q][:, :points] for q in range(ys)], 1)

    def side_by_side(block):
        return jnp.concatenate([block[i] for i in range(per_step)], 1)

    @pl.when(step < X_STEPS)
    def forward_x():
        spectrum = from_left(left_ref[...], a_ref[...] * visitor())
        start = pl.multiple_of(step * ys, ys)
        held[:, pl.ds(start, ys), :] = lanes_apart(spectrum)

    @pl.when((step >= X_STEPS) & (step < X_STEPS + PLANE_STEPS))
    def planes():
        left = left_ref[...]
        right = right_ref[...]
        first = (step - X_STEPS) * per_step
        block = held[pl.ds(first, per_step)].reshape(per_step * points, LANES)
        block = from_right(block, right).reshape(per_step, points, LANES)
        wide = from_left(left, side_by_side(block))
        wide = from_left(left, wide * side_by_side(kernel_ref[...]))
        block = jnp.concatenate(
            [wide[:, i * LANES:(i + 1) * LANES] for i in range(per_step)], 0
        )
        block = from_right(block, right)
        held[pl.ds(first, per_step)] = block.reshape(per_step, points, LANES)

    @pl.when(step >= X_STEPS + PLANE_STEPS)
    def inverse_x():
        start = pl.multiple_of((step - X_STEPS - PLANE_STEPS) * ys, ys)
        block = lanes_together(held[:, pl.ds(start, ys), :])
        potential = from_left(left_ref[...], block)
        for_a = visitor() * potential
        for_a_ref[...] = -for_a if sum_a_ref is None else sum_a_ref[...] - for_a
        if for_b_ref is not None:
            for_b = a_ref[...] * potential
            for_b_ref[...] = -for_b if sum_b_ref is None else sum_b_ref[...] - for_b


def pair_terms(a, b, constants, more=None, sum_a=None, sum_b=None, for_b=False):
    points, plane = a.shape
    columns = plane // X_STEPS
    late = X_STEPS + PLANE_STEPS
    kernel, left, right = constants

    def ends(i):
        return (0, jnp.where(i < X_STEPS, i, jnp.where(i < late, X_STEPS - 1, i - late)))

    def tail(i):
        return (0, jnp.maximum(i - late, 0))

    def middle(i):
        return (jnp.clip(i - X_STEPS, 0, PLANE_STEPS - 1), 0, 0)

    def whole(i):
        return (0, 0)

    at_ends = pl.BlockSpec((points, columns), ends)
    at_tail = pl.BlockSpec((points, columns), tail)
    operands = [(None, a, at_ends), (None, b, at_ends), ("more", more, at_ends)]
    operands.append((None, kernel, pl.BlockSpec((points // PLANE_STEPS, points, LANES), middle)))
    operands.append((None, left, pl.BlockSpec(left.shape, whole)))
    operands.append((None, right, pl.BlockSpec(right.shape, whole)))
    operands += [("sum_a", sum_a, at_tail), ("sum_b", sum_b, at_tail)]
    operands = [entry for entry in operands if entry[1] is not None]
    has = [name for name, value, spec in operands if name] + ["for_b"] * for_b
    n_out = 2 if for_b else 1
    out = pl.pallas_call(
        functools.partial(pair_body, points, has),
        grid=(2 * X_STEPS + PLANE_STEPS,),
        in_specs=[spec for name, value, spec in operands],
        out_specs=[at_tail] * n_out,
        out_shape=[jax.ShapeDtypeStruct((points, plane), jnp.float32)] * n_out,
        scratch_shapes=[pltpu.VMEM((points, points, LANES), jnp.float32)],
        compiler_params=pltpu.CompilerParams(vmem_limit_bytes=60 * 2**20),
        cost_estimate=pl.CostEstimate(
            flops=16_000_000_000, bytes_accessed=20_000_000, transcendentals=0
        ),
        name="pair_terms",
    )(*[value for name, value, spec in operands])
    return out if for_b else out[0]


def corner_body(block_ref, kernel_ref, corner_ref, sem):
    copy = pltpu.make_async_copy(block_ref.at[pl.ds(0, 8), pl.ds(0, LANES)], corner_ref, sem)
    copy.start()
    copy.wait()


def corner(block, kernel):
    anywhere = pl.BlockSpec(memory_space=pl.ANY)
    return pl.pallas_call(
        corner_body,
        in_specs=[anywhere, anywhere],
        out_specs=pl.BlockSpec(memory_space=pltpu.VMEM),
        out_shape=jax.ShapeDtypeStruct((8, LANES), block.dtype),
        scratch_shapes=[pltpu.SemaphoreType.DMA],
        compiler_params=pltpu.CompilerParams(vmem_limit_bytes=60 * 2**20),
        name="corner",
    )(block, kernel)


def after_body(token_ref, left_ref, block_ref, new_left_ref, new_block_ref, sem):
    copy = pltpu.make_async_copy(block_ref, new_block_ref, sem)
    copy.start()
    new_left_ref[...] = left_ref[...]
    copy.wait()


def after(token, left, block):
    in_vmem = pl.BlockSpec(memory_space=pltpu.VMEM)
    anywhere = pl.BlockSpec(memory_space=pl.ANY)
    return pl.pallas_call(
        after_body,
        in_specs=[in_vmem, in_vmem, anywhere],
        out_specs=[in_vmem, anywhere],
        out_shape=[
            jax.ShapeDtypeStruct(left.shape, left.dtype),
            jax.ShapeDtypeStruct(block.shape, block.dtype),
        ],
        scratch_shapes=[pltpu.SemaphoreType.DMA],
        compiler_params=pltpu.CompilerParams(vmem_limit_bytes=60 * 2**20),
        name="after",
    )(token, left, block)


def both_halves(*pairs):
    return list(pairs) + [(15 - source, 15 - target) for source, target in pairs]


CROSSING = both_halves((3, 14), (4, 9))
PARTNERS = both_halves((8, 14), (15, 9))
TURN_FIRST = both_halves((9, 11), (14, 12))
TURN_SECOND = both_halves((11, 14), (12, 9))
ARRIVED = both_halves((14, 2), (9, 5))
SINGLES = both_halves((5, 10), (2, 13))
BESIDE = both_halves((13, 14), (10, 9))
HOME_ACROSS = both_halves((9, 4), (14, 3))
HOME_FAR = both_halves((9, 15), (14, 8))
HOME_BESIDE = both_halves((9, 10), (14, 13))


def sixteen_bands(orbitals, constants):
    def send(value, pairs):
        return lax.ppermute(value, "band", pairs)

    own = orbitals[0]
    crossed = send(orbitals, CROSSING)[0]
    partner = send(orbitals, PARTNERS)[0]
    turned = send(orbitals, TURN_FIRST)
    kernel, left, right = constants
    token = send(corner(crossed, kernel)[None], ARRIVED)
    left, held_back = after(token[0], left, orbitals)
    constants = (kernel, left, right)
    single = send(held_back, SINGLES)[0]
    beside = send(held_back, BESIDE)[0]
    turned = send(turned, TURN_SECOND)[0]

    partner_sum, crossed_sum = pair_terms(partner, crossed, constants, for_b=True)
    own_sum, crossed_sum = pair_terms(own, crossed, constants, sum_b=crossed_sum, for_b=True)
    home = send(crossed_sum[None], HOME_ACROSS)[0]
    partner_sum, beside_sum = pair_terms(partner, beside, constants, sum_a=partner_sum, for_b=True)
    home_far = send(partner_sum[None], HOME_FAR)[0]
    home_beside = send(beside_sum[None], HOME_BESIDE)[0]
    own_sum = pair_terms(own, single, constants, more=turned, sum_a=own_sum)
    return (own_sum + home + home_beside + home_far)[None]


def any_bands(orbitals, constants):
    own = orbitals[0]
    lower = from_behind(orbitals, "band", OFFSET)[0]
    upper = from_behind(orbitals, "band", -OFFSET)[0]
    total = pair_terms(own, lower, constants)
    return pair_terms(own, upper, constants, sum_a=total)[None]


def local(bands, orbitals):
    points = orbitals.shape[1]
    constants = (screened_kernel(points), *hartley_tables(points))
    if bands == 16:
        return sixteen_bands(orbitals, constants)
    return any_bands(orbitals, constants)


def solution(mesh):
    return jax.shard_map(
        functools.partial(local, mesh.shape["band"]),
        mesh=mesh,
        in_specs=(P(("groups", "band"), None, None),),
        out_specs=P(("groups", "band"), None, None),
        check_vma=False,
    )
```

```python
import functools
import math

import jax
import jax.numpy as jnp
import numpy as np
from jax import lax
from jax.experimental import pallas as pl
from jax.experimental.pallas import tpu as pltpu
from jax.sharding import PartitionSpec as P

OFFSET = 5
screening = 5.44
LANES = 128
X_STEPS = 6
PLANE_STEPS = 6


def from_behind(value, axis, by):
    count = lax.axis_size(axis)
    return lax.ppermute(value, axis, [(i, (i + by) % count) for i in range(count)])


def screened_kernel(points):
    signed = jnp.arange(points, dtype=jnp.int32)
    signed = jnp.where(signed >= points // 2, signed - points, signed)
    wavenumber = signed.astype(jnp.float32) * (2.0 * math.pi / points)
    squared = (
        wavenumber[:, None, None] ** 2
        + wavenumber[None, :, None] ** 2
        + wavenumber[None, None, :] ** 2
    )
    screen_rate = screening / points
    finite = jnp.where(squared > 0.0, squared, 1.0)
    screened = 4.0 * math.pi / finite * -jnp.expm1(-finite / (4.0 * screen_rate * screen_rate))
    kernel = jnp.where(squared > 0.0, screened, math.pi / (screen_rate * screen_rate))
    kernel = kernel / float(points * points * points)
    return jnp.pad(kernel, ((0, 0), (0, 0), (0, LANES - points)))


def hartley_tables(points):
    counter = np.arange(points)
    angles = 2.0 * np.pi * (counter[:, None] * counter[None, :] % points) / points
    table = np.cos(angles) + np.sin(angles)
    high = table.astype(jnp.bfloat16)
    low = (table - high.astype(np.float64)).astype(jnp.bfloat16)
    left = np.concatenate([high, high, low], 1)
    right = np.zeros((2 * LANES, 2 * LANES), jnp.bfloat16)
    right[:points, :points] = high
    right[:points, LANES:LANES + points] = low
    right[LANES:LANES + points, :points] = high
    return jnp.asarray(left), jnp.asarray(right)


def two_terms(value):
    high = value.astype(jnp.bfloat16)
    low = (value - high.astype(jnp.float32)).astype(jnp.bfloat16)
    return high, low


def from_left(left, value):
    high, low = two_terms(value)
    terms = jnp.concatenate([high, low, high], 0)
    return jnp.dot(left, terms, preferred_element_type=jnp.float32)


def from_right(value, right):
    out = jnp.dot(jnp.concatenate(two_terms(value), 1), right, preferred_element_type=jnp.float32)
    return out[:, :LANES] + out[:, LANES:]


def pair_body(points, has, *refs):
    refs = list(refs)
    names = ["a", "b"] + [name for name in ("more", "sum_a", "sum_b") if name in has]
    far = {name: refs.pop(0) for name in names}
    kernel_ref, left_ref, right_ref = refs.pop(0), refs.pop(0), refs.pop(0)
    for_a_ref = refs.pop(0)
    for_b_ref = refs.pop(0) if "for_b" in has else None
    held, near, sems = refs
    step = pl.program_id(0)
    columns = for_a_ref.shape[1]
    ys = columns // points
    per_step = points // PLANE_STEPS
    late = X_STEPS + PLANE_STEPS

    def fetch(name, chunk):
        place = names.index(name)
        span = pl.ds(pl.multiple_of(chunk * columns, columns), columns)
        return pltpu.make_async_copy(
            far[name].at[:, span], near.at[place, :, span], sems.at[place, chunk]
        )

    def here(name, chunk):
        span = pl.ds(pl.multiple_of(chunk * columns, columns), columns)
        return near[names.index(name), :, span]

    def visitor(chunk):
        block = here("b", chunk)
        return block + here("more", chunk) if "more" in has else block

    ends = [name for name in names if not name.startswith("sum")]
    sums = [name for name in names if name.startswith("sum")]

    @pl.when(step == 0)
    def start_ends():
        for chunk in range(X_STEPS):
            for name in ends:
                fetch(name, chunk).start()

    if sums:
        @pl.when(step == X_STEPS)
        def start_sums():
            for chunk in range(X_STEPS):
                for name in sums:
                    fetch(name, chunk).start()

    def lanes_apart(block):
        gap = jnp.zeros((points, LANES - points), jnp.float32)
        rows = [
            jnp.concatenate([block[:, q * points:(q + 1) * points], gap], 1) for q in range(ys)
        ]
        return jnp.swapaxes(jnp.stack(rows, 0), 0, 1)

    def lanes_together(block):
        block = jnp.swapaxes(block, 0, 1)
        return jnp.concatenate([block[q][:, :points] for q in range(ys)], 1)

    def side_by_side(block):
        return jnp.concatenate([block[i] for i in range(per_step)], 1)

    @pl.when(step < X_STEPS)
    def forward_x():
        for name in ends:
            fetch(name, step).wait()
        spectrum = from_left(left_ref[...], here("a", step) * visitor(step))
        start = pl.multiple_of(step * ys, ys)
        held[:, pl.ds(start, ys), :] = lanes_apart(spectrum)

    @pl.when((step >= X_STEPS) & (step < late))
    def planes():
        left = left_ref[...]
        right = right_ref[...]
        first = (step - X_STEPS) * per_step
        block = held[pl.ds(first, per_step)].reshape(per_step * points, LANES)
        block = from_right(block, right).reshape(per_step, points, LANES)
        wide = from_left(left, side_by_side(block))
        wide = from_left(left, wide * side_by_side(kernel_ref[...]))
        block = jnp.concatenate(
            [wide[:, i * LANES:(i + 1) * LANES] for i in range(per_step)], 0
        )
        block = from_right(block, right)
        held[pl.ds(first, per_step)] = block.reshape(per_step, points, LANES)

    @pl.when(step >= late)
    def inverse_x():
        chunk = step - late
        start = pl.multiple_of(chunk * ys, ys)
        for name in sums:
            fetch(name, chunk).wait()
        block = lanes_together(held[:, pl.ds(start, ys), :])
        potential = from_left(left_ref[...], block)
        for_a = visitor(chunk) * potential
        for_a_ref[...] = here("sum_a", chunk) - for_a if "sum_a" in has else -for_a
        if for_b_ref is not None:
            for_b = here("a", chunk) * potential
            for_b_ref[...] = here("sum_b", chunk) - for_b if "sum_b" in has else -for_b


def pair_terms(a, b, constants, more=None, sum_a=None, sum_b=None, for_b=False):
    points, plane = a.shape
    columns = plane // X_STEPS
    late = X_STEPS + PLANE_STEPS
    kernel, left, right = constants

    def tail(i):
        return (0, jnp.maximum(i - late, 0))

    def middle(i):
        return (jnp.clip(i - X_STEPS, 0, PLANE_STEPS - 1), 0, 0)

    def whole(i):
        return (0, 0)

    at_tail = pl.BlockSpec((points, columns), tail)
    optional = {"more": more, "sum_a": sum_a, "sum_b": sum_b}
    optional = {name: value for name, value in optional.items() if value is not None}
    blocks = [a, b, *optional.values()]
    has = list(optional) + ["for_b"] * for_b
    n_out = 2 if for_b else 1
    out = pl.pallas_call(
        functools.partial(pair_body, points, has),
        grid=(2 * X_STEPS + PLANE_STEPS,),
        in_specs=[pl.BlockSpec(memory_space=pl.ANY)] * len(blocks)
        + [
            pl.BlockSpec((points // PLANE_STEPS, points, LANES), middle),
            pl.BlockSpec(left.shape, whole),
            pl.BlockSpec(right.shape, whole),
        ],
        out_specs=[at_tail] * n_out,
        out_shape=[jax.ShapeDtypeStruct((points, plane), jnp.float32)] * n_out,
        scratch_shapes=[
            pltpu.VMEM((points, points, LANES), jnp.float32),
            pltpu.VMEM((len(blocks), points, plane), jnp.float32),
            pltpu.SemaphoreType.DMA((len(blocks), X_STEPS)),
        ],
        compiler_params=pltpu.CompilerParams(vmem_limit_bytes=60 * 2**20),
        cost_estimate=pl.CostEstimate(
            flops=16_000_000_000, bytes_accessed=20_000_000, transcendentals=0
        ),
        name="pair_terms",
    )(*blocks, kernel, left, right)
    return out if for_b else out[0]


def corner_body(block_ref, kernel_ref, corner_ref, sem):
    copy = pltpu.make_async_copy(block_ref.at[pl.ds(0, 8), pl.ds(0, LANES)], corner_ref, sem)
    copy.start()
    copy.wait()


def corner(block, kernel):
    anywhere = pl.BlockSpec(memory_space=pl.ANY)
    return pl.pallas_call(
        corner_body,
        in_specs=[anywhere, anywhere],
        out_specs=pl.BlockSpec(memory_space=pltpu.VMEM),
        out_shape=jax.ShapeDtypeStruct((8, LANES), block.dtype),
        scratch_shapes=[pltpu.SemaphoreType.DMA],
        compiler_params=pltpu.CompilerParams(vmem_limit_bytes=60 * 2**20),
        name="corner",
    )(block, kernel)


def after_body(token_ref, left_ref, block_ref, new_left_ref, new_block_ref):
    new_block_ref[...] = block_ref[...]
    new_left_ref[...] = left_ref[...]


def after(token, left, block):
    points, plane = block.shape
    part = pl.BlockSpec((points, plane // X_STEPS), lambda i: (0, i))
    table = pl.BlockSpec(left.shape, lambda i: (0, 0))
    return pl.pallas_call(
        after_body,
        grid=(X_STEPS,),
        in_specs=[pl.BlockSpec(token.shape, lambda i: (0, 0)), table, part],
        out_specs=[table, part],
        out_shape=[
            jax.ShapeDtypeStruct(left.shape, left.dtype),
            jax.ShapeDtypeStruct(block.shape, block.dtype),
        ],
        compiler_params=pltpu.CompilerParams(vmem_limit_bytes=60 * 2**20),
        name="after",
    )(token, left, block)


def both_halves(*pairs):
    return list(pairs) + [(15 - source, 15 - target) for source, target in pairs]


CROSSING = both_halves((3, 14), (4, 9))
PARTNERS = both_halves((8, 14), (15, 9))
TURN_FIRST = both_halves((9, 11), (14, 12))
TURN_SECOND = both_halves((11, 14), (12, 9))
ARRIVED = both_halves((14, 2), (9, 5))
SINGLES = both_halves((5, 10), (2, 13))
BESIDE = both_halves((13, 14), (10, 9))
HOME_ACROSS = both_halves((9, 4), (14, 3))
HOME_FAR = both_halves((9, 15), (14, 8))
HOME_BESIDE = both_halves((9, 10), (14, 13))


def sixteen_bands(orbitals, constants):
    def send(value, pairs):
        return lax.ppermute(value, "band", pairs)

    own = orbitals[0]
    crossed = send(orbitals, CROSSING)[0]
    partner = send(orbitals, PARTNERS)[0]
    turned = send(orbitals, TURN_FIRST)
    kernel, left, right = constants
    token = send(corner(crossed, kernel)[None], ARRIVED)
    left, held_back = after(token[0], left, own)
    held_back = held_back[None]
    constants = (kernel, left, right)
    single = send(held_back, SINGLES)[0]
    beside = send(held_back, BESIDE)[0]
    turned = send(turned, TURN_SECOND)[0]

    partner_sum, crossed_sum = pair_terms(partner, crossed, constants, for_b=True)
    own_sum, crossed_sum = pair_terms(own, crossed, constants, sum_b=crossed_sum, for_b=True)
    home = send(crossed_sum[None], HOME_ACROSS)[0]
    partner_sum, beside_sum = pair_terms(partner, beside, constants, sum_a=partner_sum, for_b=True)
    home_far = send(partner_sum[None], HOME_FAR)[0]
    home_beside = send(beside_sum[None], HOME_BESIDE)[0]
    own_sum = pair_terms(own, single, constants, more=turned, sum_a=own_sum)
    own_sum = own_sum + home + home_beside
    return (own_sum + home_far)[None]


def any_bands(orbitals, constants):
    own = orbitals[0]
    lower = from_behind(orbitals, "band", OFFSET)[0]
    upper = from_behind(orbitals, "band", -OFFSET)[0]
    total = pair_terms(own, lower, constants)
    return pair_terms(own, upper, constants, sum_a=total)[None]


def local(bands, orbitals):
    points = orbitals.shape[1]
    constants = (screened_kernel(points), *hartley_tables(points))
    if bands == 16:
        return sixteen_bands(orbitals, constants)
    return any_bands(orbitals, constants)


def solution(mesh):
    return jax.shard_map(
        functools.partial(local, mesh.shape["band"]),
        mesh=mesh,
        in_specs=(P(("groups", "band"), None, None),),
        out_specs=P(("groups", "band"), None, None),
        check_vma=False,
    )
```

```python
import functools
import math

import jax
import jax.numpy as jnp
import numpy as np
from jax import lax
from jax.experimental import pallas as pl
from jax.experimental.pallas import tpu as pltpu
from jax.sharding import PartitionSpec as P

OFFSET = 5
screening = 5.44
LANES = 128
X_STEPS = 6
PLANE_STEPS = 6


def from_behind(value, axis, by):
    count = lax.axis_size(axis)
    return lax.ppermute(value, axis, [(i, (i + by) % count) for i in range(count)])


def screened_kernel(points):
    signed = jnp.arange(LANES, dtype=jnp.int32)
    inside = signed < points
    signed = jnp.where(signed >= points // 2, signed - points, signed)
    wavenumber = signed.astype(jnp.float32) * (2.0 * math.pi / points)
    squared = (
        wavenumber[:points, None, None] ** 2
        + wavenumber[None, :points, None] ** 2
        + wavenumber[None, None, :] ** 2
    )
    screen_rate = screening / points
    finite = jnp.where(squared > 0.0, squared, 1.0)
    screened = 4.0 * math.pi / finite * -jnp.expm1(-finite / (4.0 * screen_rate * screen_rate))
    kernel = jnp.where(squared > 0.0, screened, math.pi / (screen_rate * screen_rate))
    return jnp.where(inside, kernel / float(points * points * points), 0.0)


def hartley_tables(points):
    counter = np.arange(points)
    angles = 2.0 * np.pi * (counter[:, None] * counter[None, :] % points) / points
    table = np.cos(angles) + np.sin(angles)
    high = table.astype(jnp.bfloat16)
    low = (table - high.astype(np.float64)).astype(jnp.bfloat16)
    left = np.zeros((2 * points, 2 * points), jnp.bfloat16)
    left[:points, :points] = high
    left[:points, points:] = high
    left[points:, :points] = low
    right = np.zeros((2 * LANES, 2 * LANES), jnp.bfloat16)
    right[:points, :points] = high
    right[:points, LANES:LANES + points] = low
    right[LANES:LANES + points, :points] = high
    return jnp.asarray(left), jnp.asarray(right)


def two_terms(value):
    high = value.astype(jnp.bfloat16)
    low = (value - high.astype(jnp.float32)).astype(jnp.bfloat16)
    return high, low


def from_left(left, value):
    half = value.shape[0]
    terms = jnp.concatenate(two_terms(value), 0)
    out = jnp.dot(left, terms, preferred_element_type=jnp.float32)
    return out[:half] + out[half:]


def from_right(value, right):
    out = jnp.dot(jnp.concatenate(two_terms(value), 1), right, preferred_element_type=jnp.float32)
    return out[:, :LANES] + out[:, LANES:]


def pair_body(points, has, *refs):
    refs = list(refs)
    names = ["a", "b"] + [name for name in ("sum_a", "sum_b") if name in has]
    far = {name: refs.pop(0) for name in names}
    kernel_ref, left_ref, right_ref = refs.pop(0), refs.pop(0), refs.pop(0)
    for_a_ref = refs.pop(0)
    low_a_ref = refs.pop(0) if "halves" in has else None
    for_b_ref = refs.pop(0) if "for_b" in has else None
    held, near, sems = refs
    step = pl.program_id(0)
    columns = for_a_ref.shape[1]
    ys = columns // points
    per_step = points // PLANE_STEPS
    late = X_STEPS + PLANE_STEPS

    def fetch(name, chunk):
        place = names.index(name)
        span = pl.ds(pl.multiple_of(chunk * columns, columns), columns)
        return pltpu.make_async_copy(
            far[name].at[:, span], near.at[place, :, span], sems.at[place, chunk]
        )

    def here(name, chunk):
        span = pl.ds(pl.multiple_of(chunk * columns, columns), columns)
        return near[names.index(name), :, span]

    ends = [name for name in names if not name.startswith("sum")]
    sums = [name for name in names if name.startswith("sum")]

    @pl.when(step == 0)
    def start_ends():
        for chunk in range(X_STEPS):
            for name in ends:
                fetch(name, chunk).start()

    if sums:
        @pl.when(step == X_STEPS)
        def start_sums():
            for chunk in range(X_STEPS):
                for name in sums:
                    fetch(name, chunk).start()

    def lanes_apart(block):
        gap = jnp.zeros((points, LANES - points), jnp.float32)
        rows = [
            jnp.concatenate([block[:, q * points:(q + 1) * points], gap], 1) for q in range(ys)
        ]
        return jnp.swapaxes(jnp.stack(rows, 0), 0, 1)

    def lanes_together(block):
        block = jnp.swapaxes(block, 0, 1)
        return jnp.concatenate([block[q][:, :points] for q in range(ys)], 1)

    def side_by_side(block):
        return jnp.concatenate([block[i] for i in range(per_step)], 1)

    @pl.when(step < X_STEPS)
    def forward_x():
        for name in ends:
            fetch(name, step).wait()
        spectrum = from_left(left_ref[...], here("a", step) * here("b", step))
        start = pl.multiple_of(step * ys, ys)
        held[:, pl.ds(start, ys), :] = lanes_apart(spectrum)

    @pl.when((step >= X_STEPS) & (step < late))
    def planes():
        left = left_ref[...]
        right = right_ref[...]
        first = (step - X_STEPS) * per_step
        block = held[pl.ds(first, per_step)].reshape(per_step * points, LANES)
        block = from_right(block, right).reshape(per_step, points, LANES)
        wide = from_left(left, side_by_side(block))
        wide = from_left(left, wide * side_by_side(kernel_ref[...]))
        block = jnp.concatenate(
            [wide[:, i * LANES:(i + 1) * LANES] for i in range(per_step)], 0
        )
        block = from_right(block, right)
        held[pl.ds(first, per_step)] = block.reshape(per_step, points, LANES)

    @pl.when(step >= late)
    def inverse_x():
        chunk = step - late
        start = pl.multiple_of(chunk * ys, ys)
        for name in sums:
            fetch(name, chunk).wait()
        block = lanes_together(held[:, pl.ds(start, ys), :])
        potential = from_left(left_ref[...], block)
        for_a = here("b", chunk) * potential
        for_a = here("sum_a", chunk) - for_a if "sum_a" in has else -for_a
        if low_a_ref is None:
            for_a_ref[...] = for_a
        else:
            for_a_ref[...] = for_a[:points // 2]
            low_a_ref[...] = for_a[points // 2:]
        if for_b_ref is not None:
            for_b = here("a", chunk) * potential
            for_b_ref[...] = here("sum_b", chunk) - for_b if "sum_b" in has else -for_b


def pair_terms(a, b, constants, sum_a=None, sum_b=None, for_b=False, halves=False):
    points, plane = a.shape
    columns = plane // X_STEPS
    late = X_STEPS + PLANE_STEPS
    kernel, left, right = constants

    def tail(i):
        return (0, jnp.maximum(i - late, 0))

    def middle(i):
        return (jnp.clip(i - X_STEPS, 0, PLANE_STEPS - 1), 0, 0)

    def whole(i):
        return (0, 0)

    optional = {"sum_a": sum_a, "sum_b": sum_b}
    optional = {name: value for name, value in optional.items() if value is not None}
    blocks = [a, b, *optional.values()]
    has = list(optional) + ["for_b"] * for_b + ["halves"] * halves
    rows = ([points // 2] * 2 if halves else [points]) + [points] * for_b
    out = pl.pallas_call(
        functools.partial(pair_body, points, has),
        grid=(2 * X_STEPS + PLANE_STEPS,),
        in_specs=[pl.BlockSpec(memory_space=pl.ANY)] * len(blocks)
        + [
            pl.BlockSpec((points // PLANE_STEPS, points, LANES), middle),
            pl.BlockSpec(left.shape, whole),
            pl.BlockSpec(right.shape, whole),
        ],
        out_specs=[pl.BlockSpec((n, columns), tail) for n in rows],
        out_shape=[jax.ShapeDtypeStruct((n, plane), jnp.float32) for n in rows],
        scratch_shapes=[
            pltpu.VMEM((points, points, LANES), jnp.float32),
            pltpu.VMEM((len(blocks), points, plane), jnp.float32),
            pltpu.SemaphoreType.DMA((len(blocks), X_STEPS)),
        ],
        compiler_params=pltpu.CompilerParams(vmem_limit_bytes=60 * 2**20),
        cost_estimate=pl.CostEstimate(
            flops=16_000_000_000, bytes_accessed=20_000_000, transcendentals=0
        ),
        name="pair_terms",
    )(*blocks, kernel, left, right)
    return out if len(rows) > 1 else out[0]


def gate_body(token_ref, left_ref, role_ref, own_ref, turned_ref, new_left_ref, block_ref, near, sems):
    new_left_ref[...] = left_ref[...]
    role = role_ref[0]
    columns = own_ref.shape[1] // X_STEPS

    def copies(source_ref):
        spans = [pl.ds(i * columns, columns) for i in range(X_STEPS)]
        inward = [
            pltpu.make_async_copy(source_ref.at[:, span], near.at[:, span], sems.at[0, i])
            for i, span in enumerate(spans)
        ]
        outward = [
            pltpu.make_async_copy(near.at[:, span], block_ref.at[:, span], sems.at[1, i])
            for i, span in enumerate(spans)
        ]
        for copy in inward:
            copy.start()
        for first, second in zip(inward, outward):
            first.wait()
            second.start()
        for copy in outward:
            copy.wait()

    @pl.when(role == 1)
    def from_own():
        copies(own_ref)

    @pl.when(role == 2)
    def from_turned():
        copies(turned_ref)


def gate(token, left, role, own, turned):
    in_vmem = pl.BlockSpec(memory_space=pltpu.VMEM)
    in_smem = pl.BlockSpec(memory_space=pltpu.SMEM)
    anywhere = pl.BlockSpec(memory_space=pl.ANY)
    return pl.pallas_call(
        gate_body,
        in_specs=[in_vmem, in_vmem, in_smem, anywhere, anywhere],
        out_specs=[in_vmem, anywhere],
        out_shape=[
            jax.ShapeDtypeStruct(left.shape, left.dtype),
            jax.ShapeDtypeStruct(own.shape, own.dtype),
        ],
        scratch_shapes=[pltpu.VMEM(own.shape, own.dtype), pltpu.SemaphoreType.DMA((2, X_STEPS))],
        compiler_params=pltpu.CompilerParams(vmem_limit_bytes=60 * 2**20),
        name="gate",
    )(token, left, role, own, turned)


def both_halves(*pairs):
    return list(pairs) + [(15 - source, 15 - target) for source, target in pairs]


CROSSING = both_halves((3, 14), (4, 9), (9, 11), (14, 12))
PARTNERS = both_halves((8, 14), (15, 9))
ARRIVED = both_halves((14, 2), (9, 5))
SECOND = both_halves((5, 10), (2, 13), (11, 14), (12, 9))
BESIDE = both_halves((13, 14), (10, 9))
HOME_ACROSS = both_halves((9, 4), (14, 3))
HOME_FAR = both_halves((9, 15), (14, 8))
HOME_TURN = both_halves((9, 11), (14, 12))
HOME_TURNED = both_halves((11, 15), (12, 8))
HOME_BESIDE = both_halves((9, 10), (14, 13))
SECOND_ROLES = {5: 1, 10: 1, 2: 1, 13: 1, 11: 2, 4: 2, 12: 2, 3: 2}


def sixteen_bands(orbitals, constants):
    def send(value, pairs):
        return lax.ppermute(value[None], "band", pairs)[0]

    kernel, left, right = constants
    own = orbitals[0]
    roles = jnp.asarray([SECOND_ROLES.get(i, 0) for i in range(16)], jnp.int32)
    role = roles[lax.axis_index("band")][None]
    crossed = send(own, CROSSING)
    partner = send(own, PARTNERS)
    token = send(crossed[:8, :LANES] + kernel[0, :8], ARRIVED)
    left, held_back = gate(token, left, role, own, crossed)
    constants = (kernel, left, right)
    beside = send(held_back, BESIDE)
    second = send(held_back, SECOND)

    partner_sum, crossed_sum = pair_terms(partner, crossed, constants, for_b=True)
    own_sum, crossed_sum = pair_terms(own, crossed, constants, sum_b=crossed_sum, for_b=True)
    home = send(crossed_sum, HOME_ACROSS)
    top, bottom, beside_sum = pair_terms(
        partner, beside, constants, sum_a=partner_sum, for_b=True, halves=True
    )
    bottom = send(bottom, HOME_TURN)
    top = send(top, HOME_FAR)
    home_beside = send(beside_sum, HOME_BESIDE)
    bottom = send(bottom, HOME_TURNED)
    own_sum = pair_terms(own, second, constants, sum_a=own_sum)
    own_sum = jnp.where(role == 2, 0.0, own_sum)
    return (own_sum + home + home_beside + jnp.concatenate([top, bottom], 0))[None]


def any_bands(orbitals, constants):
    own = orbitals[0]
    lower = from_behind(orbitals, "band", OFFSET)[0]
    upper = from_behind(orbitals, "band", -OFFSET)[0]
    total = pair_terms(own, lower, constants)
    return pair_terms(own, upper, constants, sum_a=total)[None]


def local(bands, orbitals):
    points = orbitals.shape[1]
    constants = (screened_kernel(points), *hartley_tables(points))
    if bands == 16:
        return sixteen_bands(orbitals, constants)
    return any_bands(orbitals, constants)


def solution(mesh):
    return jax.shard_map(
        functools.partial(local, mesh.shape["band"]),
        mesh=mesh,
        in_specs=(P(("groups", "band"), None, None),),
        out_specs=P(("groups", "band"), None, None),
        check_vma=False,
    )
```

```python
import functools
import math

import jax
import jax.numpy as jnp
import numpy as np
from jax import lax
from jax.experimental import pallas as pl
from jax.experimental.pallas import tpu as pltpu
from jax.sharding import PartitionSpec as P

OFFSET = 5
screening = 5.44
LANES = 128
X_STEPS = 6
PLANE_STEPS = 6


def from_behind(value, axis, by):
    count = lax.axis_size(axis)
    return lax.ppermute(value, axis, [(i, (i + by) % count) for i in range(count)])


def screened_kernel(points):
    signed = jnp.arange(LANES, dtype=jnp.int32)
    inside = signed < points
    signed = jnp.where(signed >= points // 2, signed - points, signed)
    wavenumber = signed.astype(jnp.float32) * (2.0 * math.pi / points)
    squared = (
        wavenumber[:points, None, None] ** 2
        + wavenumber[None, :points, None] ** 2
        + wavenumber[None, None, :] ** 2
    )
    screen_rate = screening / points
    finite = jnp.where(squared > 0.0, squared, 1.0)
    screened = 4.0 * math.pi / finite * -jnp.expm1(-finite / (4.0 * screen_rate * screen_rate))
    kernel = jnp.where(squared > 0.0, screened, math.pi / (screen_rate * screen_rate))
    return jnp.where(inside, kernel / float(points * points * points), 0.0)


def hartley_tables(points):
    counter = np.arange(points)
    angles = 2.0 * np.pi * (counter[:, None] * counter[None, :] % points) / points
    table = np.cos(angles) + np.sin(angles)
    high = table.astype(jnp.bfloat16)
    low = (table - high.astype(np.float64)).astype(jnp.bfloat16)
    left = np.zeros((2 * points, 2 * points), jnp.bfloat16)
    left[:points, :points] = high
    left[:points, points:] = high
    left[points:, :points] = low
    right = np.zeros((2 * LANES, 2 * LANES), jnp.bfloat16)
    right[:points, :points] = high
    right[:points, LANES:LANES + points] = low
    right[LANES:LANES + points, :points] = high
    return jnp.asarray(left), jnp.asarray(right)


def two_terms(value):
    high = value.astype(jnp.bfloat16)
    low = (value - high.astype(jnp.float32)).astype(jnp.bfloat16)
    return high, low


def from_left(left, value):
    half = value.shape[0]
    terms = jnp.concatenate(two_terms(value), 0)
    out = jnp.dot(left, terms, preferred_element_type=jnp.float32)
    return out[:half] + out[half:]


def from_right(value, right):
    out = jnp.dot(jnp.concatenate(two_terms(value), 1), right, preferred_element_type=jnp.float32)
    return out[:, :LANES] + out[:, LANES:]


def pair_body(points, slot, has, *refs):
    refs = list(refs)
    flags_ref = refs.pop(0)
    names = ["a", "b"] + [name for name in ("sum_a", "sum_b") if name in has]
    far = {name: refs.pop(0) for name in names}
    if "then" in has:
        refs.pop(0)
    kernel_ref, left_ref, right_ref = refs.pop(0), refs.pop(0), refs.pop(0)
    out_refs = {"for_a": refs.pop(0)}
    if "halves" in has:
        out_refs["low_a"] = refs.pop(0)
    if "for_b" in has:
        out_refs["for_b"] = refs.pop(0)
    held, near, near_kernel, near_out, sems, kernel_sems, out_sems = refs
    outs = list(out_refs)
    step = pl.program_id(0)
    active = flags_ref[2 * slot] == 1
    with_sum = flags_ref[2 * slot + 1] == 1
    columns = near.shape[2] // X_STEPS
    ys = columns // points
    per_step = points // PLANE_STEPS
    late = X_STEPS + PLANE_STEPS

    def span_of(chunk):
        start = chunk * columns
        return pl.ds(start if isinstance(chunk, int) else pl.multiple_of(start, columns), columns)

    def fetch(name, chunk):
        place, span = names.index(name), span_of(chunk)
        return pltpu.make_async_copy(
            far[name].at[:, span], near.at[place, :, span], sems.at[place, chunk]
        )

    def fetch_kernel(part):
        span = pl.ds(part * per_step, per_step)
        return pltpu.make_async_copy(
            kernel_ref.at[span], near_kernel.at[span], kernel_sems.at[part]
        )

    def give(name, chunk):
        span = span_of(chunk)
        source = near_out.at[0 if name != "for_b" else 1]
        if "halves" in has and name != "for_b":
            rows = pl.ds(points // 2 if name == "low_a" else 0, points // 2)
            source = source.at[rows, span]
        else:
            source = source.at[:, span]
        return pltpu.make_async_copy(
            source, out_refs[name].at[:, span], out_sems.at[outs.index(name), chunk]
        )

    def here(name, chunk):
        return near[names.index(name), :, span_of(chunk)]

    sums = [name for name in names if name.startswith("sum")]

    @pl.when(active & (step == 0))
    def start_first():
        for chunk in range(2):
            for name in ("a", "b"):
                fetch(name, chunk).start()

    @pl.when(active & (step + 2 < X_STEPS))
    def start_next():
        for name in ("a", "b"):
            fetch(name, step + 2).start()

    @pl.when(active & (step == X_STEPS - 2))
    def start_kernel():
        for part in range(PLANE_STEPS):
            fetch_kernel(part).start()

    if sums:
        @pl.when(active & (step == X_STEPS))
        def start_sums():
            for chunk in range(X_STEPS):
                for name in sums:
                    fetch(name, chunk).start()

    def lanes_apart(block):
        gap = jnp.zeros((points, LANES - points), jnp.float32)
        rows = [
            jnp.concatenate([block[:, q * points:(q + 1) * points], gap], 1) for q in range(ys)
        ]
        return jnp.swapaxes(jnp.stack(rows, 0), 0, 1)

    def lanes_together(block):
        block = jnp.swapaxes(block, 0, 1)
        return jnp.concatenate([block[q][:, :points] for q in range(ys)], 1)

    def side_by_side(block):
        return jnp.concatenate([block[i] for i in range(per_step)], 1)

    @pl.when(active & (step < X_STEPS))
    def forward_x():
        for name in ("a", "b"):
            fetch(name, step).wait()
        spectrum = from_left(left_ref[...], here("a", step) * here("b", step))
        start = pl.multiple_of(step * ys, ys)
        held[:, pl.ds(start, ys), :] = lanes_apart(spectrum)

    @pl.when(active & (step >= X_STEPS) & (step < late))
    def planes():
        left = left_ref[...]
        right = right_ref[...]
        part = step - X_STEPS
        first = part * per_step
        block = held[pl.ds(first, per_step)].reshape(per_step * points, LANES)
        block = from_right(block, right).reshape(per_step, points, LANES)
        wide = from_left(left, side_by_side(block))
        fetch_kernel(part).wait()
        wide = from_left(left, wide * side_by_side(near_kernel[pl.ds(first, per_step)]))
        block = jnp.concatenate(
            [wide[:, i * LANES:(i + 1) * LANES] for i in range(per_step)], 0
        )
        block = from_right(block, right)
        held[pl.ds(first, per_step)] = block.reshape(per_step, points, LANES)

    @pl.when(active & (step >= late))
    def inverse_x():
        chunk = step - late
        start = pl.multiple_of(chunk * ys, ys)
        for name in sums:
            fetch(name, chunk).wait()
        block = lanes_together(held[:, pl.ds(start, ys), :])
        potential = from_left(left_ref[...], block)
        for_a = -(here("b", chunk) * potential)
        if "sum_a" in has:
            for_a = for_a + jnp.where(with_sum, here("sum_a", chunk), 0.0)
        near_out[0, :, span_of(chunk)] = for_a
        if "for_b" in has:
            for_b = -(here("a", chunk) * potential)
            if "sum_b" in has:
                for_b = for_b + here("sum_b", chunk)
            near_out[1, :, span_of(chunk)] = for_b
        for name in outs:
            give(name, chunk).start()

    @pl.when(active & (step == late + X_STEPS - 1))
    def wait_outs():
        for chunk in range(X_STEPS):
            for name in outs:
                give(name, chunk).wait()


def pair_terms(
    flags, slot, a, b, constants, sum_a=None, sum_b=None, for_b=False, halves=False, in_place=False, then=None
):
    points, plane = a.shape
    kernel, left, right = constants
    optional = {"sum_a": sum_a, "sum_b": sum_b}
    optional = {name: value for name, value in optional.items() if value is not None}
    blocks = [a, b, *optional.values()]
    waited = [] if then is None else [then]
    has = list(optional) + ["for_b"] * for_b + ["halves"] * halves + ["then"] * len(waited)
    rows = ([points // 2] * 2 if halves else [points]) + [points] * for_b
    anywhere = pl.BlockSpec(memory_space=pl.ANY)
    out = pl.pallas_call(
        functools.partial(pair_body, points, slot, has),
        grid=(2 * X_STEPS + PLANE_STEPS,),
        in_specs=[pl.BlockSpec(memory_space=pltpu.SMEM)]
        + [anywhere] * (len(blocks) + len(waited) + 1)
        + [pl.BlockSpec(table.shape, lambda i: (0, 0)) for table in (left, right)],
        out_specs=[anywhere] * len(rows),
        out_shape=[jax.ShapeDtypeStruct((n, plane), jnp.float32) for n in rows],
        input_output_aliases={3: 0} if in_place else {},
        scratch_shapes=[
            pltpu.VMEM((points, points, LANES), jnp.float32),
            pltpu.VMEM((len(blocks), points, plane), jnp.float32),
            pltpu.VMEM((points, points, LANES), jnp.float32),
            pltpu.VMEM((2 if for_b else 1, points, plane), jnp.float32),
            pltpu.SemaphoreType.DMA((len(blocks), X_STEPS)),
            pltpu.SemaphoreType.DMA((PLANE_STEPS,)),
            pltpu.SemaphoreType.DMA((len(rows), X_STEPS)),
        ],
        compiler_params=pltpu.CompilerParams(vmem_limit_bytes=60 * 2**20),
        cost_estimate=pl.CostEstimate(
            flops=16_000_000_000, bytes_accessed=20_000_000, transcendentals=0
        ),
        name="pair_terms",
    )(flags, *blocks, *waited, kernel, left, right)
    return out if len(rows) > 1 else out[0]


def copy_body(block_ref, new_block_ref):
    new_block_ref[...] = block_ref[...]


def copied(block):
    points, plane = block.shape
    part = pl.BlockSpec((points, plane // X_STEPS), lambda i: (0, i))
    return pl.pallas_call(
        copy_body,
        grid=(X_STEPS,),
        in_specs=[part],
        out_specs=part,
        out_shape=jax.ShapeDtypeStruct(block.shape, block.dtype),
        compiler_params=pltpu.CompilerParams(vmem_limit_bytes=60 * 2**20),
        name="copied",
    )(block)


def gate_body(token_ref, left_ref, block_ref, new_left_ref, new_block_ref):
    new_left_ref[...] = left_ref[...]


def gate(token, left, block):
    in_vmem = pl.BlockSpec(memory_space=pltpu.VMEM)
    anywhere = pl.BlockSpec(memory_space=pl.ANY)
    return pl.pallas_call(
        gate_body,
        in_specs=[in_vmem, in_vmem, anywhere],
        out_specs=[in_vmem, anywhere],
        out_shape=[
            jax.ShapeDtypeStruct(left.shape, left.dtype),
            jax.ShapeDtypeStruct(block.shape, block.dtype),
        ],
        input_output_aliases={2: 1},
        compiler_params=pltpu.CompilerParams(vmem_limit_bytes=60 * 2**20),
        name="gate",
    )(token, left, block)


def both_halves(*pairs):
    return list(pairs) + [(15 - source, 15 - target) for source, target in pairs]


CROSSING = both_halves((3, 14), (4, 9))
PARTNERS = both_halves((8, 14), (15, 9), (9, 11), (14, 12))
ARRIVED = both_halves((14, 2), (9, 5))
SINGLES = both_halves((5, 10), (2, 13))
BESIDE = both_halves((13, 14), (10, 9))
PASSED = both_halves((9, 10), (14, 13), (11, 14), (12, 9))
HOME_ACROSS = both_halves((9, 4), (14, 3))
HOME_FAR = both_halves((9, 15), (14, 8))
HOME_TURN = both_halves((9, 11), (14, 12))
HOME_TURNED = both_halves((11, 15), (12, 8))
HUB_FLAGS = (1, 0, 1, 0, 1, 1, 1, 1, 0, 0)
SINGLE_FLAGS = (0, 0, 0, 0, 0, 0, 1, 0, 1, 1)
FLAGS = {9: HUB_FLAGS, 14: HUB_FLAGS, 6: HUB_FLAGS, 1: HUB_FLAGS}
FLAGS.update({10: SINGLE_FLAGS, 13: SINGLE_FLAGS, 5: SINGLE_FLAGS, 2: SINGLE_FLAGS})


def sixteen_bands(orbitals, constants):
    def send(value, pairs):
        return lax.ppermute(value[None], "band", pairs)[0]

    kernel, left, right = constants
    own = orbitals[0]
    flags = jnp.asarray([FLAGS.get(i, (0,) * 10) for i in range(16)], jnp.int32)
    flags = flags[lax.axis_index("band")]
    pair = functools.partial(pair_terms, flags)
    crossed = send(own, CROSSING)
    partner = send(own, PARTNERS)
    own_copy = copied(own)
    token = crossed[:8, :LANES] + kernel[0, :8] + own_copy[:8, :LANES]
    left, held_back = gate(send(token, ARRIVED), left, own_copy)
    constants = (kernel, left, right)
    single = send(held_back, SINGLES)
    beside = send(held_back, BESIDE)
    passed = send(partner, PASSED)

    partner_sum, crossed_sum = pair(0, partner, crossed, constants, for_b=True)
    own_sum, crossed_sum = pair(1, own, crossed, constants, sum_b=crossed_sum, for_b=True)
    home = send(crossed_sum, HOME_ACROSS)
    top, bottom = pair(2, partner, beside, constants, sum_a=partner_sum, halves=True, then=own_sum)
    bottom = send(bottom, HOME_TURN)
    top = send(top, HOME_FAR)
    bottom = send(bottom, HOME_TURNED)
    own_sum = pair(3, own, passed, constants, sum_a=own_sum)
    own_sum = pair(4, own, single, constants, sum_a=own_sum, in_place=True)
    own_sum = jnp.where(flags[6] == 1, own_sum, 0.0)
    return (own_sum + home + jnp.concatenate([top, bottom], 0))[None]


def any_bands(orbitals, constants):
    own = orbitals[0]
    flags = jnp.ones((4,), jnp.int32)
    lower = from_behind(orbitals, "band", OFFSET)[0]
    upper = from_behind(orbitals, "band", -OFFSET)[0]
    total = pair_terms(flags, 0, own, lower, constants)
    return pair_terms(flags, 1, own, upper, constants, sum_a=total)[None]


def local(bands, orbitals):
    points = orbitals.shape[1]
    constants = (screened_kernel(points), *hartley_tables(points))
    if bands == 16:
        return sixteen_bands(orbitals, constants)
    return any_bands(orbitals, constants)


def solution(mesh):
    return jax.shard_map(
        functools.partial(local, mesh.shape["band"]),
        mesh=mesh,
        in_specs=(P(("groups", "band"), None, None),),
        out_specs=P(("groups", "band"), None, None),
        check_vma=False,
    )
```

```python
import functools
import math

import jax
import jax.numpy as jnp
import numpy as np
from jax import lax
from jax.experimental import pallas as pl
from jax.experimental.pallas import tpu as pltpu
from jax.sharding import PartitionSpec as P

OFFSET = 5
screening = 5.44
LANES = 128
X_STEPS = 6
PLANE_STEPS = 6
FAR_ROWS = 40


def from_behind(value, axis, by):
    count = lax.axis_size(axis)
    return lax.ppermute(value, axis, [(i, (i + by) % count) for i in range(count)])


def screened_kernel(points):
    signed = jnp.arange(LANES, dtype=jnp.int32)
    inside = signed < points
    signed = jnp.where(signed >= points // 2, signed - points, signed)
    wavenumber = signed.astype(jnp.float32) * (2.0 * math.pi / points)
    squared = (
        wavenumber[:points, None, None] ** 2
        + wavenumber[None, :points, None] ** 2
        + wavenumber[None, None, :] ** 2
    )
    screen_rate = screening / points
    finite = jnp.where(squared > 0.0, squared, 1.0)
    screened = 4.0 * math.pi / finite * -jnp.expm1(-finite / (4.0 * screen_rate * screen_rate))
    kernel = jnp.where(squared > 0.0, screened, math.pi / (screen_rate * screen_rate))
    return jnp.where(inside, kernel / float(points * points * points), 0.0)


def hartley_tables(points):
    counter = np.arange(points)
    angles = 2.0 * np.pi * (counter[:, None] * counter[None, :] % points) / points
    table = np.cos(angles) + np.sin(angles)
    high = table.astype(jnp.bfloat16)
    low = (table - high.astype(np.float64)).astype(jnp.bfloat16)
    left = np.zeros((2 * points, 2 * points), jnp.bfloat16)
    left[:points, :points] = high
    left[:points, points:] = high
    left[points:, :points] = low
    right = np.zeros((2 * LANES, 2 * LANES), jnp.bfloat16)
    right[:points, :points] = high
    right[:points, LANES:LANES + points] = low
    right[LANES:LANES + points, :points] = high
    return jnp.asarray(left), jnp.asarray(right)


def two_terms(value):
    high = value.astype(jnp.bfloat16)
    low = (value - high.astype(jnp.float32)).astype(jnp.bfloat16)
    return high, low


def from_left(left, value):
    half = value.shape[0]
    terms = jnp.concatenate(two_terms(value), 0)
    out = jnp.dot(left, terms, preferred_element_type=jnp.float32)
    return out[:half] + out[half:]


def from_right(value, right):
    out = jnp.dot(jnp.concatenate(two_terms(value), 1), right, preferred_element_type=jnp.float32)
    return out[:, :LANES] + out[:, LANES:]


def pair_body(points, slot, has, *refs):
    refs = list(refs)
    flags_ref = refs.pop(0)
    names = ["a", "b"] + [name for name in ("sum_a", "sum_b") if name in has]
    far = {name: refs.pop(0) for name in names}
    if "then" in has:
        refs.pop(0)
    kernel_ref, left_ref, right_ref = refs.pop(0), refs.pop(0), refs.pop(0)
    out_refs = {"for_a": refs.pop(0)}
    if "halves" in has:
        out_refs["low_a"] = refs.pop(0)
    if "for_b" in has:
        out_refs["for_b"] = refs.pop(0)
    if "hand_on" in has:
        refs.pop(0)
    held, near, near_kernel, near_out, sems, kernel_sems, out_sems = refs
    outs = list(out_refs)
    step = pl.program_id(0)
    active = flags_ref[2 * slot] == 1
    with_sum = flags_ref[2 * slot + 1] == 1
    columns = near.shape[2] // X_STEPS
    ys = columns // points
    per_step = points // PLANE_STEPS
    late = X_STEPS + PLANE_STEPS

    def span_of(chunk):
        start = chunk * columns
        return pl.ds(start if isinstance(chunk, int) else pl.multiple_of(start, columns), columns)

    def fetch(name, chunk):
        place, span = names.index(name), span_of(chunk)
        return pltpu.make_async_copy(
            far[name].at[:, span], near.at[place, :, span], sems.at[place, chunk]
        )

    def fetch_kernel(part):
        span = pl.ds(part * per_step, per_step)
        return pltpu.make_async_copy(
            kernel_ref.at[span], near_kernel.at[span], kernel_sems.at[part]
        )

    def give(name, chunk):
        span = span_of(chunk)
        source = near_out.at[0 if name != "for_b" else 1]
        if "halves" in has and name != "for_b":
            rows = pl.ds(points - FAR_ROWS, FAR_ROWS) if name == "low_a" else pl.ds(0, points - FAR_ROWS)
            source = source.at[rows, span]
        else:
            source = source.at[:, span]
        return pltpu.make_async_copy(
            source, out_refs[name].at[:, span], out_sems.at[outs.index(name), chunk]
        )

    def here(name, chunk):
        return near[names.index(name), :, span_of(chunk)]

    sums = [name for name in names if name.startswith("sum")]

    @pl.when(active & (step == 0))
    def start_first():
        for chunk in range(2):
            for name in ("a", "b"):
                fetch(name, chunk).start()

    @pl.when(active & (step + 2 < X_STEPS))
    def start_next():
        for name in ("a", "b"):
            fetch(name, step + 2).start()

    @pl.when(active & (step == X_STEPS - 2))
    def start_kernel():
        for part in range(PLANE_STEPS):
            fetch_kernel(part).start()

    if sums:
        @pl.when(active & (step == X_STEPS))
        def start_sums():
            for chunk in range(X_STEPS):
                for name in sums:
                    fetch(name, chunk).start()

    def lanes_apart(block):
        gap = jnp.zeros((points, LANES - points), jnp.float32)
        rows = [
            jnp.concatenate([block[:, q * points:(q + 1) * points], gap], 1) for q in range(ys)
        ]
        return jnp.swapaxes(jnp.stack(rows, 0), 0, 1)

    def lanes_together(block):
        block = jnp.swapaxes(block, 0, 1)
        return jnp.concatenate([block[q][:, :points] for q in range(ys)], 1)

    def side_by_side(block):
        return jnp.concatenate([block[i] for i in range(per_step)], 1)

    @pl.when(active & (step < X_STEPS))
    def forward_x():
        for name in ("a", "b"):
            fetch(name, step).wait()
        spectrum = from_left(left_ref[...], here("a", step) * here("b", step))
        start = pl.multiple_of(step * ys, ys)
        held[:, pl.ds(start, ys), :] = lanes_apart(spectrum)

    @pl.when(active & (step >= X_STEPS) & (step < late))
    def planes():
        left = left_ref[...]
        right = right_ref[...]
        part = step - X_STEPS
        first = part * per_step
        block = held[pl.ds(first, per_step)].reshape(per_step * points, LANES)
        block = from_right(block, right).reshape(per_step, points, LANES)
        wide = from_left(left, side_by_side(block))
        fetch_kernel(part).wait()
        wide = from_left(left, wide * side_by_side(near_kernel[pl.ds(first, per_step)]))
        block = jnp.concatenate(
            [wide[:, i * LANES:(i + 1) * LANES] for i in range(per_step)], 0
        )
        block = from_right(block, right)
        held[pl.ds(first, per_step)] = block.reshape(per_step, points, LANES)

    @pl.when(active & (step >= late))
    def inverse_x():
        chunk = step - late
        start = pl.multiple_of(chunk * ys, ys)
        for name in sums:
            fetch(name, chunk).wait()
        block = lanes_together(held[:, pl.ds(start, ys), :])
        potential = from_left(left_ref[...], block)
        for_a = -(here("b", chunk) * potential)
        if "sum_a" in has:
            for_a = for_a + jnp.where(with_sum, here("sum_a", chunk), 0.0)
        near_out[0, :, span_of(chunk)] = for_a
        if "for_b" in has:
            for_b = -(here("a", chunk) * potential)
            if "sum_b" in has:
                for_b = for_b + here("sum_b", chunk)
            near_out[1, :, span_of(chunk)] = for_b
        for name in outs:
            give(name, chunk).start()

    @pl.when(active & (step == late + X_STEPS - 1))
    def wait_outs():
        for chunk in range(X_STEPS):
            for name in outs:
                give(name, chunk).wait()


def pair_terms(
    flags, slot, a, b, constants, sum_a=None, sum_b=None, for_b=False, halves=False, in_place=False, then=None, hand_on=False
):
    points, plane = a.shape
    kernel, left, right = constants
    optional = {"sum_a": sum_a, "sum_b": sum_b}
    optional = {name: value for name, value in optional.items() if value is not None}
    blocks = [a, b, *optional.values()]
    waited = [] if then is None else [then]
    has = list(optional) + ["for_b"] * for_b + ["halves"] * halves + ["then"] * len(waited)
    has += ["hand_on"] * hand_on
    rows = ([points - FAR_ROWS, FAR_ROWS] if halves else [points]) + [points] * for_b
    aliases = {3: 0} if in_place else {}
    if hand_on:
        aliases[1] = len(rows)
    anywhere = pl.BlockSpec(memory_space=pl.ANY)
    out = pl.pallas_call(
        functools.partial(pair_body, points, slot, has),
        grid=(2 * X_STEPS + PLANE_STEPS,),
        in_specs=[pl.BlockSpec(memory_space=pltpu.SMEM)]
        + [anywhere] * (len(blocks) + len(waited) + 1)
        + [pl.BlockSpec(table.shape, lambda i: (0, 0)) for table in (left, right)],
        out_specs=[anywhere] * (len(rows) + hand_on),
        out_shape=[
            jax.ShapeDtypeStruct((n, plane), jnp.float32) for n in rows + [points] * hand_on
        ],
        input_output_aliases=aliases,
        scratch_shapes=[
            pltpu.VMEM((points, points, LANES), jnp.float32),
            pltpu.VMEM((len(blocks), points, plane), jnp.float32),
            pltpu.VMEM((points, points, LANES), jnp.float32),
            pltpu.VMEM((2 if for_b else 1, points, plane), jnp.float32),
            pltpu.SemaphoreType.DMA((len(blocks), X_STEPS)),
            pltpu.SemaphoreType.DMA((PLANE_STEPS,)),
            pltpu.SemaphoreType.DMA((len(rows), X_STEPS)),
        ],
        compiler_params=pltpu.CompilerParams(vmem_limit_bytes=62 * 2**20),
        cost_estimate=pl.CostEstimate(
            flops=100_000_000, bytes_accessed=1_000_000, transcendentals=0
        ),
        name="pair_terms",
    )(flags, *blocks, *waited, kernel, left, right)
    return out if len(out) > 1 else out[0]


def copy_body(flags_ref, block_ref, new_block_ref):
    new_block_ref[...] = block_ref[...]


def copied(flags, block):
    points, plane = block.shape
    part = pl.BlockSpec((points, plane // X_STEPS), lambda i: (0, i))
    return pl.pallas_call(
        copy_body,
        grid=(X_STEPS,),
        in_specs=[pl.BlockSpec(memory_space=pltpu.SMEM), part],
        out_specs=part,
        out_shape=jax.ShapeDtypeStruct(block.shape, block.dtype),
        compiler_params=pltpu.CompilerParams(vmem_limit_bytes=62 * 2**20),
        name="copied",
    )(flags, block)


def gate_body(token_ref, left_ref, block_ref, new_left_ref, new_block_ref):
    new_left_ref[...] = left_ref[...]


def gate(token, left, block):
    in_vmem = pl.BlockSpec(memory_space=pltpu.VMEM)
    anywhere = pl.BlockSpec(memory_space=pl.ANY)
    return pl.pallas_call(
        gate_body,
        in_specs=[in_vmem, in_vmem, anywhere],
        out_specs=[in_vmem, anywhere],
        out_shape=[
            jax.ShapeDtypeStruct(left.shape, left.dtype),
            jax.ShapeDtypeStruct(block.shape, block.dtype),
        ],
        input_output_aliases={2: 1},
        compiler_params=pltpu.CompilerParams(vmem_limit_bytes=62 * 2**20),
        name="gate",
    )(token, left, block)


def hold_body(block_ref, then_ref, new_block_ref):
    del block_ref, then_ref, new_block_ref


def hold(block, then):
    anywhere = pl.BlockSpec(memory_space=pl.ANY)
    return pl.pallas_call(
        hold_body,
        in_specs=[anywhere, anywhere],
        out_specs=anywhere,
        out_shape=jax.ShapeDtypeStruct(block.shape, block.dtype),
        input_output_aliases={0: 0},
        compiler_params=pltpu.CompilerParams(vmem_limit_bytes=62 * 2**20),
        name="hold",
    )(block, then)


def both_halves(*pairs):
    return list(pairs) + [(15 - source, 15 - target) for source, target in pairs]


CROSSING = both_halves((3, 14), (4, 9))
PARTNERS = both_halves((8, 14), (15, 9), (9, 11), (14, 12))
ARRIVED = both_halves((14, 2), (9, 5))
SINGLES = both_halves((5, 10), (2, 13))
BESIDE = both_halves((13, 14), (10, 9))
PASSED = both_halves((9, 10), (14, 13), (11, 14), (12, 9))
HOME_ACROSS = both_halves((9, 4), (14, 3))
HOME_FAR = both_halves((9, 15), (14, 8))
HOME_TURN = both_halves((9, 11), (14, 12))
HOME_TURNED = both_halves((11, 15), (12, 8))
HUB_FLAGS = (1, 0, 1, 0, 1, 1, 1, 1, 0, 0)
SINGLE_FLAGS = (0, 0, 0, 0, 0, 0, 1, 0, 1, 1)
FLAGS = {9: HUB_FLAGS, 14: HUB_FLAGS, 6: HUB_FLAGS, 1: HUB_FLAGS}
FLAGS.update({10: SINGLE_FLAGS, 13: SINGLE_FLAGS, 5: SINGLE_FLAGS, 2: SINGLE_FLAGS})


def sixteen_bands(orbitals, constants):
    def send(value, pairs):
        return lax.ppermute(value[None], "band", pairs)[0]

    kernel, left, right = constants
    own = orbitals[0]
    flags = jnp.asarray([FLAGS.get(i, (0,) * 10) for i in range(16)], jnp.int32)
    flags = flags[lax.axis_index("band")]
    pair = functools.partial(pair_terms, flags)
    crossed = send(own, CROSSING)
    partner = send(own, PARTNERS)
    own_copy = copied(flags, own)
    token = crossed[:8, :LANES] + kernel[0, :8] + own_copy[:8, :LANES]
    left, held_back = gate(send(token, ARRIVED), left, own_copy)
    constants = (kernel, left, right)
    single = send(held_back, SINGLES)
    beside = send(held_back, BESIDE)

    partner_sum, crossed_sum, partner = pair(
        0, partner, crossed, constants, for_b=True, hand_on=True
    )
    passed = send(partner, PASSED)
    own_sum, crossed_sum = pair(1, own, crossed, constants, sum_b=crossed_sum, for_b=True)
    home = send(crossed_sum, HOME_ACROSS)
    top, bottom = pair(
        2, partner, beside, constants, sum_a=partner_sum, halves=True, then=own_sum
    )
    bottom = send(bottom, HOME_TURN)
    top = send(top, HOME_FAR)
    own_sum = pair(3, own, passed, constants, sum_a=own_sum)
    bottom = send(hold(bottom, own_sum), HOME_TURNED)
    own_sum = pair(4, own, single, constants, sum_a=own_sum, in_place=True)
    own_sum = jnp.where(flags[6] == 1, own_sum, 0.0)
    return (own_sum + home + jnp.concatenate([top, bottom], 0))[None]


def any_bands(orbitals, constants):
    own = orbitals[0]
    flags = jnp.ones((4,), jnp.int32)
    lower = from_behind(orbitals, "band", OFFSET)[0]
    upper = from_behind(orbitals, "band", -OFFSET)[0]
    total = pair_terms(flags, 0, own, lower, constants)
    return pair_terms(flags, 1, own, upper, constants, sum_a=total)[None]


def local(bands, orbitals):
    points = orbitals.shape[1]
    constants = (screened_kernel(points), *hartley_tables(points))
    if bands == 16:
        return sixteen_bands(orbitals, constants)
    return any_bands(orbitals, constants)


def solution(mesh):
    return jax.shard_map(
        functools.partial(local, mesh.shape["band"]),
        mesh=mesh,
        in_specs=(P(("groups", "band"), None, None),),
        out_specs=P(("groups", "band"), None, None),
        check_vma=False,
    )
```

```python
import functools
import math

import jax
import jax.numpy as jnp
import numpy as np
from jax import lax
from jax.experimental import pallas as pl
from jax.experimental.pallas import tpu as pltpu
from jax.sharding import PartitionSpec as P

OFFSET = 5
screening = 5.44
LANES = 128
X_STEPS = 6
PLANE_STEPS = 3
FAR_ROWS = 40


def from_behind(value, axis, by):
    count = lax.axis_size(axis)
    return lax.ppermute(value, axis, [(i, (i + by) % count) for i in range(count)])


def screened_kernel(points):
    signed = jnp.arange(LANES, dtype=jnp.int32)
    inside = signed < points
    signed = jnp.where(signed >= points // 2, signed - points, signed)
    wavenumber = signed.astype(jnp.float32) * (2.0 * math.pi / points)
    squared = (
        wavenumber[:points, None, None] ** 2
        + wavenumber[None, :points, None] ** 2
        + wavenumber[None, None, :] ** 2
    )
    screen_rate = screening / points
    finite = jnp.where(squared > 0.0, squared, 1.0)
    screened = 4.0 * math.pi / finite * -jnp.expm1(-finite / (4.0 * screen_rate * screen_rate))
    kernel = jnp.where(squared > 0.0, screened, math.pi / (screen_rate * screen_rate))
    return jnp.where(inside, kernel / float(points * points * points), 0.0)


def hartley_tables(points):
    counter = np.arange(points)
    angles = 2.0 * np.pi * (counter[:, None] * counter[None, :] % points) / points
    table = np.cos(angles) + np.sin(angles)
    high = table.astype(jnp.bfloat16)
    low = (table - high.astype(np.float64)).astype(jnp.bfloat16)
    left = np.zeros((2 * points, 2 * points), jnp.bfloat16)
    left[:points, :points] = high
    left[:points, points:] = high
    left[points:, :points] = low
    right = np.zeros((2 * LANES, 2 * LANES), jnp.bfloat16)
    right[:points, :points] = high
    right[:points, LANES:LANES + points] = low
    right[LANES:LANES + points, :points] = high
    return jnp.asarray(left), jnp.asarray(right)


def two_terms(value):
    high = value.astype(jnp.bfloat16)
    low = (value - high.astype(jnp.float32)).astype(jnp.bfloat16)
    return high, low


def from_left(left, value):
    half = value.shape[0]
    terms = jnp.concatenate(two_terms(value), 0)
    out = jnp.dot(left, terms, preferred_element_type=jnp.float32)
    return out[:half] + out[half:]


def from_right(value, right):
    out = jnp.dot(jnp.concatenate(two_terms(value), 1), right, preferred_element_type=jnp.float32)
    return out[:, :LANES] + out[:, LANES:]


def pair_body(points, slot, has, *refs):
    refs = list(refs)
    flags_ref = refs.pop(0)
    names = ["a", "b"] + [name for name in ("sum_a", "sum_b") if name in has]
    far = {name: refs.pop(0) for name in names}
    if "then" in has:
        refs.pop(0)
    kernel_ref, left_ref, right_ref = refs.pop(0), refs.pop(0), refs.pop(0)
    out_refs = {"for_a": refs.pop(0)}
    if "halves" in has:
        out_refs["low_a"] = refs.pop(0)
    if "for_b" in has:
        out_refs["for_b"] = refs.pop(0)
    if "hand_on" in has:
        refs.pop(0)
    held, near, near_kernel, near_out, sems, kernel_sems, out_sems = refs
    outs = list(out_refs)
    step = pl.program_id(0)
    active = flags_ref[2 * slot] == 1
    with_sum = flags_ref[2 * slot + 1] == 1
    columns = near.shape[2] // X_STEPS
    ys = columns // points
    per_step = points // PLANE_STEPS
    late = X_STEPS + PLANE_STEPS

    def span_of(chunk):
        start = chunk * columns
        return pl.ds(start if isinstance(chunk, int) else pl.multiple_of(start, columns), columns)

    def fetch(name, chunk):
        place, span = names.index(name), span_of(chunk)
        return pltpu.make_async_copy(
            far[name].at[:, span], near.at[place, :, span], sems.at[place, chunk]
        )

    def fetch_kernel(part):
        span = pl.ds(part * per_step, per_step)
        return pltpu.make_async_copy(
            kernel_ref.at[span], near_kernel.at[span], kernel_sems.at[part]
        )

    def give(name, chunk):
        span = span_of(chunk)
        source = near_out.at[0 if name != "for_b" else 1]
        if "halves" in has and name != "for_b":
            rows = pl.ds(points - FAR_ROWS, FAR_ROWS) if name == "low_a" else pl.ds(0, points - FAR_ROWS)
            source = source.at[rows, span]
        else:
            source = source.at[:, span]
        return pltpu.make_async_copy(
            source, out_refs[name].at[:, span], out_sems.at[outs.index(name), chunk]
        )

    def here(name, chunk):
        return near[names.index(name), :, span_of(chunk)]

    sums = [name for name in names if name.startswith("sum")]

    @pl.when(active & (step == 0))
    def start_first():
        for chunk in range(2):
            for name in ("a", "b"):
                fetch(name, chunk).start()

    @pl.when(active & (step + 2 < X_STEPS))
    def start_next():
        for name in ("a", "b"):
            fetch(name, step + 2).start()

    @pl.when(active & (step == X_STEPS - 2))
    def start_kernel():
        for part in range(PLANE_STEPS):
            fetch_kernel(part).start()

    if sums:
        @pl.when(active & (step == X_STEPS))
        def start_sums():
            for chunk in range(X_STEPS):
                for name in sums:
                    fetch(name, chunk).start()

    def lanes_apart(block):
        gap = jnp.zeros((points, LANES - points), jnp.float32)
        rows = [
            jnp.concatenate([block[:, q * points:(q + 1) * points], gap], 1) for q in range(ys)
        ]
        return jnp.swapaxes(jnp.stack(rows, 0), 0, 1)

    def lanes_together(block):
        block = jnp.swapaxes(block, 0, 1)
        return jnp.concatenate([block[q][:, :points] for q in range(ys)], 1)

    def side_by_side(block):
        return jnp.concatenate([block[i] for i in range(per_step)], 1)

    @pl.when(active & (step < X_STEPS))
    def forward_x():
        for name in ("a", "b"):
            fetch(name, step).wait()
        spectrum = from_left(left_ref[...], here("a", step) * here("b", step))
        start = pl.multiple_of(step * ys, ys)
        held[:, pl.ds(start, ys), :] = lanes_apart(spectrum)

    @pl.when(active & (step >= X_STEPS) & (step < late))
    def planes():
        left = left_ref[...]
        right = right_ref[...]
        part = step - X_STEPS
        first = part * per_step
        block = held[pl.ds(first, per_step)].reshape(per_step * points, LANES)
        block = from_right(block, right).reshape(per_step, points, LANES)
        wide = from_left(left, side_by_side(block))
        fetch_kernel(part).wait()
        wide = from_left(left, wide * side_by_side(near_kernel[pl.ds(first, per_step)]))
        block = jnp.concatenate(
            [wide[:, i * LANES:(i + 1) * LANES] for i in range(per_step)], 0
        )
        block = from_right(block, right)
        held[pl.ds(first, per_step)] = block.reshape(per_step, points, LANES)

    @pl.when(active & (step >= late))
    def inverse_x():
        chunk = step - late
        start = pl.multiple_of(chunk * ys, ys)
        for name in sums:
            fetch(name, chunk).wait()
        block = lanes_together(held[:, pl.ds(start, ys), :])
        potential = from_left(left_ref[...], block)
        for_a = -(here("b", chunk) * potential)
        if "sum_a" in has:
            for_a = for_a + jnp.where(with_sum, here("sum_a", chunk), 0.0)
        near_out[0, :, span_of(chunk)] = for_a
        if "for_b" in has:
            for_b = -(here("a", chunk) * potential)
            if "sum_b" in has:
                for_b = for_b + here("sum_b", chunk)
            near_out[1, :, span_of(chunk)] = for_b
        for name in outs:
            give(name, chunk).start()

    @pl.when(active & (step == late + X_STEPS - 1))
    def wait_outs():
        for chunk in range(X_STEPS):
            for name in outs:
                give(name, chunk).wait()


def pair_terms(
    flags, slot, a, b, constants, sum_a=None, sum_b=None, for_b=False, halves=False, in_place=False, then=None, hand_on=False
):
    points, plane = a.shape
    kernel, left, right = constants
    optional = {"sum_a": sum_a, "sum_b": sum_b}
    optional = {name: value for name, value in optional.items() if value is not None}
    blocks = [a, b, *optional.values()]
    waited = [] if then is None else [then]
    has = list(optional) + ["for_b"] * for_b + ["halves"] * halves + ["then"] * len(waited)
    has += ["hand_on"] * hand_on
    rows = ([points - FAR_ROWS, FAR_ROWS] if halves else [points]) + [points] * for_b
    aliases = {3: 0} if in_place else {}
    if hand_on:
        aliases[1] = len(rows)
    anywhere = pl.BlockSpec(memory_space=pl.ANY)
    out = pl.pallas_call(
        functools.partial(pair_body, points, slot, has),
        grid=(2 * X_STEPS + PLANE_STEPS,),
        in_specs=[pl.BlockSpec(memory_space=pltpu.SMEM)]
        + [anywhere] * (len(blocks) + len(waited) + 1)
        + [pl.BlockSpec(table.shape, lambda i: (0, 0)) for table in (left, right)],
        out_specs=[anywhere] * (len(rows) + hand_on),
        out_shape=[
            jax.ShapeDtypeStruct((n, plane), jnp.float32) for n in rows + [points] * hand_on
        ],
        input_output_aliases=aliases,
        scratch_shapes=[
            pltpu.VMEM((points, points, LANES), jnp.float32),
            pltpu.VMEM((len(blocks), points, plane), jnp.float32),
            pltpu.VMEM((points, points, LANES), jnp.float32),
            pltpu.VMEM((2 if for_b else 1, points, plane), jnp.float32),
            pltpu.SemaphoreType.DMA((len(blocks), X_STEPS)),
            pltpu.SemaphoreType.DMA((PLANE_STEPS,)),
            pltpu.SemaphoreType.DMA((len(rows), X_STEPS)),
        ],
        compiler_params=pltpu.CompilerParams(vmem_limit_bytes=62 * 2**20),
        cost_estimate=pl.CostEstimate(
            flops=100_000_000, bytes_accessed=1_000_000, transcendentals=0
        ),
        name="pair_terms",
    )(flags, *blocks, *waited, kernel, left, right)
    return out if len(out) > 1 else out[0]


def copy_body(flags_ref, block_ref, new_block_ref):
    new_block_ref[...] = block_ref[...]


def copied(flags, block):
    points, plane = block.shape
    part = pl.BlockSpec((points, plane // X_STEPS), lambda i: (0, i))
    return pl.pallas_call(
        copy_body,
        grid=(X_STEPS,),
        in_specs=[pl.BlockSpec(memory_space=pltpu.SMEM), part],
        out_specs=part,
        out_shape=jax.ShapeDtypeStruct(block.shape, block.dtype),
        compiler_params=pltpu.CompilerParams(vmem_limit_bytes=62 * 2**20),
        name="copied",
    )(flags, block)


def gate_body(token_ref, left_ref, flags_ref, turned_ref, block_ref, new_left_ref, new_block_ref, near, sems):
    del token_ref, block_ref
    new_left_ref[...] = left_ref[...]
    columns = turned_ref.shape[1] // X_STEPS

    @pl.when(flags_ref[TURNS] == 1)
    def from_turned():
        spans = [pl.ds(i * columns, columns) for i in range(X_STEPS)]
        inward = [
            pltpu.make_async_copy(turned_ref.at[:, span], near.at[:, span], sems.at[0, i])
            for i, span in enumerate(spans)
        ]
        outward = [
            pltpu.make_async_copy(near.at[:, span], new_block_ref.at[:, span], sems.at[1, i])
            for i, span in enumerate(spans)
        ]
        for copy in inward:
            copy.start()
        for first, second in zip(inward, outward):
            first.wait()
            second.start()
        for copy in outward:
            copy.wait()


def gate(token, left, flags, turned, block):
    in_vmem = pl.BlockSpec(memory_space=pltpu.VMEM)
    in_smem = pl.BlockSpec(memory_space=pltpu.SMEM)
    anywhere = pl.BlockSpec(memory_space=pl.ANY)
    return pl.pallas_call(
        gate_body,
        in_specs=[in_vmem, in_vmem, in_smem, anywhere, anywhere],
        out_specs=[in_vmem, anywhere],
        out_shape=[
            jax.ShapeDtypeStruct(left.shape, left.dtype),
            jax.ShapeDtypeStruct(block.shape, block.dtype),
        ],
        input_output_aliases={4: 1},
        scratch_shapes=[
            pltpu.VMEM(block.shape, block.dtype),
            pltpu.SemaphoreType.DMA((2, X_STEPS)),
        ],
        compiler_params=pltpu.CompilerParams(vmem_limit_bytes=62 * 2**20),
        name="gate",
    )(token, left, flags, turned, block)


def hold_body(block_ref, then_ref, new_block_ref):
    del block_ref, then_ref, new_block_ref


def hold(block, then):
    anywhere = pl.BlockSpec(memory_space=pl.ANY)
    return pl.pallas_call(
        hold_body,
        in_specs=[anywhere, anywhere],
        out_specs=anywhere,
        out_shape=jax.ShapeDtypeStruct(block.shape, block.dtype),
        input_output_aliases={0: 0},
        compiler_params=pltpu.CompilerParams(vmem_limit_bytes=62 * 2**20),
        name="hold",
    )(block, then)


def both_halves(*pairs):
    return list(pairs) + [(15 - source, 15 - target) for source, target in pairs]


CROSSING = both_halves((3, 14), (4, 9))
PARTNERS = both_halves((8, 14), (15, 9), (9, 11), (14, 12))
ARRIVED = both_halves((14, 2), (9, 5))
SECOND = both_halves((5, 10), (2, 13), (11, 14), (12, 9))
BESIDE = both_halves((13, 14), (10, 9), (15, 10), (8, 13))
HOME_ACROSS = both_halves((9, 4), (14, 3))
HOME_FAR = both_halves((9, 15), (14, 8))
HOME_TURN = both_halves((9, 11), (14, 12))
HOME_TURNED = both_halves((11, 15), (12, 8))
TURNS = 10
FLAGS = {i: (1, 0, 1, 0, 1, 1, 0, 0, 1, 1, 0) for i in (9, 14, 6, 1)}
FLAGS.update({i: (0, 0, 0, 0, 0, 0, 1, 0, 1, 1, 0) for i in (10, 13, 5, 2)})
FLAGS.update({i: (0,) * TURNS + (1,) for i in (11, 12, 4, 3)})


def sixteen_bands(orbitals, constants):
    def send(value, pairs):
        return lax.ppermute(value[None], "band", pairs)[0]

    kernel, left, right = constants
    own = orbitals[0]
    flags = jnp.asarray([FLAGS.get(i, (0,) * (TURNS + 1)) for i in range(16)], jnp.int32)
    flags = flags[lax.axis_index("band")]
    pair = functools.partial(pair_terms, flags)
    crossed = send(own, CROSSING)
    partner = send(own, PARTNERS)
    own_copy = copied(flags, own)
    token = crossed[:8, :LANES] + kernel[0, :8] + own_copy[:8, :LANES]
    left, held_back = gate(send(token, ARRIVED), left, flags, partner, own_copy)
    constants = (kernel, left, right)
    beside = send(held_back, BESIDE)
    second = send(held_back, SECOND)

    partner_sum, crossed_sum = pair(0, partner, crossed, constants, for_b=True)
    own_sum, crossed_sum = pair(1, own, crossed, constants, sum_b=crossed_sum, for_b=True)
    home = send(crossed_sum, HOME_ACROSS)
    top, bottom = pair(
        2, partner, beside, constants, sum_a=partner_sum, halves=True, then=own_sum
    )
    bottom = send(bottom, HOME_TURN)
    top = send(top, HOME_FAR)
    own_sum = pair(3, own, beside, constants, sum_a=own_sum, in_place=True)
    own_sum = pair(4, own, second, constants, sum_a=own_sum)
    bottom = send(hold(bottom, own_sum), HOME_TURNED)
    own_sum = jnp.where(flags[8] == 1, own_sum, 0.0)
    return (own_sum + home + jnp.concatenate([top, bottom], 0))[None]


def any_bands(orbitals, constants):
    own = orbitals[0]
    flags = jnp.ones((4,), jnp.int32)
    lower = from_behind(orbitals, "band", OFFSET)[0]
    upper = from_behind(orbitals, "band", -OFFSET)[0]
    total = pair_terms(flags, 0, own, lower, constants)
    return pair_terms(flags, 1, own, upper, constants, sum_a=total)[None]


def local(bands, orbitals):
    points = orbitals.shape[1]
    constants = (screened_kernel(points), *hartley_tables(points))
    if bands == 16:
        return sixteen_bands(orbitals, constants)
    return any_bands(orbitals, constants)


def solution(mesh):
    return jax.shard_map(
        functools.partial(local, mesh.shape["band"]),
        mesh=mesh,
        in_specs=(P(("groups", "band"), None, None),),
        out_specs=P(("groups", "band"), None, None),
        check_vma=False,
    )
```

```python
import functools
import math

import jax
import jax.numpy as jnp
import numpy as np
from jax import lax
from jax.experimental import pallas as pl
from jax.experimental.pallas import tpu as pltpu
from jax.sharding import PartitionSpec as P

OFFSET = 5
screening = 5.44
LANES = 128
X_STEPS = 3
PLANE_STEPS = 1
FAR_ROWS = 40


def from_behind(value, axis, by):
    count = lax.axis_size(axis)
    return lax.ppermute(value, axis, [(i, (i + by) % count) for i in range(count)])


def screened_kernel(points):
    signed = jnp.arange(LANES, dtype=jnp.int32)
    inside = signed < points
    signed = jnp.where(signed >= points // 2, signed - points, signed)
    wavenumber = signed.astype(jnp.float32) * (2.0 * math.pi / points)
    squared = (
        wavenumber[:points, None, None] ** 2
        + wavenumber[None, :points, None] ** 2
        + wavenumber[None, None, :] ** 2
    )
    screen_rate = screening / points
    finite = jnp.where(squared > 0.0, squared, 1.0)
    screened = 4.0 * math.pi / finite * -jnp.expm1(-finite / (4.0 * screen_rate * screen_rate))
    kernel = jnp.where(squared > 0.0, screened, math.pi / (screen_rate * screen_rate))
    return jnp.where(inside, kernel / float(points * points * points), 0.0)


def hartley_tables(points):
    counter = np.arange(points)
    angles = 2.0 * np.pi * (counter[:, None] * counter[None, :] % points) / points
    table = np.cos(angles) + np.sin(angles)
    high = table.astype(jnp.bfloat16)
    low = (table - high.astype(np.float64)).astype(jnp.bfloat16)
    left = np.zeros((2 * points, 2 * points), jnp.bfloat16)
    left[:points, :points] = high
    left[:points, points:] = high
    left[points:, :points] = low
    right = np.zeros((2 * LANES, 2 * LANES), jnp.bfloat16)
    right[:points, :points] = high
    right[:points, LANES:LANES + points] = low
    right[LANES:LANES + points, :points] = high
    return jnp.asarray(left), jnp.asarray(right)


def two_terms(value):
    high = value.astype(jnp.bfloat16)
    low = (value - high.astype(jnp.float32)).astype(jnp.bfloat16)
    return high, low


def from_left(left, value):
    half = value.shape[0]
    terms = jnp.concatenate(two_terms(value), 0)
    out = jnp.dot(left, terms, preferred_element_type=jnp.float32)
    return out[:half] + out[half:]


def from_right(value, right):
    out = jnp.dot(jnp.concatenate(two_terms(value), 1), right, preferred_element_type=jnp.float32)
    return out[:, :LANES] + out[:, LANES:]


def pair_body(points, slot, has, *refs):
    refs = list(refs)
    flags_ref = refs.pop(0)
    names = ["a", "b"] + [name for name in ("sum_a", "sum_b") if name in has]
    far = {name: refs.pop(0) for name in names}
    if "then" in has:
        refs.pop(0)
    kernel_ref, left_ref, right_ref = refs.pop(0), refs.pop(0), refs.pop(0)
    out_refs = {"for_a": refs.pop(0)}
    if "halves" in has:
        out_refs["low_a"] = refs.pop(0)
    if "for_b" in has:
        out_refs["for_b"] = refs.pop(0)
    if "hand_on" in has:
        refs.pop(0)
    held, near, near_kernel, near_out, sems, kernel_sems, out_sems = refs
    outs = list(out_refs)
    step = pl.program_id(0)
    active = flags_ref[2 * slot] == 1
    with_sum = flags_ref[2 * slot + 1] == 1
    columns = near.shape[2] // X_STEPS
    ys = columns // points
    per_step = points // PLANE_STEPS
    late = X_STEPS + PLANE_STEPS

    def span_of(chunk):
        start = chunk * columns
        return pl.ds(start if isinstance(chunk, int) else pl.multiple_of(start, columns), columns)

    def fetch(name, chunk):
        place, span = names.index(name), span_of(chunk)
        return pltpu.make_async_copy(
            far[name].at[:, span], near.at[place, :, span], sems.at[place, chunk]
        )

    def fetch_kernel(part):
        span = pl.ds(part * per_step, per_step)
        return pltpu.make_async_copy(
            kernel_ref.at[span], near_kernel.at[span], kernel_sems.at[part]
        )

    def give(name, chunk):
        span = span_of(chunk)
        source = near_out.at[0 if name != "for_b" else 1]
        if "halves" in has and name != "for_b":
            rows = pl.ds(points - FAR_ROWS, FAR_ROWS) if name == "low_a" else pl.ds(0, points - FAR_ROWS)
            source = source.at[rows, span]
        else:
            source = source.at[:, span]
        return pltpu.make_async_copy(
            source, out_refs[name].at[:, span], out_sems.at[outs.index(name), chunk]
        )

    def here(name, chunk):
        return near[names.index(name), :, span_of(chunk)]

    sums = [name for name in names if name.startswith("sum")]

    @pl.when(active & (step == 0))
    def start_first():
        for chunk in range(2):
            for name in ("a", "b"):
                fetch(name, chunk).start()

    @pl.when(active & (step + 2 < X_STEPS))
    def start_next():
        for name in ("a", "b"):
            fetch(name, step + 2).start()

    @pl.when(active & (step == X_STEPS - 2))
    def start_kernel():
        for part in range(PLANE_STEPS):
            fetch_kernel(part).start()

    if sums:
        @pl.when(active & (step == X_STEPS))
        def start_sums():
            for chunk in range(X_STEPS):
                for name in sums:
                    fetch(name, chunk).start()

    def lanes_apart(block):
        gap = jnp.zeros((points, LANES - points), jnp.float32)
        rows = [
            jnp.concatenate([block[:, q * points:(q + 1) * points], gap], 1) for q in range(ys)
        ]
        return jnp.swapaxes(jnp.stack(rows, 0), 0, 1)

    def lanes_together(block):
        block = jnp.swapaxes(block, 0, 1)
        return jnp.concatenate([block[q][:, :points] for q in range(ys)], 1)

    def side_by_side(block):
        return jnp.concatenate([block[i] for i in range(per_step)], 1)

    @pl.when(active & (step < X_STEPS))
    def forward_x():
        for name in ("a", "b"):
            fetch(name, step).wait()
        spectrum = from_left(left_ref[...], here("a", step) * here("b", step))
        start = pl.multiple_of(step * ys, ys)
        held[:, pl.ds(start, ys), :] = lanes_apart(spectrum)

    @pl.when(active & (step >= X_STEPS) & (step < late))
    def planes():
        left = left_ref[...]
        right = right_ref[...]
        part = step - X_STEPS
        first = part * per_step
        block = held[pl.ds(first, per_step)].reshape(per_step * points, LANES)
        block = from_right(block, right).reshape(per_step, points, LANES)
        wide = from_left(left, side_by_side(block))
        fetch_kernel(part).wait()
        wide = from_left(left, wide * side_by_side(near_kernel[pl.ds(first, per_step)]))
        block = jnp.concatenate(
            [wide[:, i * LANES:(i + 1) * LANES] for i in range(per_step)], 0
        )
        block = from_right(block, right)
        held[pl.ds(first, per_step)] = block.reshape(per_step, points, LANES)

    @pl.when(active & (step >= late))
    def inverse_x():
        chunk = step - late
        start = pl.multiple_of(chunk * ys, ys)
        for name in sums:
            fetch(name, chunk).wait()
        block = lanes_together(held[:, pl.ds(start, ys), :])
        potential = from_left(left_ref[...], block)
        for_a = -(here("b", chunk) * potential)
        if "sum_a" in has:
            for_a = for_a + jnp.where(with_sum, here("sum_a", chunk), 0.0)
        near_out[0, :, span_of(chunk)] = for_a
        if "for_b" in has:
            for_b = -(here("a", chunk) * potential)
            if "sum_b" in has:
                for_b = for_b + here("sum_b", chunk)
            near_out[1, :, span_of(chunk)] = for_b
        for name in outs:
            give(name, chunk).start()

    @pl.when(active & (step == late + X_STEPS - 1))
    def wait_outs():
        for chunk in range(X_STEPS):
            for name in outs:
                give(name, chunk).wait()


def pair_terms(
    flags, slot, a, b, constants, sum_a=None, sum_b=None, for_b=False, halves=False, in_place=False, then=None, hand_on=False
):
    points, plane = a.shape
    kernel, left, right = constants
    optional = {"sum_a": sum_a, "sum_b": sum_b}
    optional = {name: value for name, value in optional.items() if value is not None}
    blocks = [a, b, *optional.values()]
    waited = [] if then is None else [then]
    has = list(optional) + ["for_b"] * for_b + ["halves"] * halves + ["then"] * len(waited)
    has += ["hand_on"] * hand_on
    rows = ([points - FAR_ROWS, FAR_ROWS] if halves else [points]) + [points] * for_b
    aliases = {3: 0} if in_place else {}
    if hand_on:
        aliases[1] = len(rows)
    anywhere = pl.BlockSpec(memory_space=pl.ANY)
    out = pl.pallas_call(
        functools.partial(pair_body, points, slot, has),
        grid=(2 * X_STEPS + PLANE_STEPS,),
        in_specs=[pl.BlockSpec(memory_space=pltpu.SMEM)]
        + [anywhere] * (len(blocks) + len(waited) + 1)
        + [pl.BlockSpec(table.shape, lambda i: (0, 0)) for table in (left, right)],
        out_specs=[anywhere] * (len(rows) + hand_on),
        out_shape=[
            jax.ShapeDtypeStruct((n, plane), jnp.float32) for n in rows + [points] * hand_on
        ],
        input_output_aliases=aliases,
        scratch_shapes=[
            pltpu.VMEM((points, points, LANES), jnp.float32),
            pltpu.VMEM((len(blocks), points, plane), jnp.float32),
            pltpu.VMEM((points, points, LANES), jnp.float32),
            pltpu.VMEM((2 if for_b else 1, points, plane), jnp.float32),
            pltpu.SemaphoreType.DMA((len(blocks), X_STEPS)),
            pltpu.SemaphoreType.DMA((PLANE_STEPS,)),
            pltpu.SemaphoreType.DMA((len(rows), X_STEPS)),
        ],
        compiler_params=pltpu.CompilerParams(vmem_limit_bytes=62 * 2**20),
        cost_estimate=pl.CostEstimate(
            flops=100_000_000, bytes_accessed=1_000_000, transcendentals=0
        ),
        name="pair_terms",
    )(flags, *blocks, *waited, kernel, left, right)
    return out if len(out) > 1 else out[0]


def copy_body(flags_ref, block_ref, new_block_ref):
    new_block_ref[...] = block_ref[...]


def copied(flags, block):
    points, plane = block.shape
    part = pl.BlockSpec((points, plane // X_STEPS), lambda i: (0, i))
    return pl.pallas_call(
        copy_body,
        grid=(X_STEPS,),
        in_specs=[pl.BlockSpec(memory_space=pltpu.SMEM), part],
        out_specs=part,
        out_shape=jax.ShapeDtypeStruct(block.shape, block.dtype),
        compiler_params=pltpu.CompilerParams(vmem_limit_bytes=62 * 2**20),
        name="copied",
    )(flags, block)


def gate_body(token_ref, left_ref, partner_ref, block_ref, new_left_ref, new_block_ref):
    del token_ref, partner_ref, block_ref, new_block_ref
    new_left_ref[...] = left_ref[...]


def gate(token, left, partner, block):
    in_vmem = pl.BlockSpec(memory_space=pltpu.VMEM)
    anywhere = pl.BlockSpec(memory_space=pl.ANY)
    return pl.pallas_call(
        gate_body,
        in_specs=[in_vmem, in_vmem, anywhere, anywhere],
        out_specs=[in_vmem, anywhere],
        out_shape=[
            jax.ShapeDtypeStruct(left.shape, left.dtype),
            jax.ShapeDtypeStruct(block.shape, block.dtype),
        ],
        input_output_aliases={3: 1},
        compiler_params=pltpu.CompilerParams(vmem_limit_bytes=62 * 2**20),
        name="gate",
    )(token, left, partner, block)


def hold_body(block_ref, then_ref, new_block_ref):
    del block_ref, then_ref, new_block_ref


def hold(block, then):
    anywhere = pl.BlockSpec(memory_space=pl.ANY)
    return pl.pallas_call(
        hold_body,
        in_specs=[anywhere, anywhere],
        out_specs=anywhere,
        out_shape=jax.ShapeDtypeStruct(block.shape, block.dtype),
        input_output_aliases={0: 0},
        compiler_params=pltpu.CompilerParams(vmem_limit_bytes=62 * 2**20),
        name="hold",
    )(block, then)


def both_halves(*pairs):
    return list(pairs) + [(15 - source, 15 - target) for source, target in pairs]


CROSSING = both_halves((3, 14), (4, 9))
PARTNERS = both_halves((8, 14), (15, 9), (9, 11), (14, 12))
ARRIVED = both_halves((14, 2), (9, 5))
SINGLES = both_halves((5, 10), (2, 13))
TURNED = both_halves((11, 14), (12, 9))
BESIDE = both_halves((13, 14), (10, 9), (15, 10), (8, 13))
HOME_ACROSS = both_halves((9, 4), (14, 3))
HOME_FAR = both_halves((9, 15), (14, 8))
HOME_TURN = both_halves((9, 11), (14, 12))
HOME_TURNED = both_halves((11, 15), (12, 8))
HAS_PAIRS = 12
FLAGS = {i: (1, 0, 1, 0, 1, 1, 0, 0, 0, 0, 1, 1, 1) for i in (9, 14, 6, 1)}
FLAGS.update({i: (0, 0, 0, 0, 0, 0, 1, 0, 1, 1, 0, 0, 1) for i in (10, 13, 5, 2)})


def sixteen_bands(orbitals, constants):
    def send(value, pairs):
        return lax.ppermute(value[None], "band", pairs)[0]

    kernel, left, right = constants
    own = orbitals[0]
    flags = jnp.asarray([FLAGS.get(i, (0,) * (HAS_PAIRS + 1)) for i in range(16)], jnp.int32)
    flags = flags[lax.axis_index("band")]
    pair = functools.partial(pair_terms, flags)
    crossed = send(own, CROSSING)
    partner = send(own, PARTNERS)
    own_copy = copied(flags, own)
    token = crossed[:8, :LANES] + kernel[0, :8] + own_copy[:8, :LANES]
    left, held_back = gate(send(token, ARRIVED), left, partner, own_copy)
    constants = (kernel, left, right)
    beside = send(held_back, BESIDE)
    single = send(held_back, SINGLES)

    partner_sum, crossed_sum = pair(0, partner, crossed, constants, for_b=True)
    own_sum, crossed_sum = pair(1, own, crossed, constants, sum_b=crossed_sum, for_b=True)
    home = send(crossed_sum, HOME_ACROSS)
    partner = hold(partner, own_sum)
    turned = send(partner, TURNED)
    top, bottom = pair(2, partner, beside, constants, sum_a=partner_sum, halves=True)
    bottom = send(bottom, HOME_TURN)
    top = send(top, HOME_FAR)
    own_sum = pair(3, own, beside, constants, sum_a=own_sum, in_place=True)
    own_sum = pair(4, own, single, constants, sum_a=own_sum, in_place=True)
    own_sum = pair(5, own, turned, constants, sum_a=own_sum, in_place=True)
    bottom = send(hold(bottom, own_sum), HOME_TURNED)
    own_sum = jnp.where(flags[HAS_PAIRS] == 1, own_sum, 0.0)
    return (own_sum + home + jnp.concatenate([top, bottom], 0))[None]


def any_bands(orbitals, constants):
    own = orbitals[0]
    flags = jnp.ones((4,), jnp.int32)
    lower = from_behind(orbitals, "band", OFFSET)[0]
    upper = from_behind(orbitals, "band", -OFFSET)[0]
    total = pair_terms(flags, 0, own, lower, constants)
    return pair_terms(flags, 1, own, upper, constants, sum_a=total)[None]


def local(bands, orbitals):
    points = orbitals.shape[1]
    constants = (screened_kernel(points), *hartley_tables(points))
    if bands == 16:
        return sixteen_bands(orbitals, constants)
    return any_bands(orbitals, constants)


def solution(mesh):
    return jax.shard_map(
        functools.partial(local, mesh.shape["band"]),
        mesh=mesh,
        in_specs=(P(("groups", "band"), None, None),),
        out_specs=P(("groups", "band"), None, None),
        check_vma=False,
    )
```

```python
import functools
import math

import jax
import jax.numpy as jnp
import numpy as np
from jax import lax
from jax.experimental import pallas as pl
from jax.experimental.pallas import tpu as pltpu
from jax.sharding import PartitionSpec as P

OFFSET = 5
screening = 5.44
LANES = 128
X_STEPS = 3
PLANE_STEPS = 2
FILL_STEPS = 6
FAR_ROWS = 40


def from_behind(value, axis, by):
    count = lax.axis_size(axis)
    return lax.ppermute(value, axis, [(i, (i + by) % count) for i in range(count)])


def screened_kernel(points):
    signed = jnp.arange(LANES, dtype=jnp.int32)
    inside = signed < points
    signed = jnp.where(signed >= points // 2, signed - points, signed)
    wavenumber = signed.astype(jnp.float32) * (2.0 * math.pi / points)
    squared = (
        wavenumber[:points, None, None] ** 2
        + wavenumber[None, :points, None] ** 2
        + wavenumber[None, None, :] ** 2
    )
    screen_rate = screening / points
    finite = jnp.where(squared > 0.0, squared, 1.0)
    screened = 4.0 * math.pi / finite * -jnp.expm1(-finite / (4.0 * screen_rate * screen_rate))
    kernel = jnp.where(squared > 0.0, screened, math.pi / (screen_rate * screen_rate))
    return jnp.where(inside, kernel / float(points * points * points), 0.0)


def hartley_tables(points):
    counter = np.arange(points)
    angles = 2.0 * np.pi * (counter[:, None] * counter[None, :] % points) / points
    table = np.cos(angles) + np.sin(angles)
    high = table.astype(jnp.bfloat16)
    low = (table - high.astype(np.float64)).astype(jnp.bfloat16)
    left = np.zeros((2 * points, 2 * points), jnp.bfloat16)
    left[:points, :points] = high
    left[:points, points:] = high
    left[points:, :points] = low
    right = np.zeros((2 * LANES, 2 * LANES), jnp.bfloat16)
    right[:points, :points] = high
    right[:points, LANES:LANES + points] = low
    right[LANES:LANES + points, :points] = high
    return jnp.asarray(left), jnp.asarray(right)


def two_terms(value):
    high = value.astype(jnp.bfloat16)
    low = (value - high.astype(jnp.float32)).astype(jnp.bfloat16)
    return high, low


def from_left(left, value):
    half = value.shape[0]
    terms = jnp.concatenate(two_terms(value), 0)
    out = jnp.dot(left, terms, preferred_element_type=jnp.float32)
    return out[:half] + out[half:]


def from_right(value, right):
    out = jnp.dot(jnp.concatenate(two_terms(value), 1), right, preferred_element_type=jnp.float32)
    return out[:, :LANES] + out[:, LANES:]


def pair_body(points, slot, has, *refs):
    refs = list(refs)
    flags_ref = refs.pop(0)
    names = ["a", "b"] + [name for name in ("sum_a", "sum_b") if name in has]
    far = {name: refs.pop(0) for name in names}
    if "then" in has:
        refs.pop(0)
    kernel_ref, left_ref, right_ref = refs.pop(0), refs.pop(0), refs.pop(0)
    out_refs = {"for_a": refs.pop(0)}
    if "halves" in has:
        out_refs["low_a"] = refs.pop(0)
    if "for_b" in has:
        out_refs["for_b"] = refs.pop(0)
    if "hand_on" in has:
        refs.pop(0)
    held, near, near_kernel, near_out, sems, kernel_sems, out_sems = refs
    outs = list(out_refs)
    step = pl.program_id(0)
    active = flags_ref[2 * slot] == 1
    with_sum = flags_ref[2 * slot + 1] == 1
    columns = near.shape[2] // X_STEPS
    ys = columns // points
    per_step = points // PLANE_STEPS
    late = X_STEPS + PLANE_STEPS

    def span_of(chunk):
        start = chunk * columns
        return pl.ds(start if isinstance(chunk, int) else pl.multiple_of(start, columns), columns)

    def fetch(name, chunk):
        place, span = names.index(name), span_of(chunk)
        return pltpu.make_async_copy(
            far[name].at[:, span], near.at[place, :, span], sems.at[place, chunk]
        )

    def fetch_kernel(part):
        span = pl.ds(part * per_step, per_step)
        return pltpu.make_async_copy(
            kernel_ref.at[span], near_kernel.at[span], kernel_sems.at[part]
        )

    def give(name, chunk):
        span = span_of(chunk)
        source = near_out.at[0 if name != "for_b" else 1]
        if "halves" in has and name != "for_b":
            rows = pl.ds(points - FAR_ROWS, FAR_ROWS) if name == "low_a" else pl.ds(0, points - FAR_ROWS)
            source = source.at[rows, span]
        else:
            source = source.at[:, span]
        return pltpu.make_async_copy(
            source, out_refs[name].at[:, span], out_sems.at[outs.index(name), chunk]
        )

    def here(name, chunk):
        return near[names.index(name), :, span_of(chunk)]

    sums = [name for name in names if name.startswith("sum")]

    @pl.when(active & (step == 0))
    def start_first():
        for chunk in range(2):
            for name in ("a", "b"):
                fetch(name, chunk).start()

    @pl.when(active & (step + 2 < X_STEPS))
    def start_next():
        for name in ("a", "b"):
            fetch(name, step + 2).start()

    @pl.when(active & (step == X_STEPS - 2))
    def start_kernel():
        for part in range(PLANE_STEPS):
            fetch_kernel(part).start()

    if sums:
        @pl.when(active & (step == X_STEPS))
        def start_sums():
            for chunk in range(X_STEPS):
                for name in sums:
                    fetch(name, chunk).start()

    def lanes_apart(block):
        gap = jnp.zeros((points, LANES - points), jnp.float32)
        rows = [
            jnp.concatenate([block[:, q * points:(q + 1) * points], gap], 1) for q in range(ys)
        ]
        return jnp.swapaxes(jnp.stack(rows, 0), 0, 1)

    def lanes_together(block):
        block = jnp.swapaxes(block, 0, 1)
        return jnp.concatenate([block[q][:, :points] for q in range(ys)], 1)

    def side_by_side(block):
        return jnp.concatenate([block[i] for i in range(per_step)], 1)

    @pl.when(active & (step < X_STEPS))
    def forward_x():
        for name in ("a", "b"):
            fetch(name, step).wait()
        spectrum = from_left(left_ref[...], here("a", step) * here("b", step))
        start = pl.multiple_of(step * ys, ys)
        held[:, pl.ds(start, ys), :] = lanes_apart(spectrum)

    @pl.when(active & (step >= X_STEPS) & (step < late))
    def planes():
        left = left_ref[...]
        right = right_ref[...]
        part = step - X_STEPS
        first = part * per_step
        block = held[pl.ds(first, per_step)].reshape(per_step * points, LANES)
        block = from_right(block, right).reshape(per_step, points, LANES)
        wide = from_left(left, side_by_side(block))
        fetch_kernel(part).wait()
        wide = from_left(left, wide * side_by_side(near_kernel[pl.ds(first, per_step)]))
        block = jnp.concatenate(
            [wide[:, i * LANES:(i + 1) * LANES] for i in range(per_step)], 0
        )
        block = from_right(block, right)
        held[pl.ds(first, per_step)] = block.reshape(per_step, points, LANES)

    @pl.when(active & (step >= late))
    def inverse_x():
        chunk = step - late
        start = pl.multiple_of(chunk * ys, ys)
        for name in sums:
            fetch(name, chunk).wait()
        block = lanes_together(held[:, pl.ds(start, ys), :])
        potential = from_left(left_ref[...], block)
        for_a = -(here("b", chunk) * potential)
        if "sum_a" in has:
            for_a = for_a + jnp.where(with_sum, here("sum_a", chunk), 0.0)
        near_out[0, :, span_of(chunk)] = for_a
        if "for_b" in has:
            for_b = -(here("a", chunk) * potential)
            if "sum_b" in has:
                for_b = for_b + here("sum_b", chunk)
            near_out[1, :, span_of(chunk)] = for_b
        for name in outs:
            give(name, chunk).start()

    @pl.when(active & (step == late + X_STEPS - 1))
    def wait_outs():
        for chunk in range(X_STEPS):
            for name in outs:
                give(name, chunk).wait()


def pair_terms(
    flags, slot, a, b, constants, sum_a=None, sum_b=None, for_b=False, halves=False, in_place=False, then=None, hand_on=False
):
    points, plane = a.shape
    kernel, left, right = constants
    optional = {"sum_a": sum_a, "sum_b": sum_b}
    optional = {name: value for name, value in optional.items() if value is not None}
    blocks = [a, b, *optional.values()]
    waited = [] if then is None else [then]
    has = list(optional) + ["for_b"] * for_b + ["halves"] * halves + ["then"] * len(waited)
    has += ["hand_on"] * hand_on
    rows = ([points - FAR_ROWS, FAR_ROWS] if halves else [points]) + [points] * for_b
    aliases = {3: 0} if in_place else {}
    if hand_on:
        aliases[1] = len(rows)
    anywhere = pl.BlockSpec(memory_space=pl.ANY)
    out = pl.pallas_call(
        functools.partial(pair_body, points, slot, has),
        grid=(2 * X_STEPS + PLANE_STEPS,),
        in_specs=[pl.BlockSpec(memory_space=pltpu.SMEM)]
        + [anywhere] * (len(blocks) + len(waited) + 1)
        + [pl.BlockSpec(table.shape, lambda i: (0, 0)) for table in (left, right)],
        out_specs=[anywhere] * (len(rows) + hand_on),
        out_shape=[
            jax.ShapeDtypeStruct((n, plane), jnp.float32) for n in rows + [points] * hand_on
        ],
        input_output_aliases=aliases,
        scratch_shapes=[
            pltpu.VMEM((points, points, LANES), jnp.float32),
            pltpu.VMEM((len(blocks), points, plane), jnp.float32),
            pltpu.VMEM((points, points, LANES), jnp.float32),
            pltpu.VMEM((2 if for_b else 1, points, plane), jnp.float32),
            pltpu.SemaphoreType.DMA((len(blocks), X_STEPS)),
            pltpu.SemaphoreType.DMA((PLANE_STEPS,)),
            pltpu.SemaphoreType.DMA((len(rows), X_STEPS)),
        ],
        compiler_params=pltpu.CompilerParams(vmem_limit_bytes=62 * 2**20),
        cost_estimate=pl.CostEstimate(
            flops=100_000_000, bytes_accessed=1_000_000, transcendentals=0
        ),
        name="pair_terms",
    )(flags, *blocks, *waited, kernel, left, right)
    return out if len(out) > 1 else out[0]


def copy_body(flags_ref, block_ref, new_block_ref):
    new_block_ref[...] = block_ref[...]


def copied(flags, block):
    points, plane = block.shape
    part = pl.BlockSpec((points, plane // X_STEPS), lambda i: (0, i))
    return pl.pallas_call(
        copy_body,
        grid=(X_STEPS,),
        in_specs=[pl.BlockSpec(memory_space=pltpu.SMEM), part],
        out_specs=part,
        out_shape=jax.ShapeDtypeStruct(block.shape, block.dtype),
        compiler_params=pltpu.CompilerParams(vmem_limit_bytes=62 * 2**20),
        name="copied",
    )(flags, block)


def gate_body(token_ref, left_ref, partner_ref, block_ref, new_left_ref, new_block_ref):
    del token_ref, partner_ref, block_ref, new_block_ref
    new_left_ref[...] = left_ref[...]


def gate(token, left, partner, block):
    in_vmem = pl.BlockSpec(memory_space=pltpu.VMEM)
    anywhere = pl.BlockSpec(memory_space=pl.ANY)
    return pl.pallas_call(
        gate_body,
        in_specs=[in_vmem, in_vmem, anywhere, anywhere],
        out_specs=[in_vmem, anywhere],
        out_shape=[
            jax.ShapeDtypeStruct(left.shape, left.dtype),
            jax.ShapeDtypeStruct(block.shape, block.dtype),
        ],
        input_output_aliases={3: 1},
        compiler_params=pltpu.CompilerParams(vmem_limit_bytes=62 * 2**20),
        name="gate",
    )(token, left, partner, block)


def hold_body(fills, *refs):
    if not fills:
        return
    flags_ref, own_ref, block_ref, then_ref, new_block_ref, near, sems = refs
    del block_ref, then_ref
    columns = own_ref.shape[1] // FILL_STEPS

    @pl.when(flags_ref[FILLS] == 1)
    def fill():
        spans = [pl.ds(i * columns, columns) for i in range(FILL_STEPS)]
        inward = [
            pltpu.make_async_copy(own_ref.at[:, span], near.at[:, span], sems.at[0, i])
            for i, span in enumerate(spans)
        ]
        outward = [
            pltpu.make_async_copy(near.at[:, span], new_block_ref.at[:, span], sems.at[1, i])
            for i, span in enumerate(spans)
        ]
        for copy in inward:
            copy.start()
        for first, second in zip(inward, outward):
            first.wait()
            second.start()
        for copy in outward:
            copy.wait()


def hold(block, then, flags=None, own=None):
    anywhere = pl.BlockSpec(memory_space=pl.ANY)
    fills = own is not None
    return pl.pallas_call(
        functools.partial(hold_body, fills),
        in_specs=[pl.BlockSpec(memory_space=pltpu.SMEM), anywhere] * fills + [anywhere, anywhere],
        out_specs=anywhere,
        out_shape=jax.ShapeDtypeStruct(block.shape, block.dtype),
        input_output_aliases={2 * fills: 0},
        scratch_shapes=[
            pltpu.VMEM(block.shape, block.dtype),
            pltpu.SemaphoreType.DMA((2, FILL_STEPS)),
        ] * fills,
        compiler_params=pltpu.CompilerParams(vmem_limit_bytes=62 * 2**20),
        name="hold",
    )(*([flags, own] * fills), block, then)


def both_halves(*pairs):
    return list(pairs) + [(15 - source, 15 - target) for source, target in pairs]


CROSSING = both_halves((3, 14), (4, 9))
PARTNERS = both_halves((8, 14), (15, 9), (9, 11), (14, 12))
ARRIVED = both_halves((14, 2), (9, 5))
SINGLES = both_halves((5, 10), (2, 13))
BESIDE = both_halves((13, 14), (10, 9))
PASSED = both_halves((11, 14), (12, 9), (15, 10), (8, 13))
HOME_ACROSS = both_halves((9, 4), (14, 3))
HOME_FAR = both_halves((9, 15), (14, 8))
HOME_TURN = both_halves((9, 11), (14, 12))
HOME_TURNED = both_halves((11, 15), (12, 8))
HAS_PAIRS, FILLS = 10, 11
FLAGS = {i: (1, 0, 1, 0, 1, 1, 0, 0, 1, 1, 1, 0) for i in (9, 14, 6, 1)}
FLAGS.update({i: (0, 0, 0, 0, 0, 0, 1, 0, 1, 1, 1, 0) for i in (10, 13, 5, 2)})
FLAGS.update({i: (0,) * 11 + (1,) for i in (15, 8, 0, 7)})


def sixteen_bands(orbitals, constants):
    def send(value, pairs):
        return lax.ppermute(value[None], "band", pairs)[0]

    kernel, left, right = constants
    own = orbitals[0]
    flags = jnp.asarray([FLAGS.get(i, (0,) * 12) for i in range(16)], jnp.int32)
    flags = flags[lax.axis_index("band")]
    pair = functools.partial(pair_terms, flags)
    crossed = send(own, CROSSING)
    partner = send(own, PARTNERS)
    own_copy = copied(flags, own)
    token = crossed[:8, :LANES] + kernel[0, :8] + own_copy[:8, :LANES]
    left, held_back = gate(send(token, ARRIVED), left, partner, own_copy)
    constants = (kernel, left, right)
    beside = send(held_back, BESIDE)
    single = send(held_back, SINGLES)

    partner_sum, crossed_sum = pair(0, partner, crossed, constants, for_b=True)
    partner = hold(partner, partner_sum, flags, own)
    passed = send(partner, PASSED)
    own_sum, crossed_sum = pair(1, own, crossed, constants, sum_b=crossed_sum, for_b=True)
    home = send(crossed_sum, HOME_ACROSS)
    top, bottom = pair(2, partner, beside, constants, sum_a=partner_sum, halves=True)
    bottom = send(bottom, HOME_TURN)
    top = send(top, HOME_FAR)
    own_sum = pair(3, own, single, constants, sum_a=own_sum, in_place=True)
    own_sum = pair(4, own, passed, constants, sum_a=own_sum, in_place=True)
    bottom = send(hold(bottom, own_sum), HOME_TURNED)
    own_sum = jnp.where(flags[HAS_PAIRS] == 1, own_sum, 0.0)
    return (own_sum + home + jnp.concatenate([top, bottom], 0))[None]


def any_bands(orbitals, constants):
    own = orbitals[0]
    flags = jnp.ones((4,), jnp.int32)
    lower = from_behind(orbitals, "band", OFFSET)[0]
    upper = from_behind(orbitals, "band", -OFFSET)[0]
    total = pair_terms(flags, 0, own, lower, constants)
    return pair_terms(flags, 1, own, upper, constants, sum_a=total)[None]


def local(bands, orbitals):
    points = orbitals.shape[1]
    constants = (screened_kernel(points), *hartley_tables(points))
    if bands == 16:
        return sixteen_bands(orbitals, constants)
    return any_bands(orbitals, constants)


def solution(mesh):
    return jax.shard_map(
        functools.partial(local, mesh.shape["band"]),
        mesh=mesh,
        in_specs=(P(("groups", "band"), None, None),),
        out_specs=P(("groups", "band"), None, None),
        check_vma=False,
    )
```

```python
import functools
import math

import jax
import jax.numpy as jnp
import numpy as np
from jax import lax
from jax.experimental import pallas as pl
from jax.experimental.pallas import tpu as pltpu
from jax.sharding import PartitionSpec as P

OFFSET = 5
screening = 5.44
LANES = 128
X_STEPS = 3
PLANE_STEPS = 2
SETTLE_STEPS = 6
FAR_ROWS = 40


def from_behind(value, axis, by):
    count = lax.axis_size(axis)
    return lax.ppermute(value, axis, [(i, (i + by) % count) for i in range(count)])


def screened_kernel(points):
    signed = jnp.arange(LANES, dtype=jnp.int32)
    inside = signed < points
    signed = jnp.where(signed >= points // 2, signed - points, signed)
    wavenumber = signed.astype(jnp.float32) * (2.0 * math.pi / points)
    squared = (
        wavenumber[:points, None, None] ** 2
        + wavenumber[None, :points, None] ** 2
        + wavenumber[None, None, :] ** 2
    )
    screen_rate = screening / points
    finite = jnp.where(squared > 0.0, squared, 1.0)
    screened = 4.0 * math.pi / finite * -jnp.expm1(-finite / (4.0 * screen_rate * screen_rate))
    kernel = jnp.where(squared > 0.0, screened, math.pi / (screen_rate * screen_rate))
    return jnp.where(inside, kernel / float(points * points * points), 0.0)


def hartley_tables(points):
    counter = np.arange(points)
    angles = 2.0 * np.pi * (counter[:, None] * counter[None, :] % points) / points
    table = np.cos(angles) + np.sin(angles)
    high = table.astype(jnp.bfloat16)
    low = (table - high.astype(np.float64)).astype(jnp.bfloat16)
    left = np.zeros((2 * points, 2 * points), jnp.bfloat16)
    left[:points, :points] = high
    left[:points, points:] = high
    left[points:, :points] = low
    right = np.zeros((2 * LANES, 2 * LANES), jnp.bfloat16)
    right[:points, :points] = high
    right[:points, LANES:LANES + points] = low
    right[LANES:LANES + points, :points] = high
    return jnp.asarray(left), jnp.asarray(right)


def two_terms(value):
    high = value.astype(jnp.bfloat16)
    low = (value - high.astype(jnp.float32)).astype(jnp.bfloat16)
    return high, low


def from_left(left, value):
    half = value.shape[0]
    terms = jnp.concatenate(two_terms(value), 0)
    out = jnp.dot(left, terms, preferred_element_type=jnp.float32)
    return out[:half] + out[half:]


def from_right(value, right):
    out = jnp.dot(jnp.concatenate(two_terms(value), 1), right, preferred_element_type=jnp.float32)
    return out[:, :LANES] + out[:, LANES:]


def pair_body(points, slot, has, *refs):
    refs = list(refs)
    flags_ref = refs.pop(0)
    names = ["a", "b"] + [name for name in ("sum_a", "sum_b") if name in has]
    far = {name: refs.pop(0) for name in names}
    if "then" in has:
        refs.pop(0)
    kernel_ref, left_ref, right_ref = refs.pop(0), refs.pop(0), refs.pop(0)
    out_refs = {"for_a": refs.pop(0)}
    if "halves" in has:
        out_refs["low_a"] = refs.pop(0)
    if "for_b" in has:
        out_refs["for_b"] = refs.pop(0)
    if "hand_on" in has:
        refs.pop(0)
    held, near, near_kernel, near_out, sems, kernel_sems, out_sems = refs
    outs = list(out_refs)
    step = pl.program_id(0)
    active = flags_ref[2 * slot] == 1
    with_sum = flags_ref[2 * slot + 1] == 1
    columns = near.shape[2] // X_STEPS
    ys = columns // points
    per_step = points // PLANE_STEPS
    late = X_STEPS + PLANE_STEPS

    def span_of(chunk):
        start = chunk * columns
        return pl.ds(start if isinstance(chunk, int) else pl.multiple_of(start, columns), columns)

    def fetch(name, chunk):
        place, span = names.index(name), span_of(chunk)
        return pltpu.make_async_copy(
            far[name].at[:, span], near.at[place, :, span], sems.at[place, chunk]
        )

    def fetch_kernel(part):
        span = pl.ds(part * per_step, per_step)
        return pltpu.make_async_copy(
            kernel_ref.at[span], near_kernel.at[span], kernel_sems.at[part]
        )

    def give(name, chunk):
        span = span_of(chunk)
        source = near_out.at[0 if name != "for_b" else 1]
        if "halves" in has and name != "for_b":
            rows = pl.ds(points - FAR_ROWS, FAR_ROWS) if name == "low_a" else pl.ds(0, points - FAR_ROWS)
            source = source.at[rows, span]
        else:
            source = source.at[:, span]
        return pltpu.make_async_copy(
            source, out_refs[name].at[:, span], out_sems.at[outs.index(name), chunk]
        )

    def here(name, chunk):
        return near[names.index(name), :, span_of(chunk)]

    sums = [name for name in names if name.startswith("sum")]

    @pl.when(active & (step == 0))
    def start_first():
        for chunk in range(2):
            for name in ("a", "b"):
                fetch(name, chunk).start()

    @pl.when(active & (step + 2 < X_STEPS))
    def start_next():
        for name in ("a", "b"):
            fetch(name, step + 2).start()

    @pl.when(active & (step == X_STEPS - 2))
    def start_kernel():
        for part in range(PLANE_STEPS):
            fetch_kernel(part).start()

    if sums:
        @pl.when(active & (step == X_STEPS))
        def start_sums():
            for chunk in range(X_STEPS):
                for name in sums:
                    fetch(name, chunk).start()

    def lanes_apart(block):
        gap = jnp.zeros((points, LANES - points), jnp.float32)
        rows = [
            jnp.concatenate([block[:, q * points:(q + 1) * points], gap], 1) for q in range(ys)
        ]
        return jnp.swapaxes(jnp.stack(rows, 0), 0, 1)

    def lanes_together(block):
        block = jnp.swapaxes(block, 0, 1)
        return jnp.concatenate([block[q][:, :points] for q in range(ys)], 1)

    def side_by_side(block):
        return jnp.concatenate([block[i] for i in range(per_step)], 1)

    @pl.when(active & (step < X_STEPS))
    def forward_x():
        for name in ("a", "b"):
            fetch(name, step).wait()
        spectrum = from_left(left_ref[...], here("a", step) * here("b", step))
        start = pl.multiple_of(step * ys, ys)
        held[:, pl.ds(start, ys), :] = lanes_apart(spectrum)

    @pl.when(active & (step >= X_STEPS) & (step < late))
    def planes():
        left = left_ref[...]
        right = right_ref[...]
        part = step - X_STEPS
        first = part * per_step
        block = held[pl.ds(first, per_step)].reshape(per_step * points, LANES)
        block = from_right(block, right).reshape(per_step, points, LANES)
        wide = from_left(left, side_by_side(block))
        fetch_kernel(part).wait()
        wide = from_left(left, wide * side_by_side(near_kernel[pl.ds(first, per_step)]))
        block = jnp.concatenate(
            [wide[:, i * LANES:(i + 1) * LANES] for i in range(per_step)], 0
        )
        block = from_right(block, right)
        held[pl.ds(first, per_step)] = block.reshape(per_step, points, LANES)

    @pl.when(active & (step >= late))
    def inverse_x():
        chunk = step - late
        start = pl.multiple_of(chunk * ys, ys)
        for name in sums:
            fetch(name, chunk).wait()
        block = lanes_together(held[:, pl.ds(start, ys), :])
        potential = from_left(left_ref[...], block)
        for_a = -(here("b", chunk) * potential)
        if "sum_a" in has:
            for_a = for_a + jnp.where(with_sum, here("sum_a", chunk), 0.0)
        near_out[0, :, span_of(chunk)] = for_a
        if "for_b" in has:
            for_b = -(here("a", chunk) * potential)
            if "sum_b" in has:
                for_b = for_b + here("sum_b", chunk)
            near_out[1, :, span_of(chunk)] = for_b
        for name in outs:
            give(name, chunk).start()

    @pl.when(active & (step == late + X_STEPS - 1))
    def wait_outs():
        for chunk in range(X_STEPS):
            for name in outs:
                give(name, chunk).wait()


def pair_terms(
    flags, slot, a, b, constants, sum_a=None, sum_b=None, for_b=False, halves=False, in_place=False, then=None, hand_on=False
):
    points, plane = a.shape
    kernel, left, right = constants
    optional = {"sum_a": sum_a, "sum_b": sum_b}
    optional = {name: value for name, value in optional.items() if value is not None}
    blocks = [a, b, *optional.values()]
    waited = [] if then is None else [then]
    has = list(optional) + ["for_b"] * for_b + ["halves"] * halves + ["then"] * len(waited)
    has += ["hand_on"] * hand_on
    rows = ([points - FAR_ROWS, FAR_ROWS] if halves else [points]) + [points] * for_b
    aliases = {3: 0} if in_place else {}
    if hand_on:
        aliases[1] = len(rows)
    anywhere = pl.BlockSpec(memory_space=pl.ANY)
    out = pl.pallas_call(
        functools.partial(pair_body, points, slot, has),
        grid=(2 * X_STEPS + PLANE_STEPS,),
        in_specs=[pl.BlockSpec(memory_space=pltpu.SMEM)]
        + [anywhere] * (len(blocks) + len(waited) + 1)
        + [pl.BlockSpec(table.shape, lambda i: (0, 0)) for table in (left, right)],
        out_specs=[anywhere] * (len(rows) + hand_on),
        out_shape=[
            jax.ShapeDtypeStruct((n, plane), jnp.float32) for n in rows + [points] * hand_on
        ],
        input_output_aliases=aliases,
        scratch_shapes=[
            pltpu.VMEM((points, points, LANES), jnp.float32),
            pltpu.VMEM((len(blocks), points, plane), jnp.float32),
            pltpu.VMEM((points, points, LANES), jnp.float32),
            pltpu.VMEM((2 if for_b else 1, points, plane), jnp.float32),
            pltpu.SemaphoreType.DMA((len(blocks), X_STEPS)),
            pltpu.SemaphoreType.DMA((PLANE_STEPS,)),
            pltpu.SemaphoreType.DMA((len(rows), X_STEPS)),
        ],
        compiler_params=pltpu.CompilerParams(vmem_limit_bytes=62 * 2**20),
        cost_estimate=pl.CostEstimate(
            flops=100_000_000, bytes_accessed=1_000_000, transcendentals=0
        ),
        name="pair_terms",
    )(flags, *blocks, *waited, kernel, left, right)
    return out if len(out) > 1 else out[0]


def copy_body(flags_ref, block_ref, new_block_ref):
    new_block_ref[...] = block_ref[...]


def copied(flags, block):
    points, plane = block.shape
    part = pl.BlockSpec((points, plane // X_STEPS), lambda i: (0, i))
    return pl.pallas_call(
        copy_body,
        grid=(X_STEPS,),
        in_specs=[pl.BlockSpec(memory_space=pltpu.SMEM), part],
        out_specs=part,
        out_shape=jax.ShapeDtypeStruct(block.shape, block.dtype),
        compiler_params=pltpu.CompilerParams(vmem_limit_bytes=62 * 2**20),
        name="copied",
    )(flags, block)


def gate_body(token_ref, left_ref, partner_ref, block_ref, new_left_ref, new_block_ref):
    del token_ref, partner_ref, block_ref, new_block_ref
    new_left_ref[...] = left_ref[...]


def gate(token, left, partner, block):
    in_vmem = pl.BlockSpec(memory_space=pltpu.VMEM)
    anywhere = pl.BlockSpec(memory_space=pl.ANY)
    return pl.pallas_call(
        gate_body,
        in_specs=[in_vmem, in_vmem, anywhere, anywhere],
        out_specs=[in_vmem, anywhere],
        out_shape=[
            jax.ShapeDtypeStruct(left.shape, left.dtype),
            jax.ShapeDtypeStruct(block.shape, block.dtype),
        ],
        input_output_aliases={3: 1},
        compiler_params=pltpu.CompilerParams(vmem_limit_bytes=62 * 2**20),
        name="gate",
    )(token, left, partner, block)


def hold_body(*refs):
    del refs


def hold(block, *then):
    anywhere = pl.BlockSpec(memory_space=pl.ANY)
    return pl.pallas_call(
        hold_body,
        in_specs=[anywhere] * (1 + len(then)),
        out_specs=anywhere,
        out_shape=jax.ShapeDtypeStruct(block.shape, block.dtype),
        input_output_aliases={0: 0},
        compiler_params=pltpu.CompilerParams(vmem_limit_bytes=62 * 2**20),
        name="hold",
    )(block, *then)


def settle_body(flags_ref, home_ref, top_ref, bottom_ref, own_ref, out_ref, near, sems):
    del own_ref
    columns = out_ref.shape[1] // SETTLE_STEPS
    split = top_ref.shape[0]

    def move(parts):
        copies = []
        for i in range(SETTLE_STEPS):
            span = pl.ds(i * columns, columns)
            for j, (source_ref, start) in enumerate(parts):
                rows = pl.ds(start, source_ref.shape[0])
                copies.append((
                    pltpu.make_async_copy(
                        source_ref.at[:, span], near.at[rows, span], sems.at[0, j, i]
                    ),
                    pltpu.make_async_copy(
                        near.at[rows, span], out_ref.at[rows, span], sems.at[1, j, i]
                    ),
                ))
        for inward, outward in copies:
            inward.start()
        for inward, outward in copies:
            inward.wait()
            outward.start()
        for inward, outward in copies:
            outward.wait()

    @pl.when(flags_ref[RESULT] == 1)
    def from_home():
        move([(home_ref, 0)])

    @pl.when(flags_ref[RESULT] == 2)
    def from_far():
        move([(top_ref, 0), (bottom_ref, split)])


def settle(flags, home, top, bottom, own_sum):
    anywhere = pl.BlockSpec(memory_space=pl.ANY)
    return pl.pallas_call(
        settle_body,
        in_specs=[pl.BlockSpec(memory_space=pltpu.SMEM)] + [anywhere] * 4,
        out_specs=anywhere,
        out_shape=jax.ShapeDtypeStruct(own_sum.shape, own_sum.dtype),
        input_output_aliases={4: 0},
        scratch_shapes=[
            pltpu.VMEM(own_sum.shape, own_sum.dtype),
            pltpu.SemaphoreType.DMA((2, 2, SETTLE_STEPS)),
        ],
        compiler_params=pltpu.CompilerParams(vmem_limit_bytes=62 * 2**20),
        name="settle",
    )(flags, home, top, bottom, own_sum)


def both_halves(*pairs):
    return list(pairs) + [(15 - source, 15 - target) for source, target in pairs]


CROSSING = both_halves((3, 14), (4, 9))
PARTNERS = both_halves((8, 14), (15, 9), (9, 11), (14, 12))
ARRIVED = both_halves((14, 2), (9, 5))
SINGLES = both_halves((5, 10), (2, 13))
BESIDE = both_halves((13, 14), (10, 9))
DIRECT = both_halves((15, 10), (8, 13))
TURNED = both_halves((11, 14), (12, 9))
HOME_ACROSS = both_halves((9, 4), (14, 3))
HOME_FAR = both_halves((9, 15), (14, 8))
HOME_TURN = both_halves((9, 11), (14, 12))
HOME_TURNED = both_halves((11, 15), (12, 8))
RESULT = 12
FLAGS = {i: (1, 0, 1, 0, 1, 1, 0, 0, 0, 0, 1, 1, 0) for i in (9, 14, 6, 1)}
FLAGS.update({i: (0, 0, 0, 0, 0, 0, 1, 0, 1, 1, 0, 0, 0) for i in (10, 13, 5, 2)})
FLAGS.update({i: (0,) * RESULT + (1,) for i in (3, 4, 11, 12)})
FLAGS.update({i: (0,) * RESULT + (2,) for i in (15, 8, 0, 7)})


def sixteen_bands(orbitals, constants):
    def send(value, pairs):
        return lax.ppermute(value[None], "band", pairs)[0]

    kernel, left, right = constants
    own = orbitals[0]
    flags = jnp.asarray([FLAGS[i] for i in range(16)], jnp.int32)
    flags = flags[lax.axis_index("band")]
    pair = functools.partial(pair_terms, flags)
    crossed = send(own, CROSSING)
    partner = send(own, PARTNERS)
    own_copy = copied(flags, own)
    token = crossed[:8, :LANES] + kernel[0, :8] + own_copy[:8, :LANES]
    left, held_back = gate(send(token, ARRIVED), left, partner, own_copy)
    constants = (kernel, left, right)
    beside = send(held_back, BESIDE)
    single = send(held_back, SINGLES)
    direct = send(held_back, DIRECT)

    partner_sum, crossed_sum = pair(0, partner, crossed, constants, for_b=True)
    own_sum, crossed_sum = pair(1, own, crossed, constants, sum_b=crossed_sum, for_b=True)
    home = send(crossed_sum, HOME_ACROSS)
    partner = hold(partner, own_sum, beside)
    turned = send(partner, TURNED)
    top, bottom = pair(2, partner, beside, constants, sum_a=partner_sum, halves=True)
    bottom = send(bottom, HOME_TURN)
    top = send(top, HOME_FAR)
    bottom = send(bottom, HOME_TURNED)
    own_sum = pair(3, own, single, constants, sum_a=own_sum, in_place=True)
    own_sum = pair(4, own, direct, constants, sum_a=own_sum, in_place=True, then=home)
    own_sum = pair(5, own, turned, constants, sum_a=own_sum, in_place=True)
    return settle(flags, home, top, bottom, own_sum)[None]


def any_bands(orbitals, constants):
    own = orbitals[0]
    flags = jnp.ones((4,), jnp.int32)
    lower = from_behind(orbitals, "band", OFFSET)[0]
    upper = from_behind(orbitals, "band", -OFFSET)[0]
    total = pair_terms(flags, 0, own, lower, constants)
    return pair_terms(flags, 1, own, upper, constants, sum_a=total)[None]


def local(bands, orbitals):
    points = orbitals.shape[1]
    constants = (screened_kernel(points), *hartley_tables(points))
    if bands == 16:
        return sixteen_bands(orbitals, constants)
    return any_bands(orbitals, constants)


def solution(mesh):
    return jax.shard_map(
        functools.partial(local, mesh.shape["band"]),
        mesh=mesh,
        in_specs=(P(("groups", "band"), None, None),),
        out_specs=P(("groups", "band"), None, None),
        check_vma=False,
    )
```

```python
import functools
import math

import jax
import jax.numpy as jnp
import numpy as np
from jax import lax
from jax.experimental import pallas as pl
from jax.experimental.pallas import tpu as pltpu
from jax.sharding import PartitionSpec as P

OFFSET = 5
screening = 5.44
LANES = 128
X_STEPS = 3
PLANE_STEPS = 2
SETTLE_STEPS = 6
FAR_ROWS = 40


def from_behind(value, axis, by):
    count = lax.axis_size(axis)
    return lax.ppermute(value, axis, [(i, (i + by) % count) for i in range(count)])


def screened_kernel(points):
    signed = jnp.arange(LANES, dtype=jnp.int32)
    inside = signed < points
    signed = jnp.where(signed >= points // 2, signed - points, signed)
    wavenumber = signed.astype(jnp.float32) * (2.0 * math.pi / points)
    squared = (
        wavenumber[:points, None, None] ** 2
        + wavenumber[None, :points, None] ** 2
        + wavenumber[None, None, :] ** 2
    )
    screen_rate = screening / points
    finite = jnp.where(squared > 0.0, squared, 1.0)
    screened = 4.0 * math.pi / finite * -jnp.expm1(-finite / (4.0 * screen_rate * screen_rate))
    kernel = jnp.where(squared > 0.0, screened, math.pi / (screen_rate * screen_rate))
    return jnp.where(inside, kernel / float(points * points * points), 0.0)


def hartley_tables(points):
    counter = np.arange(points)
    angles = 2.0 * np.pi * (counter[:, None] * counter[None, :] % points) / points
    table = np.cos(angles) + np.sin(angles)
    high = table.astype(jnp.bfloat16)
    low = (table - high.astype(np.float64)).astype(jnp.bfloat16)
    left = np.zeros((2 * points, 2 * points), jnp.bfloat16)
    left[:points, :points] = high
    left[:points, points:] = high
    left[points:, :points] = low
    right = np.zeros((2 * LANES, 2 * LANES), jnp.bfloat16)
    right[:points, :points] = high
    right[:points, LANES:LANES + points] = low
    right[LANES:LANES + points, :points] = high
    return jnp.asarray(left), jnp.asarray(right)


def two_terms(value):
    high = value.astype(jnp.bfloat16)
    low = (value - high.astype(jnp.float32)).astype(jnp.bfloat16)
    return high, low


def from_left(left, value):
    half = value.shape[0]
    terms = jnp.concatenate(two_terms(value), 0)
    out = jnp.dot(left, terms, preferred_element_type=jnp.float32)
    return out[:half] + out[half:]


def from_right(value, right):
    out = jnp.dot(jnp.concatenate(two_terms(value), 1), right, preferred_element_type=jnp.float32)
    return out[:, :LANES] + out[:, LANES:]


def pair_body(points, slot, has, *refs):
    refs = list(refs)
    flags_ref = refs.pop(0)
    names = ["a", "b"] + [name for name in ("sum_a", "sum_b") if name in has]
    far = {name: refs.pop(0) for name in names}
    if "then" in has:
        refs.pop(0)
    kernel_ref, left_ref, right_ref = refs.pop(0), refs.pop(0), refs.pop(0)
    out_refs = {"for_a": refs.pop(0)}
    if "halves" in has:
        out_refs["low_a"] = refs.pop(0)
    if "for_b" in has:
        out_refs["for_b"] = refs.pop(0)
    if "hand_on" in has:
        refs.pop(0)
    held, near, near_kernel, near_out, sems, kernel_sems, out_sems = refs
    outs = list(out_refs)
    step = pl.program_id(0)
    active = flags_ref[2 * slot] == 1
    with_sum = flags_ref[2 * slot + 1] == 1
    columns = near.shape[2] // X_STEPS
    ys = columns // points
    per_step = points // PLANE_STEPS
    late = X_STEPS + PLANE_STEPS

    def span_of(chunk):
        start = chunk * columns
        return pl.ds(start if isinstance(chunk, int) else pl.multiple_of(start, columns), columns)

    def fetch(name, chunk):
        place, span = names.index(name), span_of(chunk)
        return pltpu.make_async_copy(
            far[name].at[:, span], near.at[place, :, span], sems.at[place, chunk]
        )

    def fetch_kernel(part):
        span = pl.ds(part * per_step, per_step)
        return pltpu.make_async_copy(
            kernel_ref.at[span], near_kernel.at[span], kernel_sems.at[part]
        )

    def give(name, chunk):
        span = span_of(chunk)
        source = near_out.at[0 if name != "for_b" else 1]
        if "halves" in has and name != "for_b":
            rows = pl.ds(points - FAR_ROWS, FAR_ROWS) if name == "low_a" else pl.ds(0, points - FAR_ROWS)
            source = source.at[rows, span]
        else:
            source = source.at[:, span]
        return pltpu.make_async_copy(
            source, out_refs[name].at[:, span], out_sems.at[outs.index(name), chunk]
        )

    def here(name, chunk):
        return near[names.index(name), :, span_of(chunk)]

    sums = [name for name in names if name.startswith("sum")]

    @pl.when(active & (step == 0))
    def start_first():
        for chunk in range(2):
            for name in ("a", "b"):
                fetch(name, chunk).start()

    @pl.when(active & (step + 2 < X_STEPS))
    def start_next():
        for name in ("a", "b"):
            fetch(name, step + 2).start()

    @pl.when(active & (step == X_STEPS - 2))
    def start_kernel():
        for part in range(PLANE_STEPS):
            fetch_kernel(part).start()

    if sums:
        @pl.when(active & (step == X_STEPS))
        def start_sums():
            for chunk in range(X_STEPS):
                for name in sums:
                    fetch(name, chunk).start()

    def lanes_apart(block):
        gap = jnp.zeros((points, LANES - points), jnp.float32)
        rows = [
            jnp.concatenate([block[:, q * points:(q + 1) * points], gap], 1) for q in range(ys)
        ]
        return jnp.swapaxes(jnp.stack(rows, 0), 0, 1)

    def lanes_together(block):
        block = jnp.swapaxes(block, 0, 1)
        return jnp.concatenate([block[q][:, :points] for q in range(ys)], 1)

    def side_by_side(block):
        return jnp.concatenate([block[i] for i in range(per_step)], 1)

    @pl.when(active & (step < X_STEPS))
    def forward_x():
        for name in ("a", "b"):
            fetch(name, step).wait()
        spectrum = from_left(left_ref[...], here("a", step) * here("b", step))
        start = pl.multiple_of(step * ys, ys)
        held[:, pl.ds(start, ys), :] = lanes_apart(spectrum)

    @pl.when(active & (step >= X_STEPS) & (step < late))
    def planes():
        left = left_ref[...]
        right = right_ref[...]
        part = step - X_STEPS
        first = part * per_step
        block = held[pl.ds(first, per_step)].reshape(per_step * points, LANES)
        block = from_right(block, right).reshape(per_step, points, LANES)
        wide = from_left(left, side_by_side(block))
        fetch_kernel(part).wait()
        wide = from_left(left, wide * side_by_side(near_kernel[pl.ds(first, per_step)]))
        block = jnp.concatenate(
            [wide[:, i * LANES:(i + 1) * LANES] for i in range(per_step)], 0
        )
        block = from_right(block, right)
        held[pl.ds(first, per_step)] = block.reshape(per_step, points, LANES)

    @pl.when(active & (step >= late))
    def inverse_x():
        chunk = step - late
        start = pl.multiple_of(chunk * ys, ys)
        for name in sums:
            fetch(name, chunk).wait()
        block = lanes_together(held[:, pl.ds(start, ys), :])
        potential = from_left(left_ref[...], block)
        for_a = -(here("b", chunk) * potential)
        if "sum_a" in has:
            for_a = for_a + jnp.where(with_sum, here("sum_a", chunk), 0.0)
        near_out[0, :, span_of(chunk)] = for_a
        if "for_b" in has:
            for_b = -(here("a", chunk) * potential)
            if "sum_b" in has:
                for_b = for_b + here("sum_b", chunk)
            near_out[1, :, span_of(chunk)] = for_b
        for name in outs:
            give(name, chunk).start()

    @pl.when(active & (step == late + X_STEPS - 1))
    def wait_outs():
        for chunk in range(X_STEPS):
            for name in outs:
                give(name, chunk).wait()


def pair_terms(
    flags, slot, a, b, constants, sum_a=None, sum_b=None, for_b=False, halves=False, in_place=False, then=None, hand_on=False
):
    points, plane = a.shape
    kernel, left, right = constants
    optional = {"sum_a": sum_a, "sum_b": sum_b}
    optional = {name: value for name, value in optional.items() if value is not None}
    blocks = [a, b, *optional.values()]
    waited = [] if then is None else [then]
    has = list(optional) + ["for_b"] * for_b + ["halves"] * halves + ["then"] * len(waited)
    has += ["hand_on"] * hand_on
    rows = ([points - FAR_ROWS, FAR_ROWS] if halves else [points]) + [points] * for_b
    aliases = {3: 0} if in_place else {}
    if hand_on:
        aliases[1] = len(rows)
    anywhere = pl.BlockSpec(memory_space=pl.ANY)
    out = pl.pallas_call(
        functools.partial(pair_body, points, slot, has),
        grid=(2 * X_STEPS + PLANE_STEPS,),
        in_specs=[pl.BlockSpec(memory_space=pltpu.SMEM)]
        + [anywhere] * (len(blocks) + len(waited) + 1)
        + [pl.BlockSpec(table.shape, lambda i: (0, 0)) for table in (left, right)],
        out_specs=[anywhere] * (len(rows) + hand_on),
        out_shape=[
            jax.ShapeDtypeStruct((n, plane), jnp.float32) for n in rows + [points] * hand_on
        ],
        input_output_aliases=aliases,
        scratch_shapes=[
            pltpu.VMEM((points, points, LANES), jnp.float32),
            pltpu.VMEM((len(blocks), points, plane), jnp.float32),
            pltpu.VMEM((points, points, LANES), jnp.float32),
            pltpu.VMEM((2 if for_b else 1, points, plane), jnp.float32),
            pltpu.SemaphoreType.DMA((len(blocks), X_STEPS)),
            pltpu.SemaphoreType.DMA((PLANE_STEPS,)),
            pltpu.SemaphoreType.DMA((len(rows), X_STEPS)),
        ],
        compiler_params=pltpu.CompilerParams(vmem_limit_bytes=62 * 2**20),
        cost_estimate=pl.CostEstimate(
            flops=100_000_000, bytes_accessed=1_000_000, transcendentals=0
        ),
        name="pair_terms",
    )(flags, *blocks, *waited, kernel, left, right)
    return out if len(out) > 1 else out[0]


def copy_body(flags_ref, block_ref, first_ref, second_ref):
    del flags_ref
    first_ref[...] = block_ref[...]
    second_ref[...] = block_ref[...]


def copied(flags, block):
    points, plane = block.shape
    part = pl.BlockSpec((points, plane // X_STEPS), lambda i: (0, i))
    return pl.pallas_call(
        copy_body,
        grid=(X_STEPS,),
        in_specs=[pl.BlockSpec(memory_space=pltpu.SMEM), part],
        out_specs=[part, part],
        out_shape=[jax.ShapeDtypeStruct(block.shape, block.dtype)] * 2,
        compiler_params=pltpu.CompilerParams(vmem_limit_bytes=62 * 2**20),
        name="copied",
    )(flags, block)


def gate_body(token_ref, left_ref, partner_ref, block_ref, new_left_ref, new_block_ref):
    del token_ref, partner_ref, block_ref, new_block_ref
    new_left_ref[...] = left_ref[...]


def gate(token, left, partner, block):
    in_vmem = pl.BlockSpec(memory_space=pltpu.VMEM)
    anywhere = pl.BlockSpec(memory_space=pl.ANY)
    return pl.pallas_call(
        gate_body,
        in_specs=[in_vmem, in_vmem, anywhere, anywhere],
        out_specs=[in_vmem, anywhere],
        out_shape=[
            jax.ShapeDtypeStruct(left.shape, left.dtype),
            jax.ShapeDtypeStruct(block.shape, block.dtype),
        ],
        input_output_aliases={3: 1},
        compiler_params=pltpu.CompilerParams(vmem_limit_bytes=62 * 2**20),
        name="gate",
    )(token, left, partner, block)


def hold_body(*refs):
    del refs


def hold(block, *then):
    anywhere = pl.BlockSpec(memory_space=pl.ANY)
    return pl.pallas_call(
        hold_body,
        in_specs=[anywhere] * (1 + len(then)),
        out_specs=anywhere,
        out_shape=jax.ShapeDtypeStruct(block.shape, block.dtype),
        input_output_aliases={0: 0},
        compiler_params=pltpu.CompilerParams(vmem_limit_bytes=62 * 2**20),
        name="hold",
    )(block, *then)


def settle_body(flags_ref, home_ref, top_ref, bottom_ref, own_ref, out_ref, near, sems):
    del own_ref
    columns = out_ref.shape[1] // SETTLE_STEPS
    split = top_ref.shape[0]

    def move(parts):
        copies = []
        for i in range(SETTLE_STEPS):
            span = pl.ds(i * columns, columns)
            for j, (source_ref, start) in enumerate(parts):
                rows = pl.ds(start, source_ref.shape[0])
                copies.append((
                    pltpu.make_async_copy(
                        source_ref.at[:, span], near.at[rows, span], sems.at[0, j, i]
                    ),
                    pltpu.make_async_copy(
                        near.at[rows, span], out_ref.at[rows, span], sems.at[1, j, i]
                    ),
                ))
        for inward, outward in copies:
            inward.start()
        for inward, outward in copies:
            inward.wait()
            outward.start()
        for inward, outward in copies:
            outward.wait()

    @pl.when(flags_ref[RESULT] == 1)
    def from_home():
        move([(home_ref, 0)])

    @pl.when(flags_ref[RESULT] == 2)
    def from_far():
        move([(top_ref, 0), (bottom_ref, split)])


def settle(flags, home, top, bottom, own_sum):
    anywhere = pl.BlockSpec(memory_space=pl.ANY)
    return pl.pallas_call(
        settle_body,
        in_specs=[pl.BlockSpec(memory_space=pltpu.SMEM)] + [anywhere] * 4,
        out_specs=anywhere,
        out_shape=jax.ShapeDtypeStruct(own_sum.shape, own_sum.dtype),
        input_output_aliases={4: 0},
        scratch_shapes=[
            pltpu.VMEM(own_sum.shape, own_sum.dtype),
            pltpu.SemaphoreType.DMA((2, 2, SETTLE_STEPS)),
        ],
        compiler_params=pltpu.CompilerParams(vmem_limit_bytes=62 * 2**20),
        name="settle",
    )(flags, home, top, bottom, own_sum)


def both_halves(*pairs):
    return list(pairs) + [(15 - source, 15 - target) for source, target in pairs]


CROSSING = both_halves((3, 14), (4, 9))
PARTNERS = both_halves((8, 14), (15, 9), (9, 11), (14, 12))
ARRIVED = both_halves((14, 2), (9, 5))
SINGLES = both_halves((5, 10), (2, 13))
BESIDE = both_halves((13, 14), (10, 9))
DIRECT = both_halves((15, 10), (8, 13))
TURNED = both_halves((11, 14), (12, 9))
HOME_ACROSS = both_halves((9, 4), (14, 3))
HOME_FAR = both_halves((9, 15), (14, 8))
HOME_TURN = both_halves((9, 11), (14, 12))
HOME_TURNED = both_halves((11, 15), (12, 8))
RESULT = 12
FLAGS = {i: (1, 0, 1, 0, 1, 1, 0, 0, 0, 0, 1, 1, 0) for i in (9, 14, 6, 1)}
FLAGS.update({i: (0, 0, 0, 0, 0, 0, 1, 0, 1, 1, 0, 0, 0) for i in (10, 13, 5, 2)})
FLAGS.update({i: (0,) * RESULT + (1,) for i in (3, 4, 11, 12)})
FLAGS.update({i: (0,) * RESULT + (2,) for i in (15, 8, 0, 7)})


def sixteen_bands(orbitals, constants):
    def send(value, pairs):
        return lax.ppermute(value[None], "band", pairs)[0]

    kernel, left, right = constants
    own = orbitals[0]
    flags = jnp.asarray([FLAGS[i] for i in range(16)], jnp.int32)
    flags = flags[lax.axis_index("band")]
    pair = functools.partial(pair_terms, flags)
    crossed = send(own, CROSSING)
    partner = send(own, PARTNERS)
    own_copy, direct_copy = copied(flags, own)
    token = crossed[:8, :LANES] + kernel[0, :8] + own_copy[:8, :LANES]
    direct_copy = hold(direct_copy, partner)
    direct = send(direct_copy, DIRECT)
    left, held_back = gate(send(token, ARRIVED), left, direct_copy, own_copy)
    constants = (kernel, left, right)
    beside = send(held_back, BESIDE)
    single = send(held_back, SINGLES)

    partner_sum, crossed_sum = pair(0, partner, crossed, constants, for_b=True)
    own_sum, crossed_sum = pair(1, own, crossed, constants, sum_b=crossed_sum, for_b=True, then=direct)
    home = send(crossed_sum, HOME_ACROSS)
    partner = hold(partner, own_sum, beside)
    turned = send(partner, TURNED)
    top, bottom = pair(2, partner, beside, constants, sum_a=partner_sum, halves=True)
    bottom = send(bottom, HOME_TURN)
    top = send(top, HOME_FAR)
    bottom = send(bottom, HOME_TURNED)
    own_sum = pair(3, own, direct, constants, sum_a=own_sum, in_place=True)
    own_sum = pair(4, own, single, constants, sum_a=own_sum, in_place=True, then=home)
    own_sum = pair(5, own, turned, constants, sum_a=own_sum, in_place=True)
    return settle(flags, home, top, bottom, own_sum)[None]


def any_bands(orbitals, constants):
    own = orbitals[0]
    flags = jnp.ones((4,), jnp.int32)
    lower = from_behind(orbitals, "band", OFFSET)[0]
    upper = from_behind(orbitals, "band", -OFFSET)[0]
    total = pair_terms(flags, 0, own, lower, constants)
    return pair_terms(flags, 1, own, upper, constants, sum_a=total)[None]


def local(bands, orbitals):
    points = orbitals.shape[1]
    constants = (screened_kernel(points), *hartley_tables(points))
    if bands == 16:
        return sixteen_bands(orbitals, constants)
    return any_bands(orbitals, constants)


def solution(mesh):
    return jax.shard_map(
        functools.partial(local, mesh.shape["band"]),
        mesh=mesh,
        in_specs=(P(("groups", "band"), None, None),),
        out_specs=P(("groups", "band"), None, None),
        check_vma=False,
    )
```

```python
import functools
import math

import jax
import jax.numpy as jnp
import numpy as np
from jax import lax
from jax.experimental import pallas as pl
from jax.experimental.pallas import tpu as pltpu
from jax.sharding import PartitionSpec as P

OFFSET = 5
screening = 5.44
LANES = 128
X_STEPS = 3
PLANE_STEPS = 2
SETTLE_STEPS = 6
FAR_ROWS = 40


def from_behind(value, axis, by):
    count = lax.axis_size(axis)
    return lax.ppermute(value, axis, [(i, (i + by) % count) for i in range(count)])


def screened_kernel(points):
    signed = jnp.arange(LANES, dtype=jnp.int32)
    inside = signed < points
    signed = jnp.where(signed >= points // 2, signed - points, signed)
    wavenumber = signed.astype(jnp.float32) * (2.0 * math.pi / points)
    squared = (
        wavenumber[:points, None, None] ** 2
        + wavenumber[None, :points, None] ** 2
        + wavenumber[None, None, :] ** 2
    )
    screen_rate = screening / points
    finite = jnp.where(squared > 0.0, squared, 1.0)
    screened = 4.0 * math.pi / finite * -jnp.expm1(-finite / (4.0 * screen_rate * screen_rate))
    kernel = jnp.where(squared > 0.0, screened, math.pi / (screen_rate * screen_rate))
    return jnp.where(inside, kernel / -float(points * points * points), 0.0)


def hartley_tables(points):
    counter = np.arange(points)
    angles = 2.0 * np.pi * (counter[:, None] * counter[None, :] % points) / points
    table = np.cos(angles) + np.sin(angles)
    high = table.astype(jnp.bfloat16)
    low = (table - high.astype(np.float64)).astype(jnp.bfloat16)
    left = np.zeros((2 * points, 2 * points), jnp.bfloat16)
    left[:points, :points] = high
    left[:points, points:] = high
    left[points:, :points] = low
    right = np.zeros((2 * LANES, 2 * LANES), jnp.bfloat16)
    right[:points, :points] = high
    right[:points, LANES:LANES + points] = low
    right[LANES:LANES + points, :points] = high
    return jnp.asarray(left), jnp.asarray(right)


def two_terms(value):
    high = value.astype(jnp.bfloat16)
    low = (value - high.astype(jnp.float32)).astype(jnp.bfloat16)
    return high, low


def from_left(left, value):
    half = value.shape[0]
    terms = jnp.concatenate(two_terms(value), 0)
    out = jnp.dot(left, terms, preferred_element_type=jnp.float32)
    return out[:half] + out[half:]


def from_right(value, right):
    out = jnp.dot(jnp.concatenate(two_terms(value), 1), right, preferred_element_type=jnp.float32)
    return out[:, :LANES] + out[:, LANES:]


def pair_body(points, slot, has, *refs):
    refs = list(refs)
    flags_ref = refs.pop(0)
    names = ["a", "b"] + [name for name in ("sum_a", "sum_b") if name in has]
    far = {name: refs.pop(0) for name in names}
    if "then" in has:
        refs.pop(0)
    kernel_ref, left_ref, right_ref = refs.pop(0), refs.pop(0), refs.pop(0)
    out_refs = {"for_a": refs.pop(0)}
    if "halves" in has:
        out_refs["low_a"] = refs.pop(0)
    if "for_b" in has:
        out_refs["for_b"] = refs.pop(0)
    if "hand_on" in has:
        refs.pop(0)
    held, near, near_kernel, near_out, sems, kernel_sems, out_sems = refs
    outs = list(out_refs)
    step = pl.program_id(0)
    active = flags_ref[2 * slot] == 1
    with_sum = flags_ref[2 * slot + 1] == 1
    columns = near.shape[2] // X_STEPS
    ys = columns // points
    per_step = points // PLANE_STEPS
    late = X_STEPS + PLANE_STEPS

    def span_of(chunk):
        start = chunk * columns
        return pl.ds(start if isinstance(chunk, int) else pl.multiple_of(start, columns), columns)

    def fetch(name, chunk):
        place, span = names.index(name), span_of(chunk)
        return pltpu.make_async_copy(
            far[name].at[:, span], near.at[place, :, span], sems.at[place, chunk]
        )

    def fetch_kernel(part):
        span = pl.ds(part * per_step, per_step)
        return pltpu.make_async_copy(
            kernel_ref.at[span], near_kernel.at[span], kernel_sems.at[part]
        )

    def give(name, chunk):
        span = span_of(chunk)
        source = near_out.at[0 if name != "for_b" else 1]
        if "halves" in has and name != "for_b":
            rows = pl.ds(points - FAR_ROWS, FAR_ROWS) if name == "low_a" else pl.ds(0, points - FAR_ROWS)
            source = source.at[rows, span]
        else:
            source = source.at[:, span]
        return pltpu.make_async_copy(
            source, out_refs[name].at[:, span], out_sems.at[outs.index(name), chunk]
        )

    def here(name, chunk):
        return near[names.index(name), :, span_of(chunk)]

    sums = [name for name in names if name.startswith("sum")]

    @pl.when(active & (step == 0))
    def start_first():
        for chunk in range(2):
            for name in ("a", "b"):
                fetch(name, chunk).start()

    @pl.when(active & (step + 2 < X_STEPS))
    def start_next():
        for name in ("a", "b"):
            fetch(name, step + 2).start()

    @pl.when(active & (step == X_STEPS - 2))
    def start_kernel():
        for part in range(PLANE_STEPS):
            fetch_kernel(part).start()

    if sums:
        @pl.when(active & (step == X_STEPS))
        def start_sums():
            for chunk in range(X_STEPS):
                for name in sums:
                    fetch(name, chunk).start()

    def lanes_apart(block):
        tail = jnp.zeros((points, LANES), jnp.float32)
        wide = jnp.concatenate([block, tail], 1)
        rows = [wide[:, q * points:q * points + LANES] for q in range(ys)]
        return jnp.swapaxes(jnp.stack(rows, 0), 0, 1)

    def lanes_together(block):
        block = jnp.swapaxes(block, 0, 1)
        return jnp.concatenate([block[q][:, :points] for q in range(ys)], 1)

    def side_by_side(block):
        return jnp.concatenate([block[i] for i in range(per_step)], 1)

    @pl.when(active & (step < X_STEPS))
    def forward_x():
        for name in ("a", "b"):
            fetch(name, step).wait()
        spectrum = from_left(left_ref[...], here("a", step) * here("b", step))
        start = pl.multiple_of(step * ys, ys)
        held[:, pl.ds(start, ys), :] = lanes_apart(spectrum)

    @pl.when(active & (step >= X_STEPS) & (step < late))
    def planes():
        left = left_ref[...]
        right = right_ref[...]
        part = step - X_STEPS
        first = part * per_step
        block = held[pl.ds(first, per_step)].reshape(per_step * points, LANES)
        block = from_right(block, right).reshape(per_step, points, LANES)
        wide = from_left(left, side_by_side(block))
        fetch_kernel(part).wait()
        wide = from_left(left, wide * side_by_side(near_kernel[pl.ds(first, per_step)]))
        block = jnp.concatenate(
            [wide[:, i * LANES:(i + 1) * LANES] for i in range(per_step)], 0
        )
        block = from_right(block, right)
        held[pl.ds(first, per_step)] = block.reshape(per_step, points, LANES)

    @pl.when(active & (step >= late))
    def inverse_x():
        chunk = step - late
        start = pl.multiple_of(chunk * ys, ys)
        for name in sums:
            fetch(name, chunk).wait()
        block = lanes_together(held[:, pl.ds(start, ys), :])
        potential = from_left(left_ref[...], block)
        for_a = here("b", chunk) * potential
        if "sum_a" in has:
            for_a = for_a + jnp.where(with_sum, here("sum_a", chunk), 0.0)
        near_out[0, :, span_of(chunk)] = for_a
        if "for_b" in has:
            for_b = here("a", chunk) * potential
            if "sum_b" in has:
                for_b = for_b + here("sum_b", chunk)
            near_out[1, :, span_of(chunk)] = for_b
        for name in outs:
            give(name, chunk).start()

    @pl.when(active & (step == late + X_STEPS - 1))
    def wait_outs():
        for chunk in range(X_STEPS):
            for name in outs:
                give(name, chunk).wait()


def pair_terms(
    flags, slot, a, b, constants, sum_a=None, sum_b=None, for_b=False, halves=False, in_place=False, then=None, hand_on=False
):
    points, plane = a.shape
    kernel, left, right = constants
    optional = {"sum_a": sum_a, "sum_b": sum_b}
    optional = {name: value for name, value in optional.items() if value is not None}
    blocks = [a, b, *optional.values()]
    waited = [] if then is None else [then]
    has = list(optional) + ["for_b"] * for_b + ["halves"] * halves + ["then"] * len(waited)
    has += ["hand_on"] * hand_on
    rows = ([points - FAR_ROWS, FAR_ROWS] if halves else [points]) + [points] * for_b
    aliases = {3: 0} if in_place else {}
    if hand_on:
        aliases[1] = len(rows)
    anywhere = pl.BlockSpec(memory_space=pl.ANY)
    out = pl.pallas_call(
        functools.partial(pair_body, points, slot, has),
        grid=(2 * X_STEPS + PLANE_STEPS,),
        in_specs=[pl.BlockSpec(memory_space=pltpu.SMEM)]
        + [anywhere] * (len(blocks) + len(waited) + 1)
        + [pl.BlockSpec(table.shape, lambda i: (0, 0)) for table in (left, right)],
        out_specs=[anywhere] * (len(rows) + hand_on),
        out_shape=[
            jax.ShapeDtypeStruct((n, plane), jnp.float32) for n in rows + [points] * hand_on
        ],
        input_output_aliases=aliases,
        scratch_shapes=[
            pltpu.VMEM((points, points, LANES), jnp.float32),
            pltpu.VMEM((len(blocks), points, plane), jnp.float32),
            pltpu.VMEM((points, points, LANES), jnp.float32),
            pltpu.VMEM((2 if for_b else 1, points, plane), jnp.float32),
            pltpu.SemaphoreType.DMA((len(blocks), X_STEPS)),
            pltpu.SemaphoreType.DMA((PLANE_STEPS,)),
            pltpu.SemaphoreType.DMA((len(rows), X_STEPS)),
        ],
        compiler_params=pltpu.CompilerParams(vmem_limit_bytes=63 * 2**20),
        cost_estimate=pl.CostEstimate(
            flops=100_000_000, bytes_accessed=1_000_000, transcendentals=0
        ),
        name="pair_terms",
    )(flags, *blocks, *waited, kernel, left, right)
    return out if len(out) > 1 else out[0]


def copy_body(flags_ref, block_ref, first_ref, second_ref):
    del flags_ref
    first_ref[...] = block_ref[...]
    second_ref[...] = block_ref[...]


def copied(flags, block):
    points, plane = block.shape
    part = pl.BlockSpec((points, plane // X_STEPS), lambda i: (0, i))
    return pl.pallas_call(
        copy_body,
        grid=(X_STEPS,),
        in_specs=[pl.BlockSpec(memory_space=pltpu.SMEM), part],
        out_specs=[part, part],
        out_shape=[jax.ShapeDtypeStruct(block.shape, block.dtype)] * 2,
        compiler_params=pltpu.CompilerParams(vmem_limit_bytes=63 * 2**20),
        name="copied",
    )(flags, block)


def gate_body(token_ref, left_ref, partner_ref, block_ref, new_left_ref, new_block_ref):
    del token_ref, partner_ref, block_ref, new_block_ref
    new_left_ref[...] = left_ref[...]


def gate(token, left, partner, block):
    in_vmem = pl.BlockSpec(memory_space=pltpu.VMEM)
    anywhere = pl.BlockSpec(memory_space=pl.ANY)
    return pl.pallas_call(
        gate_body,
        in_specs=[in_vmem, in_vmem, anywhere, anywhere],
        out_specs=[in_vmem, anywhere],
        out_shape=[
            jax.ShapeDtypeStruct(left.shape, left.dtype),
            jax.ShapeDtypeStruct(block.shape, block.dtype),
        ],
        input_output_aliases={3: 1},
        compiler_params=pltpu.CompilerParams(vmem_limit_bytes=63 * 2**20),
        name="gate",
    )(token, left, partner, block)


def hold_body(*refs):
    del refs


def hold(block, *then):
    anywhere = pl.BlockSpec(memory_space=pl.ANY)
    return pl.pallas_call(
        hold_body,
        in_specs=[anywhere] * (1 + len(then)),
        out_specs=anywhere,
        out_shape=jax.ShapeDtypeStruct(block.shape, block.dtype),
        input_output_aliases={0: 0},
        compiler_params=pltpu.CompilerParams(vmem_limit_bytes=63 * 2**20),
        name="hold",
    )(block, *then)


def settle_body(flags_ref, home_ref, top_ref, bottom_ref, own_ref, out_ref, near, sems):
    del own_ref
    columns = out_ref.shape[1] // SETTLE_STEPS
    split = top_ref.shape[0]

    def move(parts):
        copies = []
        for i in range(SETTLE_STEPS):
            span = pl.ds(i * columns, columns)
            for j, (source_ref, start) in enumerate(parts):
                rows = pl.ds(start, source_ref.shape[0])
                copies.append((
                    pltpu.make_async_copy(
                        source_ref.at[:, span], near.at[rows, span], sems.at[0, j, i]
                    ),
                    pltpu.make_async_copy(
                        near.at[rows, span], out_ref.at[rows, span], sems.at[1, j, i]
                    ),
                ))
        for inward, outward in copies:
            inward.start()
        for inward, outward in copies:
            inward.wait()
            outward.start()
        for inward, outward in copies:
            outward.wait()

    @pl.when(flags_ref[RESULT] == 1)
    def from_home():
        move([(home_ref, 0)])

    @pl.when(flags_ref[RESULT] == 2)
    def from_far():
        move([(top_ref, 0), (bottom_ref, split)])


def settle(flags, home, top, bottom, own_sum):
    anywhere = pl.BlockSpec(memory_space=pl.ANY)
    return pl.pallas_call(
        settle_body,
        in_specs=[pl.BlockSpec(memory_space=pltpu.SMEM)] + [anywhere] * 4,
        out_specs=anywhere,
        out_shape=jax.ShapeDtypeStruct(own_sum.shape, own_sum.dtype),
        input_output_aliases={4: 0},
        scratch_shapes=[
            pltpu.VMEM(own_sum.shape, own_sum.dtype),
            pltpu.SemaphoreType.DMA((2, 2, SETTLE_STEPS)),
        ],
        compiler_params=pltpu.CompilerParams(vmem_limit_bytes=63 * 2**20),
        name="settle",
    )(flags, home, top, bottom, own_sum)


def both_halves(*pairs):
    return list(pairs) + [(15 - source, 15 - target) for source, target in pairs]


CROSSING = both_halves((3, 14), (4, 9))
PARTNERS = both_halves((8, 14), (15, 9), (9, 11), (14, 12))
ARRIVED = both_halves((14, 2), (9, 5))
SINGLES = both_halves((5, 10), (2, 13))
BESIDE = both_halves((13, 14), (10, 9))
DIRECT = both_halves((15, 10), (8, 13))
TURNED = both_halves((11, 14), (12, 9))
HOME_ACROSS = both_halves((9, 4), (14, 3))
HOME_FAR = both_halves((9, 15), (14, 8))
HOME_TURN = both_halves((9, 11), (14, 12))
HOME_TURNED = both_halves((11, 15), (12, 8))
RESULT = 12
FLAGS = {i: (1, 0, 1, 0, 1, 1, 0, 0, 0, 0, 1, 1, 0) for i in (9, 14, 6, 1)}
FLAGS.update({i: (0, 0, 0, 0, 0, 0, 1, 0, 1, 1, 0, 0, 0) for i in (10, 13, 5, 2)})
FLAGS.update({i: (0,) * RESULT + (1,) for i in (3, 4, 11, 12)})
FLAGS.update({i: (0,) * RESULT + (2,) for i in (15, 8, 0, 7)})


def sixteen_bands(orbitals, constants):
    def send(value, pairs):
        return lax.ppermute(value[None], "band", pairs)[0]

    kernel, left, right = constants
    own = orbitals[0]
    flags = jnp.asarray([FLAGS[i] for i in range(16)], jnp.int32)
    flags = flags[lax.axis_index("band")]
    pair = functools.partial(pair_terms, flags)
    crossed = send(own, CROSSING)
    partner = send(own, PARTNERS)
    own_copy, direct_copy = copied(flags, own)
    token = crossed[:8, :LANES] + kernel[0, :8] + own_copy[:8, :LANES]
    direct_copy = hold(direct_copy, partner)
    direct = send(direct_copy, DIRECT)
    left, held_back = gate(send(token, ARRIVED), left, direct_copy, own_copy)
    constants = (kernel, left, right)
    beside = send(held_back, BESIDE)
    single = send(held_back, SINGLES)

    partner_sum, crossed_sum = pair(0, partner, crossed, constants, for_b=True)
    own_sum, crossed_sum = pair(1, own, crossed, constants, sum_b=crossed_sum, for_b=True, then=direct)
    home = send(crossed_sum, HOME_ACROSS)
    partner = hold(partner, own_sum)
    turned = send(partner, TURNED)
    top, bottom = pair(2, partner, beside, constants, sum_a=partner_sum, halves=True)
    bottom = send(bottom, HOME_TURN)
    top = send(top, HOME_FAR)
    bottom = send(bottom, HOME_TURNED)
    own_sum = pair(3, own, direct, constants, sum_a=own_sum, in_place=True)
    own_sum = pair(4, own, single, constants, sum_a=own_sum, in_place=True, then=home)
    own_sum = pair(5, own, turned, constants, sum_a=own_sum, in_place=True)
    return settle(flags, home, top, bottom, own_sum)[None]


def any_bands(orbitals, constants):
    own = orbitals[0]
    flags = jnp.ones((4,), jnp.int32)
    lower = from_behind(orbitals, "band", OFFSET)[0]
    upper = from_behind(orbitals, "band", -OFFSET)[0]
    total = pair_terms(flags, 0, own, lower, constants)
    return pair_terms(flags, 1, own, upper, constants, sum_a=total)[None]


def local(bands, orbitals):
    points = orbitals.shape[1]
    constants = (screened_kernel(points), *hartley_tables(points))
    if bands == 16:
        return sixteen_bands(orbitals, constants)
    return any_bands(orbitals, constants)


def solution(mesh):
    return jax.shard_map(
        functools.partial(local, mesh.shape["band"]),
        mesh=mesh,
        in_specs=(P(("groups", "band"), None, None),),
        out_specs=P(("groups", "band"), None, None),
        check_vma=False,
    )
```

```python
import functools
import math

import jax
import jax.numpy as jnp
import numpy as np
from jax import lax
from jax.experimental import pallas as pl
from jax.experimental.pallas import tpu as pltpu
from jax.sharding import PartitionSpec as P

OFFSET = 5
screening = 5.44
LANES = 128
X_STEPS = 3
PLANE_STEPS = 2
SETTLE_STEPS = 6
FAR_ROWS = 40


def from_behind(value, axis, by):
    count = lax.axis_size(axis)
    return lax.ppermute(value, axis, [(i, (i + by) % count) for i in range(count)])


def screened_kernel(points):
    signed = jnp.arange(LANES, dtype=jnp.int32)
    inside = signed < points
    signed = jnp.where(signed >= points // 2, signed - points, signed)
    wavenumber = signed.astype(jnp.float32) * (2.0 * math.pi / points)
    squared = (
        wavenumber[:points, None, None] ** 2
        + wavenumber[None, :points, None] ** 2
        + wavenumber[None, None, :] ** 2
    )
    screen_rate = screening / points
    finite = jnp.where(squared > 0.0, squared, 1.0)
    screened = 4.0 * math.pi / finite * -jnp.expm1(-finite / (4.0 * screen_rate * screen_rate))
    kernel = jnp.where(squared > 0.0, screened, math.pi / (screen_rate * screen_rate))
    return jnp.where(inside, kernel / -float(points * points * points), 0.0)


def hartley_tables(points):
    counter = np.arange(points)
    angles = 2.0 * np.pi * (counter[:, None] * counter[None, :] % points) / points
    table = np.cos(angles) + np.sin(angles)
    high = table.astype(jnp.bfloat16)
    low = (table - high.astype(np.float64)).astype(jnp.bfloat16)
    left = np.zeros((2 * points, 2 * points), jnp.bfloat16)
    left[:points, :points] = high
    left[:points, points:] = high
    left[points:, :points] = low
    right = np.zeros((2 * LANES, 2 * LANES), jnp.bfloat16)
    right[:points, :points] = high
    right[:points, LANES:LANES + points] = low
    right[LANES:LANES + points, :points] = high
    return jnp.asarray(left), jnp.asarray(right)


def two_terms(value):
    high = value.astype(jnp.bfloat16)
    low = (value - high.astype(jnp.float32)).astype(jnp.bfloat16)
    return high, low


def from_left(left, value):
    half = value.shape[0]
    terms = jnp.concatenate(two_terms(value), 0)
    out = jnp.dot(left, terms, preferred_element_type=jnp.float32)
    return out[:half] + out[half:]


def from_right(value, right):
    out = jnp.dot(jnp.concatenate(two_terms(value), 1), right, preferred_element_type=jnp.float32)
    return out[:, :LANES] + out[:, LANES:]


def pair_body(points, slot, has, *refs):
    refs = list(refs)
    flags_ref = refs.pop(0)
    names = ["a", "b"] + [name for name in ("sum_a", "sum_b") if name in has]
    far = {name: refs.pop(0) for name in names}
    if "then" in has:
        refs.pop(0)
    kernel_ref, left_ref, right_ref = refs.pop(0), refs.pop(0), refs.pop(0)
    out_refs = {"for_a": refs.pop(0)}
    if "halves" in has:
        out_refs["low_a"] = refs.pop(0)
    if "for_b" in has:
        out_refs["for_b"] = refs.pop(0)
    if "hand_on" in has:
        refs.pop(0)
    held, near, near_kernel, near_out, sems, kernel_sems, out_sems = refs
    outs = list(out_refs)
    step = pl.program_id(0)
    active = flags_ref[2 * slot] == 1
    with_sum = flags_ref[2 * slot + 1] == 1
    columns = near.shape[2] // X_STEPS
    ys = columns // points
    per_step = points // PLANE_STEPS
    late = X_STEPS + PLANE_STEPS

    def span_of(chunk):
        start = chunk * columns
        return pl.ds(start if isinstance(chunk, int) else pl.multiple_of(start, columns), columns)

    def fetch(name, chunk):
        place, span = names.index(name), span_of(chunk)
        return pltpu.make_async_copy(
            far[name].at[:, span], near.at[place, :, span], sems.at[place, chunk]
        )

    def fetch_kernel(part):
        span = pl.ds(part * per_step, per_step)
        return pltpu.make_async_copy(
            kernel_ref.at[span], near_kernel.at[span], kernel_sems.at[part]
        )

    def give(name, chunk):
        span = span_of(chunk)
        source = near_out.at[0 if name != "for_b" else 1]
        if "halves" in has and name != "for_b":
            rows = pl.ds(points - FAR_ROWS, FAR_ROWS) if name == "low_a" else pl.ds(0, points - FAR_ROWS)
            source = source.at[rows, span]
        else:
            source = source.at[:, span]
        return pltpu.make_async_copy(
            source, out_refs[name].at[:, span], out_sems.at[outs.index(name), chunk]
        )

    def here(name, chunk):
        return near[names.index(name), :, span_of(chunk)]

    sums = [name for name in names if name.startswith("sum")]

    @pl.when(active & (step == 0))
    def start_first():
        for chunk in range(2):
            for name in ("a", "b"):
                fetch(name, chunk).start()

    @pl.when(active & (step + 2 < X_STEPS))
    def start_next():
        for name in ("a", "b"):
            fetch(name, step + 2).start()

    @pl.when(active & (step == X_STEPS - 2))
    def start_kernel():
        for part in range(PLANE_STEPS):
            fetch_kernel(part).start()

    if sums:
        @pl.when(active & (step == X_STEPS))
        def start_sums():
            for chunk in range(X_STEPS):
                for name in sums:
                    fetch(name, chunk).start()

    def lanes_apart(block):
        tail = jnp.zeros((points, LANES), jnp.float32)
        wide = jnp.concatenate([block, tail], 1)
        rows = [wide[:, q * points:q * points + LANES] for q in range(ys)]
        return jnp.swapaxes(jnp.stack(rows, 0), 0, 1)

    def lanes_together(block):
        block = jnp.swapaxes(block, 0, 1)
        return jnp.concatenate([block[q][:, :points] for q in range(ys)], 1)

    def side_by_side(block):
        return jnp.concatenate([block[i] for i in range(per_step)], 1)

    @pl.when(active & (step < X_STEPS))
    def forward_x():
        for name in ("a", "b"):
            fetch(name, step).wait()
        spectrum = from_left(left_ref[...], here("a", step) * here("b", step))
        start = pl.multiple_of(step * ys, ys)
        held[:, pl.ds(start, ys), :] = lanes_apart(spectrum)

    @pl.when(active & (step >= X_STEPS) & (step < late))
    def planes():
        left = left_ref[...]
        right = right_ref[...]
        part = step - X_STEPS
        first = part * per_step
        block = held[pl.ds(first, per_step)].reshape(per_step * points, LANES)
        block = from_right(block, right).reshape(per_step, points, LANES)
        wide = from_left(left, side_by_side(block))
        fetch_kernel(part).wait()
        wide = from_left(left, wide * side_by_side(near_kernel[pl.ds(first, per_step)]))
        block = jnp.concatenate(
            [wide[:, i * LANES:(i + 1) * LANES] for i in range(per_step)], 0
        )
        block = from_right(block, right)
        held[pl.ds(first, per_step)] = block.reshape(per_step, points, LANES)

    @pl.when(active & (step >= late))
    def inverse_x():
        chunk = step - late
        start = pl.multiple_of(chunk * ys, ys)
        for name in sums:
            fetch(name, chunk).wait()
        block = lanes_together(held[:, pl.ds(start, ys), :])
        potential = from_left(left_ref[...], block)
        for_a = here("b", chunk) * potential
        if "sum_a" in has:
            for_a = for_a + jnp.where(with_sum, here("sum_a", chunk), 0.0)
        near_out[0, :, span_of(chunk)] = for_a
        if "for_b" in has:
            for_b = here("a", chunk) * potential
            if "sum_b" in has:
                for_b = for_b + here("sum_b", chunk)
            near_out[1, :, span_of(chunk)] = for_b
        for name in outs:
            give(name, chunk).start()

    @pl.when(active & (step == late + X_STEPS - 1))
    def wait_outs():
        for chunk in range(X_STEPS):
            for name in outs:
                give(name, chunk).wait()


def pair_terms(
    flags, slot, a, b, constants, sum_a=None, sum_b=None, for_b=False, halves=False, in_place=False, then=None, hand_on=False
):
    points, plane = a.shape
    kernel, left, right = constants
    optional = {"sum_a": sum_a, "sum_b": sum_b}
    optional = {name: value for name, value in optional.items() if value is not None}
    blocks = [a, b, *optional.values()]
    waited = [] if then is None else [then]
    has = list(optional) + ["for_b"] * for_b + ["halves"] * halves + ["then"] * len(waited)
    has += ["hand_on"] * hand_on
    rows = ([points - FAR_ROWS, FAR_ROWS] if halves else [points]) + [points] * for_b
    aliases = {3: 0} if in_place else {}
    if hand_on:
        aliases[1] = len(rows)
    anywhere = pl.BlockSpec(memory_space=pl.ANY)
    out = pl.pallas_call(
        functools.partial(pair_body, points, slot, has),
        grid=(2 * X_STEPS + PLANE_STEPS,),
        in_specs=[pl.BlockSpec(memory_space=pltpu.SMEM)]
        + [anywhere] * (len(blocks) + len(waited) + 1)
        + [pl.BlockSpec(table.shape, lambda i: (0, 0)) for table in (left, right)],
        out_specs=[anywhere] * (len(rows) + hand_on),
        out_shape=[
            jax.ShapeDtypeStruct((n, plane), jnp.float32) for n in rows + [points] * hand_on
        ],
        input_output_aliases=aliases,
        scratch_shapes=[
            pltpu.VMEM((points, points, LANES), jnp.float32),
            pltpu.VMEM((len(blocks), points, plane), jnp.float32),
            pltpu.VMEM((points, points, LANES), jnp.float32),
            pltpu.VMEM((2 if for_b else 1, points, plane), jnp.float32),
            pltpu.SemaphoreType.DMA((len(blocks), X_STEPS)),
            pltpu.SemaphoreType.DMA((PLANE_STEPS,)),
            pltpu.SemaphoreType.DMA((len(rows), X_STEPS)),
        ],
        compiler_params=pltpu.CompilerParams(vmem_limit_bytes=63 * 2**20),
        cost_estimate=pl.CostEstimate(
            flops=100_000_000, bytes_accessed=1_000_000, transcendentals=0
        ),
        name="pair_terms",
    )(flags, *blocks, *waited, kernel, left, right)
    return out if len(out) > 1 else out[0]


def copy_body(flags_ref, kernel_ref, block_ref, first_ref, second_ref):
    del flags_ref, kernel_ref
    first_ref[...] = block_ref[...]
    second_ref[...] = block_ref[...]


def copied(flags, kernel, block):
    points, plane = block.shape
    part = pl.BlockSpec((points, plane // X_STEPS), lambda i: (0, i))
    return pl.pallas_call(
        copy_body,
        grid=(X_STEPS,),
        in_specs=[
            pl.BlockSpec(memory_space=pltpu.SMEM),
            pl.BlockSpec(memory_space=pl.ANY),
            part,
        ],
        out_specs=[part, part],
        out_shape=[jax.ShapeDtypeStruct(block.shape, block.dtype)] * 2,
        compiler_params=pltpu.CompilerParams(vmem_limit_bytes=63 * 2**20),
        name="copied",
    )(flags, kernel, block)


def gate_body(token_ref, left_ref, partner_ref, block_ref, new_left_ref, new_block_ref):
    del token_ref, partner_ref, block_ref, new_block_ref
    new_left_ref[...] = left_ref[...]


def gate(token, left, partner, block):
    in_vmem = pl.BlockSpec(memory_space=pltpu.VMEM)
    anywhere = pl.BlockSpec(memory_space=pl.ANY)
    return pl.pallas_call(
        gate_body,
        in_specs=[in_vmem, in_vmem, anywhere, anywhere],
        out_specs=[in_vmem, anywhere],
        out_shape=[
            jax.ShapeDtypeStruct(left.shape, left.dtype),
            jax.ShapeDtypeStruct(block.shape, block.dtype),
        ],
        input_output_aliases={3: 1},
        compiler_params=pltpu.CompilerParams(vmem_limit_bytes=63 * 2**20),
        name="gate",
    )(token, left, partner, block)


def hold_body(*refs):
    del refs


def hold(block, *then):
    anywhere = pl.BlockSpec(memory_space=pl.ANY)
    return pl.pallas_call(
        hold_body,
        in_specs=[anywhere] * (1 + len(then)),
        out_specs=anywhere,
        out_shape=jax.ShapeDtypeStruct(block.shape, block.dtype),
        input_output_aliases={0: 0},
        compiler_params=pltpu.CompilerParams(vmem_limit_bytes=63 * 2**20),
        name="hold",
    )(block, *then)


def settle_body(flags_ref, home_ref, top_ref, bottom_ref, own_ref, out_ref, near, sems):
    del own_ref
    columns = out_ref.shape[1] // SETTLE_STEPS
    split = top_ref.shape[0]

    def move(parts):
        copies = []
        for i in range(SETTLE_STEPS):
            span = pl.ds(i * columns, columns)
            for j, (source_ref, start) in enumerate(parts):
                rows = pl.ds(start, source_ref.shape[0])
                copies.append((
                    pltpu.make_async_copy(
                        source_ref.at[:, span], near.at[rows, span], sems.at[0, j, i]
                    ),
                    pltpu.make_async_copy(
                        near.at[rows, span], out_ref.at[rows, span], sems.at[1, j, i]
                    ),
                ))
        for inward, outward in copies:
            inward.start()
        for inward, outward in copies:
            inward.wait()
            outward.start()
        for inward, outward in copies:
            outward.wait()

    @pl.when(flags_ref[RESULT] == 1)
    def from_home():
        move([(home_ref, 0)])

    @pl.when(flags_ref[RESULT] == 2)
    def from_far():
        move([(top_ref, 0), (bottom_ref, split)])


def settle(flags, home, top, bottom, own_sum):
    anywhere = pl.BlockSpec(memory_space=pl.ANY)
    return pl.pallas_call(
        settle_body,
        in_specs=[pl.BlockSpec(memory_space=pltpu.SMEM)] + [anywhere] * 4,
        out_specs=anywhere,
        out_shape=jax.ShapeDtypeStruct(own_sum.shape, own_sum.dtype),
        input_output_aliases={4: 0},
        scratch_shapes=[
            pltpu.VMEM(own_sum.shape, own_sum.dtype),
            pltpu.SemaphoreType.DMA((2, 2, SETTLE_STEPS)),
        ],
        compiler_params=pltpu.CompilerParams(vmem_limit_bytes=63 * 2**20),
        name="settle",
    )(flags, home, top, bottom, own_sum)


def both_halves(*pairs):
    return list(pairs) + [(15 - source, 15 - target) for source, target in pairs]


CROSSING = both_halves((3, 14), (4, 9))
PARTNERS = both_halves((8, 14), (15, 9), (9, 11), (14, 12))
ARRIVED = both_halves((14, 2), (9, 5))
SINGLES = both_halves((5, 10), (2, 13))
BESIDE = both_halves((13, 14), (10, 9))
DIRECT = both_halves((15, 10), (8, 13))
TURNED = both_halves((11, 14), (12, 9))
HOME_ACROSS = both_halves((9, 4), (14, 3))
HOME_FAR = both_halves((9, 15), (14, 8))
HOME_TURN = both_halves((9, 11), (14, 12))
HOME_TURNED = both_halves((11, 15), (12, 8))
RESULT = 12
FLAGS = {i: (1, 0, 1, 0, 1, 1, 0, 0, 0, 0, 1, 1, 0) for i in (9, 14, 6, 1)}
FLAGS.update({i: (0, 0, 0, 0, 0, 0, 1, 0, 1, 1, 0, 0, 0) for i in (10, 13, 5, 2)})
FLAGS.update({i: (0,) * RESULT + (1,) for i in (3, 4, 11, 12)})
FLAGS.update({i: (0,) * RESULT + (2,) for i in (15, 8, 0, 7)})


def sixteen_bands(orbitals, constants):
    def send(value, pairs):
        return lax.ppermute(value[None], "band", pairs)[0]

    kernel, left, right = constants
    own = orbitals[0]
    flags = jnp.asarray([FLAGS[i] for i in range(16)], jnp.int32)
    flags = flags[lax.axis_index("band")]
    pair = functools.partial(pair_terms, flags)
    crossed = send(own, CROSSING)
    partner = send(own, PARTNERS)
    own_copy, direct_copy = copied(flags, kernel, own)
    token = crossed[:8, :LANES] + own_copy[:8, :LANES]
    direct_copy = hold(direct_copy, partner)
    direct = send(direct_copy, DIRECT)
    left, held_back = gate(send(token, ARRIVED), left, direct_copy, own_copy)
    constants = (kernel, left, right)
    beside = send(held_back, BESIDE)
    single = send(held_back, SINGLES)

    partner_sum, crossed_sum = pair(0, partner, crossed, constants, for_b=True)
    own_sum, crossed_sum = pair(1, own, crossed, constants, sum_b=crossed_sum, for_b=True, then=direct)
    home = send(crossed_sum, HOME_ACROSS)
    partner = hold(partner, own_sum)
    turned = send(partner, TURNED)
    top, bottom = pair(2, partner, beside, constants, sum_a=partner_sum, halves=True)
    bottom = send(bottom, HOME_TURN)
    top = send(top, HOME_FAR)
    bottom = send(bottom, HOME_TURNED)
    own_sum = pair(3, own, direct, constants, sum_a=own_sum, in_place=True)
    own_sum = pair(4, own, single, constants, sum_a=own_sum, in_place=True, then=home)
    own_sum = pair(5, own, turned, constants, sum_a=own_sum, in_place=True)
    return settle(flags, home, top, bottom, own_sum)[None]


def any_bands(orbitals, constants):
    own = orbitals[0]
    flags = jnp.ones((4,), jnp.int32)
    lower = from_behind(orbitals, "band", OFFSET)[0]
    upper = from_behind(orbitals, "band", -OFFSET)[0]
    total = pair_terms(flags, 0, own, lower, constants)
    return pair_terms(flags, 1, own, upper, constants, sum_a=total)[None]


def local(bands, orbitals):
    points = orbitals.shape[1]
    constants = (screened_kernel(points), *hartley_tables(points))
    if bands == 16:
        return sixteen_bands(orbitals, constants)
    return any_bands(orbitals, constants)


def solution(mesh):
    return jax.shard_map(
        functools.partial(local, mesh.shape["band"]),
        mesh=mesh,
        in_specs=(P(("groups", "band"), None, None),),
        out_specs=P(("groups", "band"), None, None),
        check_vma=False,
    )
```

```python
import functools
import math

import jax
import jax.numpy as jnp
import numpy as np
from jax import lax
from jax.experimental import pallas as pl
from jax.experimental.pallas import tpu as pltpu
from jax.sharding import PartitionSpec as P

OFFSET = 5
screening = 5.44
LANES = 128
X_STEPS = 3
PLANE_STEPS = 2
SETTLE_STEPS = 6
FAR_ROWS = 40


def from_behind(value, axis, by):
    count = lax.axis_size(axis)
    return lax.ppermute(value, axis, [(i, (i + by) % count) for i in range(count)])


def screened_kernel(points):
    signed = jnp.arange(LANES, dtype=jnp.int32)
    inside = signed < points
    signed = jnp.where(signed >= points // 2, signed - points, signed)
    wavenumber = signed.astype(jnp.float32) * (2.0 * math.pi / points)
    squared = (
        wavenumber[:points, None, None] ** 2
        + wavenumber[None, :points, None] ** 2
        + wavenumber[None, None, :] ** 2
    )
    screen_rate = screening / points
    finite = jnp.where(squared > 0.0, squared, 1.0)
    screened = 4.0 * math.pi / finite * -jnp.expm1(-finite / (4.0 * screen_rate * screen_rate))
    kernel = jnp.where(squared > 0.0, screened, math.pi / (screen_rate * screen_rate))
    return jnp.where(inside, kernel / -float(points * points * points), 0.0)


def hartley_tables(points):
    counter = np.arange(points)
    angles = 2.0 * np.pi * (counter[:, None] * counter[None, :] % points) / points
    table = np.cos(angles) + np.sin(angles)
    high = table.astype(jnp.bfloat16)
    low = (table - high.astype(np.float64)).astype(jnp.bfloat16)
    left = np.zeros((2 * points, 2 * points), jnp.bfloat16)
    left[:points, :points] = high
    left[:points, points:] = high
    left[points:, :points] = low
    right = np.zeros((2 * LANES, 2 * LANES), jnp.bfloat16)
    right[:points, :points] = high
    right[:points, LANES:LANES + points] = low
    right[LANES:LANES + points, :points] = high
    return jnp.asarray(left), jnp.asarray(right)


def two_terms(value):
    high = value.astype(jnp.bfloat16)
    low = (value - high.astype(jnp.float32)).astype(jnp.bfloat16)
    return high, low


def from_left(left, value):
    half = value.shape[0]
    terms = jnp.concatenate(two_terms(value), 0)
    out = jnp.dot(left, terms, preferred_element_type=jnp.float32)
    return out[:half] + out[half:]


def from_right(value, right):
    out = jnp.dot(jnp.concatenate(two_terms(value), 1), right, preferred_element_type=jnp.float32)
    return out[:, :LANES] + out[:, LANES:]


def pair_body(points, slot, jobs, has, *refs):
    refs = list(refs)
    flags_ref = refs.pop(0)
    a_names = ["a%d" % job for job in range(jobs)]
    names = a_names + ["b"] + ["sum_a"] * ("sum_a" in has)
    far = {name: refs.pop(0) for name in names}
    if "then" in has:
        refs.pop(0)
    kernel_ref, left_ref, right_ref = refs.pop(0), refs.pop(0), refs.pop(0)
    outs = ["for_a%d" % job for job in range(jobs)]
    if "halves" in has:
        outs.append("low_a0")
    if "for_b" in has:
        outs.append("for_b")
    out_refs = {name: refs.pop(0) for name in outs}
    held, near, near_kernel, near_out, sems, kernel_sems, out_sems = refs
    step = pl.program_id(0)
    active = flags_ref[2 * slot] == 1
    with_sum = flags_ref[2 * slot + 1] == 1
    columns = near.shape[2] // X_STEPS
    ys = columns // points
    per_step = points // PLANE_STEPS
    late = X_STEPS + PLANE_STEPS
    steps = late + X_STEPS
    job = step // steps if jobs > 1 else 0
    at = step % steps if jobs > 1 else step

    def span_of(chunk):
        start = chunk * columns
        return pl.ds(start if isinstance(chunk, int) else pl.multiple_of(start, columns), columns)

    def fetch(name, chunk):
        place, span = names.index(name), span_of(chunk)
        return pltpu.make_async_copy(
            far[name].at[:, span], near.at[place, :, span], sems.at[place, chunk]
        )

    def fetch_kernel(part):
        span = pl.ds(part * per_step, per_step)
        return pltpu.make_async_copy(
            kernel_ref.at[span], near_kernel.at[span], kernel_sems.at[part]
        )

    def give(name, chunk):
        span = span_of(chunk)
        source = near_out.at[jobs if name == "for_b" else int(name[-1])]
        if "halves" in has and name != "for_b":
            rows = pl.ds(points - FAR_ROWS, FAR_ROWS) if name == "low_a0" else pl.ds(0, points - FAR_ROWS)
            source = source.at[rows, span]
        else:
            source = source.at[:, span]
        return pltpu.make_async_copy(
            source, out_refs[name].at[:, span], out_sems.at[outs.index(name), chunk]
        )

    def here(name, chunk):
        place = job if name == "a" else names.index(name)
        return near[place, :, span_of(chunk)]

    def when_job(number, work):
        if jobs > 1:
            pl.when(job == number)(work)
        elif number == 0:
            work()

    @pl.when(active & (step == 0))
    def start_first():
        for chunk in range(2):
            for name in ("a0", "b"):
                fetch(name, chunk).start()

    @pl.when(active & (step + 2 < X_STEPS))
    def start_next():
        for name in ("a0", "b"):
            fetch(name, step + 2).start()

    @pl.when(active & (step == X_STEPS - 2))
    def start_kernel():
        for part in range(PLANE_STEPS):
            fetch_kernel(part).start()

    @pl.when(active & (step == X_STEPS))
    def start_rest():
        for chunk in range(X_STEPS):
            for name in a_names[1:] + ["sum_a"] * ("sum_a" in has):
                fetch(name, chunk).start()

    def lanes_apart(block):
        tail = jnp.zeros((points, LANES), jnp.float32)
        wide = jnp.concatenate([block, tail], 1)
        rows = [wide[:, q * points:q * points + LANES] for q in range(ys)]
        return jnp.swapaxes(jnp.stack(rows, 0), 0, 1)

    def lanes_together(block):
        block = jnp.swapaxes(block, 0, 1)
        return jnp.concatenate([block[q][:, :points] for q in range(ys)], 1)

    def side_by_side(block):
        return jnp.concatenate([block[i] for i in range(per_step)], 1)

    @pl.when(active & (at < X_STEPS))
    def forward_x():
        chunk = at

        def first_waits():
            fetch("a0", chunk).wait()
            fetch("b", chunk).wait()

        when_job(0, first_waits)
        for number in range(1, jobs):
            when_job(number, fetch(a_names[number], chunk).wait)
        spectrum = from_left(left_ref[...], here("a", chunk) * here("b", chunk))
        start = pl.multiple_of(chunk * ys, ys)
        held[:, pl.ds(start, ys), :] = lanes_apart(spectrum)

    @pl.when(active & (at >= X_STEPS) & (at < late))
    def planes():
        part = at - X_STEPS
        left = left_ref[...]
        right = right_ref[...]
        first = part * per_step
        when_job(0, lambda: fetch_kernel(part).wait())
        block = held[pl.ds(first, per_step)].reshape(per_step * points, LANES)
        block = from_right(block, right).reshape(per_step, points, LANES)
        wide = from_left(left, side_by_side(block))
        wide = from_left(left, wide * side_by_side(near_kernel[pl.ds(first, per_step)]))
        block = jnp.concatenate(
            [wide[:, i * LANES:(i + 1) * LANES] for i in range(per_step)], 0
        )
        block = from_right(block, right)
        held[pl.ds(first, per_step)] = block.reshape(per_step, points, LANES)

    @pl.when(active & (at >= late))
    def inverse_x():
        chunk = at - late
        start = pl.multiple_of(chunk * ys, ys)
        if "sum_a" in has:
            fetch("sum_a", chunk).wait()
        block = lanes_together(held[:, pl.ds(start, ys), :])
        potential = from_left(left_ref[...], block)
        for_a = here("b", chunk) * potential
        if "sum_a" in has:
            for_a = for_a + jnp.where(with_sum, here("sum_a", chunk), 0.0)
        near_out[job, :, span_of(chunk)] = for_a
        if "for_b" in has:
            for_b = here("a", chunk) * potential
            if jobs > 1:
                for_b = for_b + jnp.where(job > 0, near_out[jobs, :, span_of(chunk)], 0.0)
            near_out[jobs, :, span_of(chunk)] = for_b

        def give_all(number):
            for name in outs:
                if number == (jobs - 1 if name == "for_b" else int(name[-1])):
                    give(name, chunk).start()

        for number in range(jobs):
            when_job(number, functools.partial(give_all, number))

    @pl.when(active & (step == jobs * steps - 1))
    def wait_outs():
        for chunk in range(X_STEPS):
            for name in outs:
                give(name, chunk).wait()


def pair_terms(
    flags, slot, a, b, constants, sum_a=None, for_b=False, halves=False, in_place=False, then=None
):
    points, plane = b.shape
    kernel, left, right = constants
    jobs = len(a)
    blocks = [*a, b] + [sum_a] * (sum_a is not None)
    waited = [] if then is None else [then]
    has = ["sum_a"] * (sum_a is not None) + ["for_b"] * for_b + ["halves"] * halves + ["then"] * len(waited)
    rows = ([points - FAR_ROWS, FAR_ROWS] if halves else [points] * jobs) + [points] * for_b
    anywhere = pl.BlockSpec(memory_space=pl.ANY)
    return pl.pallas_call(
        functools.partial(pair_body, points, slot, jobs, has),
        grid=(jobs * (2 * X_STEPS + PLANE_STEPS),),
        in_specs=[pl.BlockSpec(memory_space=pltpu.SMEM)]
        + [anywhere] * (len(blocks) + len(waited) + 1)
        + [pl.BlockSpec(table.shape, lambda i: (0, 0)) for table in (left, right)],
        out_specs=[anywhere] * len(rows),
        out_shape=[jax.ShapeDtypeStruct((n, plane), jnp.float32) for n in rows],
        input_output_aliases={3: 0} if in_place else {},
        scratch_shapes=[
            pltpu.VMEM((points, points, LANES), jnp.float32),
            pltpu.VMEM((len(blocks), points, plane), jnp.float32),
            pltpu.VMEM((points, points, LANES), jnp.float32),
            pltpu.VMEM((jobs + for_b, points, plane), jnp.float32),
            pltpu.SemaphoreType.DMA((len(blocks), X_STEPS)),
            pltpu.SemaphoreType.DMA((PLANE_STEPS,)),
            pltpu.SemaphoreType.DMA((len(rows), X_STEPS)),
        ],
        compiler_params=pltpu.CompilerParams(vmem_limit_bytes=63 * 2**20),
        cost_estimate=pl.CostEstimate(
            flops=100_000_000, bytes_accessed=1_000_000, transcendentals=0
        ),
        name="pair_terms",
    )(flags, *blocks, *waited, kernel, left, right)


def copy_body(flags_ref, kernel_ref, block_ref, first_ref, second_ref):
    del flags_ref, kernel_ref
    first_ref[...] = block_ref[...]
    second_ref[...] = block_ref[...]


def copied(flags, kernel, block):
    points, plane = block.shape
    part = pl.BlockSpec((points, plane // X_STEPS), lambda i: (0, i))
    return pl.pallas_call(
        copy_body,
        grid=(X_STEPS,),
        in_specs=[
            pl.BlockSpec(memory_space=pltpu.SMEM),
            pl.BlockSpec(memory_space=pl.ANY),
            part,
        ],
        out_specs=[part, part],
        out_shape=[jax.ShapeDtypeStruct(block.shape, block.dtype)] * 2,
        compiler_params=pltpu.CompilerParams(vmem_limit_bytes=63 * 2**20),
        name="copied",
    )(flags, kernel, block)


def gate_body(token_ref, left_ref, partner_ref, block_ref, new_left_ref, new_block_ref):
    del token_ref, partner_ref, block_ref, new_block_ref
    new_left_ref[...] = left_ref[...]


def gate(token, left, partner, block):
    in_vmem = pl.BlockSpec(memory_space=pltpu.VMEM)
    anywhere = pl.BlockSpec(memory_space=pl.ANY)
    return pl.pallas_call(
        gate_body,
        in_specs=[anywhere, in_vmem, anywhere, anywhere],
        out_specs=[in_vmem, anywhere],
        out_shape=[
            jax.ShapeDtypeStruct(left.shape, left.dtype),
            jax.ShapeDtypeStruct(block.shape, block.dtype),
        ],
        input_output_aliases={3: 1},
        compiler_params=pltpu.CompilerParams(vmem_limit_bytes=63 * 2**20),
        name="gate",
    )(token, left, partner, block)


def hold_body(*refs):
    del refs


def hold(block, *then):
    anywhere = pl.BlockSpec(memory_space=pl.ANY)
    return pl.pallas_call(
        hold_body,
        in_specs=[anywhere] * (1 + len(then)),
        out_specs=anywhere,
        out_shape=jax.ShapeDtypeStruct(block.shape, block.dtype),
        input_output_aliases={0: 0},
        compiler_params=pltpu.CompilerParams(vmem_limit_bytes=63 * 2**20),
        name="hold",
    )(block, *then)


def settle_body(wanted, count, flags_ref, *refs):
    parts, (out_ref, near, sems) = refs[:count], refs[count + 1:]
    columns = out_ref.shape[1] // SETTLE_STEPS

    @pl.when(flags_ref[RESULT] == wanted)
    def move():
        copies = []
        for i in range(SETTLE_STEPS):
            span = pl.ds(i * columns, columns)
            start = 0
            for j, part in enumerate(parts):
                rows = pl.ds(start, part.shape[0])
                start += part.shape[0]
                copies.append((
                    pltpu.make_async_copy(part.at[:, span], near.at[rows, span], sems.at[0, j, i]),
                    pltpu.make_async_copy(near.at[rows, span], out_ref.at[rows, span], sems.at[1, j, i]),
                ))
        for inward, outward in copies:
            inward.start()
        for inward, outward in copies:
            inward.wait()
            outward.start()
        for inward, outward in copies:
            outward.wait()


def settle(flags, wanted, parts, own_sum):
    anywhere = pl.BlockSpec(memory_space=pl.ANY)
    count = len(parts)
    return pl.pallas_call(
        functools.partial(settle_body, wanted, count),
        in_specs=[pl.BlockSpec(memory_space=pltpu.SMEM)] + [anywhere] * (count + 1),
        out_specs=anywhere,
        out_shape=jax.ShapeDtypeStruct(own_sum.shape, own_sum.dtype),
        input_output_aliases={count + 1: 0},
        scratch_shapes=[
            pltpu.VMEM(own_sum.shape, own_sum.dtype),
            pltpu.SemaphoreType.DMA((2, count, SETTLE_STEPS)),
        ],
        compiler_params=pltpu.CompilerParams(vmem_limit_bytes=63 * 2**20),
        name="settle",
    )(flags, *parts, own_sum)


def both_halves(*pairs):
    return list(pairs) + [(15 - source, 15 - target) for source, target in pairs]


CROSSING = both_halves((3, 14), (4, 9))
PARTNERS = both_halves((8, 14), (15, 9), (9, 11), (14, 12))
ARRIVED = both_halves((14, 2), (9, 5))
SINGLES = both_halves((5, 10), (2, 13))
BESIDE = both_halves((13, 14), (10, 9))
DIRECT = both_halves((15, 10), (8, 13))
TURNED = both_halves((11, 14), (12, 9))
HOME_ACROSS = both_halves((9, 4), (14, 3))
HOME_FAR = both_halves((9, 15), (14, 8))
HOME_TURN = both_halves((9, 11), (14, 12))
HOME_TURNED = both_halves((11, 15), (12, 8))
RESULT = 10
FLAGS = {i: (1, 0, 1, 1, 0, 0, 0, 0, 1, 1, 0) for i in (9, 14, 6, 1)}
FLAGS.update({i: (0, 0, 0, 0, 1, 0, 1, 1, 0, 0, 0) for i in (10, 13, 5, 2)})
FLAGS.update({i: (0,) * RESULT + (1,) for i in (3, 4, 11, 12)})
FLAGS.update({i: (0,) * RESULT + (2,) for i in (15, 8, 0, 7)})


def sixteen_bands(orbitals, constants):
    def send(value, pairs):
        return lax.ppermute(value[None], "band", pairs)[0]

    kernel, left, right = constants
    own = orbitals[0]
    flags = jnp.asarray([FLAGS[i] for i in range(16)], jnp.int32)
    flags = flags[lax.axis_index("band")]
    pair = functools.partial(pair_terms, flags)
    crossed = send(own, CROSSING)
    partner = send(own, PARTNERS)
    own_copy, direct_copy = copied(flags, kernel, own)
    token = crossed[:8, :LANES] + own_copy[:8, :LANES]
    direct_copy = hold(direct_copy, partner)
    direct = send(direct_copy, DIRECT)
    left, held_back = gate(send(token, ARRIVED), left, direct_copy, own_copy)
    constants = (kernel, left, right)
    beside = send(held_back, BESIDE)
    single = send(held_back, SINGLES)

    partner_sum, own_sum, crossed_sum = pair(
        0, [partner, own], crossed, constants, for_b=True, then=direct
    )
    home = send(crossed_sum, HOME_ACROSS)
    partner = hold(partner, own_sum)
    turned = send(partner, TURNED)
    top, bottom = pair(1, [partner], beside, constants, sum_a=partner_sum, halves=True)
    bottom = send(bottom, HOME_TURN)
    top = send(top, HOME_FAR)
    bottom = send(bottom, HOME_TURNED)
    (own_sum,) = pair(2, [own], direct, constants, sum_a=own_sum, in_place=True)
    (own_sum,) = pair(3, [own], single, constants, sum_a=own_sum, in_place=True)
    own_sum = settle(flags, 1, [home], own_sum)
    (own_sum,) = pair(4, [own], turned, constants, sum_a=own_sum, in_place=True)
    return settle(flags, 2, [top, bottom], own_sum)[None]


def any_bands(orbitals, constants):
    own = orbitals[0]
    flags = jnp.ones((4,), jnp.int32)
    lower = from_behind(orbitals, "band", OFFSET)[0]
    upper = from_behind(orbitals, "band", -OFFSET)[0]
    (total,) = pair_terms(flags, 0, [own], lower, constants)
    return pair_terms(flags, 1, [own], upper, constants, sum_a=total)[0][None]


def local(bands, orbitals):
    points = orbitals.shape[1]
    constants = (screened_kernel(points), *hartley_tables(points))
    if bands == 16:
        return sixteen_bands(orbitals, constants)
    return any_bands(orbitals, constants)


def solution(mesh):
    return jax.shard_map(
        functools.partial(local, mesh.shape["band"]),
        mesh=mesh,
        in_specs=(P(("groups", "band"), None, None),),
        out_specs=P(("groups", "band"), None, None),
        check_vma=False,
    )
```

```python
import functools
import math

import jax
import jax.numpy as jnp
import numpy as np
from jax import lax
from jax.experimental import pallas as pl
from jax.experimental.pallas import tpu as pltpu
from jax.sharding import PartitionSpec as P

OFFSET = 5
screening = 5.44
LANES = 128
X_STEPS = 3
PLANE_STEPS = 2
SETTLE_STEPS = 6
FAR_ROWS = 32


def from_behind(value, axis, by):
    count = lax.axis_size(axis)
    return lax.ppermute(value, axis, [(i, (i + by) % count) for i in range(count)])


def screened_kernel(points):
    signed = jnp.arange(LANES, dtype=jnp.int32)
    inside = signed < points
    signed = jnp.where(signed >= points // 2, signed - points, signed)
    wavenumber = signed.astype(jnp.float32) * (2.0 * math.pi / points)
    squared = (
        wavenumber[:points, None, None] ** 2
        + wavenumber[None, :points, None] ** 2
        + wavenumber[None, None, :] ** 2
    )
    screen_rate = screening / points
    finite = jnp.where(squared > 0.0, squared, 1.0)
    screened = 4.0 * math.pi / finite * -jnp.expm1(-finite / (4.0 * screen_rate * screen_rate))
    kernel = jnp.where(squared > 0.0, screened, math.pi / (screen_rate * screen_rate))
    return jnp.where(inside, kernel / -float(points * points * points), 0.0)


def hartley_tables(points):
    counter = np.arange(points)
    angles = 2.0 * np.pi * (counter[:, None] * counter[None, :] % points) / points
    table = np.cos(angles) + np.sin(angles)
    high = table.astype(jnp.bfloat16)
    low = (table - high.astype(np.float64)).astype(jnp.bfloat16)
    left = np.zeros((2 * points, 2 * points), jnp.bfloat16)
    left[:points, :points] = high
    left[:points, points:] = high
    left[points:, :points] = low
    right = np.zeros((2 * LANES, 2 * LANES), jnp.bfloat16)
    right[:points, :points] = high
    right[:points, LANES:LANES + points] = low
    right[LANES:LANES + points, :points] = high
    return jnp.asarray(left), jnp.asarray(right)


def two_terms(value):
    high = value.astype(jnp.bfloat16)
    low = (value - high.astype(jnp.float32)).astype(jnp.bfloat16)
    return high, low


def from_left(left, value):
    half = value.shape[0]
    terms = jnp.concatenate(two_terms(value), 0)
    out = jnp.dot(left, terms, preferred_element_type=jnp.float32)
    return out[:half] + out[half:]


def from_right(value, right):
    out = jnp.dot(jnp.concatenate(two_terms(value), 1), right, preferred_element_type=jnp.float32)
    return out[:, :LANES] + out[:, LANES:]


def pair_body(points, slot, jobs, has, *refs):
    refs = list(refs)
    flags_ref = refs.pop(0)
    a_names = ["a%d" % job for job in range(jobs)]
    names = a_names + ["b"] + ["sum_a"] * ("sum_a" in has)
    far = {name: refs.pop(0) for name in names}
    if "then" in has:
        refs.pop(0)
    kernel_ref, left_ref, right_ref = refs.pop(0), refs.pop(0), refs.pop(0)
    outs = ["for_a%d" % job for job in range(jobs)]
    if "halves" in has:
        outs.append("low_a0")
    if "for_b" in has:
        outs.append("for_b")
    out_refs = {name: refs.pop(0) for name in outs}
    held, near, near_kernel, near_out, sems, kernel_sems, out_sems = refs
    step = pl.program_id(0)
    active = flags_ref[2 * slot] == 1
    with_sum = flags_ref[2 * slot + 1] == 1
    columns = near.shape[2] // X_STEPS
    ys = columns // points
    per_step = points // PLANE_STEPS
    late = X_STEPS + PLANE_STEPS
    steps = late + X_STEPS
    job = step // steps if jobs > 1 else 0
    at = step % steps if jobs > 1 else step

    def span_of(chunk):
        start = chunk * columns
        return pl.ds(start if isinstance(chunk, int) else pl.multiple_of(start, columns), columns)

    def fetch(name, chunk):
        place, span = names.index(name), span_of(chunk)
        return pltpu.make_async_copy(
            far[name].at[:, span], near.at[place, :, span], sems.at[place, chunk]
        )

    def fetch_kernel(part):
        span = pl.ds(part * per_step, per_step)
        return pltpu.make_async_copy(
            kernel_ref.at[span], near_kernel.at[span], kernel_sems.at[part]
        )

    def give(name, chunk):
        span = span_of(chunk)
        source = near_out.at[jobs if name == "for_b" else int(name[-1])]
        if "halves" in has and name != "for_b":
            rows = pl.ds(points - FAR_ROWS, FAR_ROWS) if name == "low_a0" else pl.ds(0, points - FAR_ROWS)
            source = source.at[rows, span]
        else:
            source = source.at[:, span]
        return pltpu.make_async_copy(
            source, out_refs[name].at[:, span], out_sems.at[outs.index(name), chunk]
        )

    def here(name, chunk):
        place = job if name == "a" else names.index(name)
        return near[place, :, span_of(chunk)]

    def when_job(number, work):
        if jobs > 1:
            pl.when(job == number)(work)
        elif number == 0:
            work()

    @pl.when(active & (step == 0))
    def start_first():
        for chunk in range(2):
            for name in ("a0", "b"):
                fetch(name, chunk).start()

    @pl.when(active & (step + 2 < X_STEPS))
    def start_next():
        for name in ("a0", "b"):
            fetch(name, step + 2).start()

    @pl.when(active & (step == X_STEPS - 2))
    def start_kernel():
        for part in range(PLANE_STEPS):
            fetch_kernel(part).start()

    @pl.when(active & (step == X_STEPS))
    def start_rest():
        for chunk in range(X_STEPS):
            for name in a_names[1:] + ["sum_a"] * ("sum_a" in has):
                fetch(name, chunk).start()

    def lanes_apart(block):
        tail = jnp.zeros((points, LANES), jnp.float32)
        wide = jnp.concatenate([block, tail], 1)
        rows = [wide[:, q * points:q * points + LANES] for q in range(ys)]
        return jnp.swapaxes(jnp.stack(rows, 0), 0, 1)

    def lanes_together(block):
        block = jnp.swapaxes(block, 0, 1)
        return jnp.concatenate([block[q][:, :points] for q in range(ys)], 1)

    def side_by_side(block):
        return jnp.concatenate([block[i] for i in range(per_step)], 1)

    @pl.when(active & (at < X_STEPS))
    def forward_x():
        chunk = at

        def first_waits():
            fetch("a0", chunk).wait()
            fetch("b", chunk).wait()

        when_job(0, first_waits)
        for number in range(1, jobs):
            when_job(number, fetch(a_names[number], chunk).wait)
        spectrum = from_left(left_ref[...], here("a", chunk) * here("b", chunk))
        start = pl.multiple_of(chunk * ys, ys)
        held[:, pl.ds(start, ys), :] = lanes_apart(spectrum)

    @pl.when(active & (at >= X_STEPS) & (at < late))
    def planes():
        part = at - X_STEPS
        left = left_ref[...]
        right = right_ref[...]
        first = part * per_step
        when_job(0, lambda: fetch_kernel(part).wait())
        block = held[pl.ds(first, per_step)].reshape(per_step * points, LANES)
        block = from_right(block, right).reshape(per_step, points, LANES)
        wide = from_left(left, side_by_side(block))
        wide = from_left(left, wide * side_by_side(near_kernel[pl.ds(first, per_step)]))
        block = jnp.concatenate(
            [wide[:, i * LANES:(i + 1) * LANES] for i in range(per_step)], 0
        )
        block = from_right(block, right)
        held[pl.ds(first, per_step)] = block.reshape(per_step, points, LANES)

    @pl.when(active & (at >= late))
    def inverse_x():
        chunk = at - late
        start = pl.multiple_of(chunk * ys, ys)
        if "sum_a" in has:
            fetch("sum_a", chunk).wait()
        block = lanes_together(held[:, pl.ds(start, ys), :])
        potential = from_left(left_ref[...], block)
        for_a = here("b", chunk) * potential
        if "sum_a" in has:
            for_a = for_a + jnp.where(with_sum, here("sum_a", chunk), 0.0)
        near_out[job, :, span_of(chunk)] = for_a
        if "for_b" in has:
            for_b = here("a", chunk) * potential
            if jobs > 1:
                for_b = for_b + jnp.where(job > 0, near_out[jobs, :, span_of(chunk)], 0.0)
            near_out[jobs, :, span_of(chunk)] = for_b

        def give_all(number):
            for name in outs:
                if number == (jobs - 1 if name == "for_b" else int(name[-1])):
                    give(name, chunk).start()

        for number in range(jobs):
            when_job(number, functools.partial(give_all, number))

    @pl.when(active & (step == jobs * steps - 1))
    def wait_outs():
        for chunk in range(X_STEPS):
            for name in outs:
                give(name, chunk).wait()


def pair_terms(
    flags, slot, a, b, constants, sum_a=None, for_b=False, halves=False, in_place=False, then=None
):
    points, plane = b.shape
    kernel, left, right = constants
    jobs = len(a)
    blocks = [*a, b] + [sum_a] * (sum_a is not None)
    waited = [] if then is None else [then]
    has = ["sum_a"] * (sum_a is not None) + ["for_b"] * for_b + ["halves"] * halves + ["then"] * len(waited)
    rows = ([points - FAR_ROWS, FAR_ROWS] if halves else [points] * jobs) + [points] * for_b
    anywhere = pl.BlockSpec(memory_space=pl.ANY)
    return pl.pallas_call(
        functools.partial(pair_body, points, slot, jobs, has),
        grid=(jobs * (2 * X_STEPS + PLANE_STEPS),),
        in_specs=[pl.BlockSpec(memory_space=pltpu.SMEM)]
        + [anywhere] * (len(blocks) + len(waited) + 1)
        + [pl.BlockSpec(table.shape, lambda i: (0, 0)) for table in (left, right)],
        out_specs=[anywhere] * len(rows),
        out_shape=[jax.ShapeDtypeStruct((n, plane), jnp.float32) for n in rows],
        input_output_aliases={3: 0} if in_place else {},
        scratch_shapes=[
            pltpu.VMEM((points, points, LANES), jnp.float32),
            pltpu.VMEM((len(blocks), points, plane), jnp.float32),
            pltpu.VMEM((points, points, LANES), jnp.float32),
            pltpu.VMEM((jobs + for_b, points, plane), jnp.float32),
            pltpu.SemaphoreType.DMA((len(blocks), X_STEPS)),
            pltpu.SemaphoreType.DMA((PLANE_STEPS,)),
            pltpu.SemaphoreType.DMA((len(rows), X_STEPS)),
        ],
        compiler_params=pltpu.CompilerParams(vmem_limit_bytes=63 * 2**20),
        cost_estimate=pl.CostEstimate(
            flops=100_000_000, bytes_accessed=1_000_000, transcendentals=0
        ),
        name="pair_terms",
    )(flags, *blocks, *waited, kernel, left, right)


def copy_body(flags_ref, kernel_ref, block_ref, first_ref, second_ref):
    del flags_ref, kernel_ref
    first_ref[...] = block_ref[...]
    second_ref[...] = block_ref[...]


def copied(flags, kernel, block):
    points, plane = block.shape
    part = pl.BlockSpec((points, plane // X_STEPS), lambda i: (0, i))
    return pl.pallas_call(
        copy_body,
        grid=(X_STEPS,),
        in_specs=[
            pl.BlockSpec(memory_space=pltpu.SMEM),
            pl.BlockSpec(memory_space=pl.ANY),
            part,
        ],
        out_specs=[part, part],
        out_shape=[jax.ShapeDtypeStruct(block.shape, block.dtype)] * 2,
        compiler_params=pltpu.CompilerParams(vmem_limit_bytes=63 * 2**20),
        name="copied",
    )(flags, kernel, block)


def gate_body(*refs):
    del refs


def gate(token, left, partner, block):
    anywhere = pl.BlockSpec(memory_space=pl.ANY)
    return pl.pallas_call(
        gate_body,
        in_specs=[anywhere] * 4,
        out_specs=[anywhere] * 2,
        out_shape=[
            jax.ShapeDtypeStruct(left.shape, left.dtype),
            jax.ShapeDtypeStruct(block.shape, block.dtype),
        ],
        input_output_aliases={1: 0, 3: 1},
        compiler_params=pltpu.CompilerParams(vmem_limit_bytes=63 * 2**20),
        name="gate",
    )(token, left, partner, block)


def hold_body(*refs):
    del refs


def hold(block, *then):
    anywhere = pl.BlockSpec(memory_space=pl.ANY)
    return pl.pallas_call(
        hold_body,
        in_specs=[anywhere] * (1 + len(then)),
        out_specs=anywhere,
        out_shape=jax.ShapeDtypeStruct(block.shape, block.dtype),
        input_output_aliases={0: 0},
        compiler_params=pltpu.CompilerParams(vmem_limit_bytes=63 * 2**20),
        name="hold",
    )(block, *then)


def settle_body(wanted, count, flags_ref, *refs):
    parts, (out_ref, near, sems) = refs[:count], refs[count + 1:]
    columns = out_ref.shape[1] // SETTLE_STEPS

    @pl.when(flags_ref[RESULT] == wanted)
    def move():
        copies = []
        for i in range(SETTLE_STEPS):
            span = pl.ds(i * columns, columns)
            start = 0
            for j, part in enumerate(parts):
                rows = pl.ds(start, part.shape[0])
                start += part.shape[0]
                copies.append((
                    pltpu.make_async_copy(part.at[:, span], near.at[rows, span], sems.at[0, j, i]),
                    pltpu.make_async_copy(near.at[rows, span], out_ref.at[rows, span], sems.at[1, j, i]),
                ))
        for inward, outward in copies:
            inward.start()
        for inward, outward in copies:
            inward.wait()
            outward.start()
        for inward, outward in copies:
            outward.wait()


def settle(flags, wanted, parts, own_sum):
    anywhere = pl.BlockSpec(memory_space=pl.ANY)
    count = len(parts)
    return pl.pallas_call(
        functools.partial(settle_body, wanted, count),
        in_specs=[pl.BlockSpec(memory_space=pltpu.SMEM)] + [anywhere] * (count + 1),
        out_specs=anywhere,
        out_shape=jax.ShapeDtypeStruct(own_sum.shape, own_sum.dtype),
        input_output_aliases={count + 1: 0},
        scratch_shapes=[
            pltpu.VMEM(own_sum.shape, own_sum.dtype),
            pltpu.SemaphoreType.DMA((2, count, SETTLE_STEPS)),
        ],
        compiler_params=pltpu.CompilerParams(vmem_limit_bytes=63 * 2**20),
        name="settle",
    )(flags, *parts, own_sum)


def both_halves(*pairs):
    return list(pairs) + [(15 - source, 15 - target) for source, target in pairs]


CROSSING = both_halves((3, 14), (4, 9))
PARTNERS = both_halves((8, 14), (15, 9), (9, 11), (14, 12))
ARRIVED = both_halves((14, 2), (9, 5))
SINGLES = both_halves((5, 10), (2, 13))
BESIDE = both_halves((13, 14), (10, 9))
DIRECT = both_halves((15, 10), (8, 13))
TURNED = both_halves((11, 14), (12, 9))
HOME_ACROSS = both_halves((9, 4), (14, 3))
HOME_FAR = both_halves((9, 15), (14, 8))
HOME_TURN = both_halves((9, 11), (14, 12))
HOME_TURNED = both_halves((11, 15), (12, 8))
RESULT = 10
FLAGS = {i: (1, 0, 1, 1, 0, 0, 0, 0, 1, 1, 0) for i in (9, 14, 6, 1)}
FLAGS.update({i: (0, 0, 0, 0, 1, 0, 1, 1, 0, 0, 0) for i in (10, 13, 5, 2)})
FLAGS.update({i: (0,) * RESULT + (1,) for i in (3, 4, 11, 12)})
FLAGS.update({i: (0,) * RESULT + (2,) for i in (15, 8, 0, 7)})


def sixteen_bands(orbitals, constants):
    def send(value, pairs):
        return lax.ppermute(value[None], "band", pairs)[0]

    kernel, left, right = constants
    own = orbitals[0]
    flags = jnp.asarray([FLAGS[i] for i in range(16)], jnp.int32)
    flags = flags[lax.axis_index("band")]
    pair = functools.partial(pair_terms, flags)
    crossed = send(own, CROSSING)
    partner = send(own, PARTNERS)
    own_copy, direct_copy = copied(flags, kernel, own)
    token = crossed[:8, :LANES] + own_copy[:8, :LANES]
    direct_copy = hold(direct_copy, partner)
    direct = send(direct_copy, DIRECT)
    left, held_back = gate(send(token, ARRIVED), left, direct_copy, own_copy)
    constants = (kernel, left, right)
    beside = send(held_back, BESIDE)
    single = send(held_back, SINGLES)

    partner_sum, own_sum, crossed_sum = pair(
        0, [partner, own], crossed, constants, for_b=True, then=direct
    )
    home = send(crossed_sum, HOME_ACROSS)
    partner = hold(partner, own_sum)
    turned = send(partner, TURNED)
    top, bottom = pair(1, [partner], beside, constants, sum_a=partner_sum, halves=True)
    bottom = send(bottom, HOME_TURN)
    top = send(top, HOME_FAR)
    (own_sum,) = pair(2, [own], direct, constants, sum_a=own_sum, in_place=True)
    (own_sum,) = pair(3, [own], single, constants, sum_a=own_sum, in_place=True)
    bottom = send(hold(bottom, own_sum), HOME_TURNED)
    own_sum = settle(flags, 1, [home], own_sum)
    (own_sum,) = pair(4, [own], turned, constants, sum_a=own_sum, in_place=True)
    return settle(flags, 2, [top, bottom], own_sum)[None]


def any_bands(orbitals, constants):
    own = orbitals[0]
    flags = jnp.ones((4,), jnp.int32)
    lower = from_behind(orbitals, "band", OFFSET)[0]
    upper = from_behind(orbitals, "band", -OFFSET)[0]
    (total,) = pair_terms(flags, 0, [own], lower, constants)
    return pair_terms(flags, 1, [own], upper, constants, sum_a=total)[0][None]


def local(bands, orbitals):
    points = orbitals.shape[1]
    constants = (screened_kernel(points), *hartley_tables(points))
    if bands == 16:
        return sixteen_bands(orbitals, constants)
    return any_bands(orbitals, constants)


def solution(mesh):
    return jax.shard_map(
        functools.partial(local, mesh.shape["band"]),
        mesh=mesh,
        in_specs=(P(("groups", "band"), None, None),),
        out_specs=P(("groups", "band"), None, None),
        check_vma=False,
    )
```

```python
import functools
import math

import jax
import jax.numpy as jnp
import numpy as np
from jax import lax
from jax.experimental import pallas as pl
from jax.experimental.pallas import tpu as pltpu
from jax.sharding import PartitionSpec as P

OFFSET = 5
screening = 5.44
LANES = 128
X_STEPS = 3
PLANE_STEPS = 2
SETTLE_STEPS = 6
FAR_ROWS = 32


def from_behind(value, axis, by):
    count = lax.axis_size(axis)
    return lax.ppermute(value, axis, [(i, (i + by) % count) for i in range(count)])


def screened_kernel(points):
    signed = jnp.arange(LANES, dtype=jnp.int32)
    inside = signed < points
    signed = jnp.where(signed >= points // 2, signed - points, signed)
    wavenumber = signed.astype(jnp.float32) * (2.0 * math.pi / points)
    squared = (
        wavenumber[:points, None, None] ** 2
        + wavenumber[None, :points, None] ** 2
        + wavenumber[None, None, :] ** 2
    )
    screen_rate = screening / points
    finite = jnp.where(squared > 0.0, squared, 1.0)
    screened = 4.0 * math.pi / finite * -jnp.expm1(-finite / (4.0 * screen_rate * screen_rate))
    kernel = jnp.where(squared > 0.0, screened, math.pi / (screen_rate * screen_rate))
    return jnp.where(inside, kernel / -float(points * points * points), 0.0)


def hartley_tables(points):
    counter = np.arange(points)
    angles = 2.0 * np.pi * (counter[:, None] * counter[None, :] % points) / points
    table = np.cos(angles) + np.sin(angles)
    high = table.astype(jnp.bfloat16)
    low = (table - high.astype(np.float64)).astype(jnp.bfloat16)
    left = np.zeros((2 * points, 2 * points), jnp.bfloat16)
    left[:points, :points] = high
    left[:points, points:] = high
    left[points:, :points] = low
    right = np.zeros((2 * LANES, 2 * LANES), jnp.bfloat16)
    right[:points, :points] = high
    right[:points, LANES:LANES + points] = low
    right[LANES:LANES + points, :points] = high
    return jnp.asarray(left), jnp.asarray(right)


def two_terms(value):
    high = value.astype(jnp.bfloat16)
    low = (value - high.astype(jnp.float32)).astype(jnp.bfloat16)
    return high, low


def from_left(left, value):
    half = value.shape[0]
    terms = jnp.concatenate(two_terms(value), 0)
    out = jnp.dot(left, terms, preferred_element_type=jnp.float32)
    return out[:half] + out[half:]


def from_right(value, right):
    out = jnp.dot(jnp.concatenate(two_terms(value), 1), right, preferred_element_type=jnp.float32)
    return out[:, :LANES] + out[:, LANES:]


def pair_body(points, slot, jobs, has, *refs):
    refs = list(refs)
    flags_ref = refs.pop(0)
    a_names = ["a%d" % job for job in range(jobs)]
    names = a_names + ["b"] + ["sum_a"] * ("sum_a" in has)
    far = {name: refs.pop(0) for name in names}
    if "then" in has:
        refs.pop(0)
    kernel_ref, left_ref, right_ref = refs.pop(0), refs.pop(0), refs.pop(0)
    outs = ["for_a%d" % job for job in range(jobs)]
    if "halves" in has:
        outs.append("low_a0")
    if "for_b" in has:
        outs.append("for_b")
    out_refs = {name: refs.pop(0) for name in outs}
    held, near, near_kernel, near_out, sems, kernel_sems, out_sems = refs
    step = pl.program_id(0)
    active = flags_ref[2 * slot] == 1
    with_sum = flags_ref[2 * slot + 1] == 1
    columns = near.shape[2] // X_STEPS
    ys = columns // points
    per_step = points // PLANE_STEPS
    late = X_STEPS + PLANE_STEPS
    steps = late + X_STEPS
    job = step // steps if jobs > 1 else 0
    at = step % steps if jobs > 1 else step

    def span_of(chunk):
        start = chunk * columns
        return pl.ds(start if isinstance(chunk, int) else pl.multiple_of(start, columns), columns)

    def fetch(name, chunk):
        place, span = names.index(name), span_of(chunk)
        return pltpu.make_async_copy(
            far[name].at[:, span], near.at[place, :, span], sems.at[place, chunk]
        )

    def fetch_kernel(part):
        span = pl.ds(part * per_step, per_step)
        return pltpu.make_async_copy(
            kernel_ref.at[span], near_kernel.at[span], kernel_sems.at[part]
        )

    def give(name, chunk):
        span = span_of(chunk)
        source = near_out.at[jobs if name == "for_b" else int(name[-1])]
        if "halves" in has and name != "for_b":
            rows = pl.ds(points - FAR_ROWS, FAR_ROWS) if name == "low_a0" else pl.ds(0, points - FAR_ROWS)
            source = source.at[rows, span]
        else:
            source = source.at[:, span]
        return pltpu.make_async_copy(
            source, out_refs[name].at[:, span], out_sems.at[outs.index(name), chunk]
        )

    def here(name, chunk):
        place = job if name == "a" else names.index(name)
        return near[place, :, span_of(chunk)]

    def when_job(number, work):
        if jobs > 1:
            pl.when(job == number)(work)
        elif number == 0:
            work()

    @pl.when(active & (step == 0))
    def start_first():
        for chunk in range(2):
            for name in ("a0", "b"):
                fetch(name, chunk).start()

    @pl.when(active & (step + 2 < X_STEPS))
    def start_next():
        for name in ("a0", "b"):
            fetch(name, step + 2).start()

    @pl.when(active & (step == X_STEPS - 2))
    def start_kernel():
        for part in range(PLANE_STEPS):
            fetch_kernel(part).start()

    @pl.when(active & (step == X_STEPS))
    def start_rest():
        for chunk in range(X_STEPS):
            for name in a_names[1:] + ["sum_a"] * ("sum_a" in has):
                fetch(name, chunk).start()

    def lanes_apart(block):
        tail = jnp.zeros((points, LANES), jnp.float32)
        wide = jnp.concatenate([block, tail], 1)
        rows = [wide[:, q * points:q * points + LANES] for q in range(ys)]
        return jnp.swapaxes(jnp.stack(rows, 0), 0, 1)

    def lanes_together(block):
        block = jnp.swapaxes(block, 0, 1)
        return jnp.concatenate([block[q][:, :points] for q in range(ys)], 1)

    def side_by_side(block):
        return jnp.concatenate([block[i] for i in range(per_step)], 1)

    @pl.when(active & (at < X_STEPS))
    def forward_x():
        chunk = at

        def first_waits():
            fetch("a0", chunk).wait()
            fetch("b", chunk).wait()

        when_job(0, first_waits)
        for number in range(1, jobs):
            when_job(number, fetch(a_names[number], chunk).wait)
        spectrum = from_left(left_ref[...], here("a", chunk) * here("b", chunk))
        start = pl.multiple_of(chunk * ys, ys)
        held[:, pl.ds(start, ys), :] = lanes_apart(spectrum)

    @pl.when(active & (at >= X_STEPS) & (at < late))
    def planes():
        part = at - X_STEPS
        left = left_ref[...]
        right = right_ref[...]
        first = part * per_step
        when_job(0, lambda: fetch_kernel(part).wait())
        block = held[pl.ds(first, per_step)].reshape(per_step * points, LANES)
        block = from_right(block, right).reshape(per_step, points, LANES)
        wide = from_left(left, side_by_side(block))
        wide = from_left(left, wide * side_by_side(near_kernel[pl.ds(first, per_step)]))
        block = jnp.concatenate(
            [wide[:, i * LANES:(i + 1) * LANES] for i in range(per_step)], 0
        )
        block = from_right(block, right)
        held[pl.ds(first, per_step)] = block.reshape(per_step, points, LANES)

    @pl.when(active & (at >= late))
    def inverse_x():
        chunk = at - late
        start = pl.multiple_of(chunk * ys, ys)
        if "sum_a" in has:
            fetch("sum_a", chunk).wait()
        block = lanes_together(held[:, pl.ds(start, ys), :])
        potential = from_left(left_ref[...], block)
        for_a = here("b", chunk) * potential
        if "sum_a" in has:
            for_a = for_a + jnp.where(with_sum, here("sum_a", chunk), 0.0)
        near_out[job, :, span_of(chunk)] = for_a
        if "for_b" in has:
            for_b = here("a", chunk) * potential
            if jobs > 1:
                for_b = for_b + jnp.where(job > 0, near_out[jobs, :, span_of(chunk)], 0.0)
            near_out[jobs, :, span_of(chunk)] = for_b

        def give_all(number):
            for name in outs:
                if number == (jobs - 1 if name == "for_b" else int(name[-1])):
                    give(name, chunk).start()

        for number in range(jobs):
            when_job(number, functools.partial(give_all, number))

    @pl.when(active & (step == jobs * steps - 1))
    def wait_outs():
        for chunk in range(X_STEPS):
            for name in outs:
                give(name, chunk).wait()


def pair_terms(
    flags, slot, a, b, constants, sum_a=None, for_b=False, halves=False, in_place=False, then=None
):
    points, plane = b.shape
    kernel, left, right = constants
    jobs = len(a)
    blocks = [*a, b] + [sum_a] * (sum_a is not None)
    waited = [] if then is None else [then]
    has = ["sum_a"] * (sum_a is not None) + ["for_b"] * for_b + ["halves"] * halves + ["then"] * len(waited)
    rows = ([points - FAR_ROWS, FAR_ROWS] if halves else [points] * jobs) + [points] * for_b
    anywhere = pl.BlockSpec(memory_space=pl.ANY)
    return pl.pallas_call(
        functools.partial(pair_body, points, slot, jobs, has),
        grid=(jobs * (2 * X_STEPS + PLANE_STEPS),),
        in_specs=[pl.BlockSpec(memory_space=pltpu.SMEM)]
        + [anywhere] * (len(blocks) + len(waited) + 1)
        + [pl.BlockSpec(table.shape, lambda i: (0, 0)) for table in (left, right)],
        out_specs=[anywhere] * len(rows),
        out_shape=[jax.ShapeDtypeStruct((n, plane), jnp.float32) for n in rows],
        input_output_aliases={3: 0} if in_place else {},
        scratch_shapes=[
            pltpu.VMEM((points, points, LANES), jnp.float32),
            pltpu.VMEM((len(blocks), points, plane), jnp.float32),
            pltpu.VMEM((points, points, LANES), jnp.float32),
            pltpu.VMEM((jobs + for_b, points, plane), jnp.float32),
            pltpu.SemaphoreType.DMA((len(blocks), X_STEPS)),
            pltpu.SemaphoreType.DMA((PLANE_STEPS,)),
            pltpu.SemaphoreType.DMA((len(rows), X_STEPS)),
        ],
        compiler_params=pltpu.CompilerParams(vmem_limit_bytes=63 * 2**20),
        cost_estimate=pl.CostEstimate(
            flops=100_000_000, bytes_accessed=1_000_000, transcendentals=0
        ),
        name="pair_terms",
    )(flags, *blocks, *waited, kernel, left, right)


def copy_body(flags_ref, kernel_ref, left_ref, right_ref, block_ref, first_ref, second_ref):
    del flags_ref, kernel_ref, left_ref, right_ref
    first_ref[...] = block_ref[...]
    second_ref[...] = block_ref[...]


def copied(flags, constants, block):
    points, plane = block.shape
    part = pl.BlockSpec((points, plane // X_STEPS), lambda i: (0, i))
    return pl.pallas_call(
        copy_body,
        grid=(X_STEPS,),
        in_specs=[
            pl.BlockSpec(memory_space=pltpu.SMEM),
            *[pl.BlockSpec(memory_space=pl.ANY)] * 3,
            part,
        ],
        out_specs=[part, part],
        out_shape=[jax.ShapeDtypeStruct(block.shape, block.dtype)] * 2,
        compiler_params=pltpu.CompilerParams(vmem_limit_bytes=63 * 2**20),
        name="copied",
    )(flags, *constants, block)


def gate_body(*refs):
    del refs


def gate(token, kernel, partner, block):
    anywhere = pl.BlockSpec(memory_space=pl.ANY)
    return pl.pallas_call(
        gate_body,
        in_specs=[anywhere] * 4,
        out_specs=[anywhere] * 2,
        out_shape=[
            jax.ShapeDtypeStruct(kernel.shape, kernel.dtype),
            jax.ShapeDtypeStruct(block.shape, block.dtype),
        ],
        input_output_aliases={1: 0, 3: 1},
        compiler_params=pltpu.CompilerParams(vmem_limit_bytes=63 * 2**20),
        name="gate",
    )(token, kernel, partner, block)


def hold_body(*refs):
    del refs


def hold(block, *then):
    anywhere = pl.BlockSpec(memory_space=pl.ANY)
    return pl.pallas_call(
        hold_body,
        in_specs=[anywhere] * (1 + len(then)),
        out_specs=anywhere,
        out_shape=jax.ShapeDtypeStruct(block.shape, block.dtype),
        input_output_aliases={0: 0},
        compiler_params=pltpu.CompilerParams(vmem_limit_bytes=63 * 2**20),
        name="hold",
    )(block, *then)


def settle_body(wanted, count, flags_ref, *refs):
    parts, (out_ref, near, sems) = refs[:count], refs[count + 1:]
    columns = out_ref.shape[1] // SETTLE_STEPS

    @pl.when(flags_ref[RESULT] == wanted)
    def move():
        copies = []
        for i in range(SETTLE_STEPS):
            span = pl.ds(i * columns, columns)
            start = 0
            for j, part in enumerate(parts):
                rows = pl.ds(start, part.shape[0])
                start += part.shape[0]
                copies.append((
                    pltpu.make_async_copy(part.at[:, span], near.at[rows, span], sems.at[0, j, i]),
                    pltpu.make_async_copy(near.at[rows, span], out_ref.at[rows, span], sems.at[1, j, i]),
                ))
        for inward, outward in copies:
            inward.start()
        for inward, outward in copies:
            inward.wait()
            outward.start()
        for inward, outward in copies:
            outward.wait()


def settle(flags, wanted, parts, own_sum):
    anywhere = pl.BlockSpec(memory_space=pl.ANY)
    count = len(parts)
    return pl.pallas_call(
        functools.partial(settle_body, wanted, count),
        in_specs=[pl.BlockSpec(memory_space=pltpu.SMEM)] + [anywhere] * (count + 1),
        out_specs=anywhere,
        out_shape=jax.ShapeDtypeStruct(own_sum.shape, own_sum.dtype),
        input_output_aliases={count + 1: 0},
        scratch_shapes=[
            pltpu.VMEM(own_sum.shape, own_sum.dtype),
            pltpu.SemaphoreType.DMA((2, count, SETTLE_STEPS)),
        ],
        compiler_params=pltpu.CompilerParams(vmem_limit_bytes=63 * 2**20),
        name="settle",
    )(flags, *parts, own_sum)


def both_halves(*pairs):
    return list(pairs) + [(15 - source, 15 - target) for source, target in pairs]


CROSSING = both_halves((3, 14), (4, 9))
PARTNERS = both_halves((8, 14), (15, 9), (9, 11), (14, 12))
ARRIVED = both_halves((14, 2), (9, 5))
SINGLES = both_halves((5, 10), (2, 13))
BESIDE = both_halves((13, 14), (10, 9))
DIRECT = both_halves((15, 10), (8, 13))
TURNED = both_halves((11, 14), (12, 9))
HOME_ACROSS = both_halves((9, 4), (14, 3))
HOME_FAR = both_halves((9, 15), (14, 8))
HOME_TURN = both_halves((9, 11), (14, 12))
HOME_TURNED = both_halves((11, 15), (12, 8))
RESULT = 10
FLAGS = {i: (1, 0, 1, 1, 0, 0, 0, 0, 1, 1, 0) for i in (9, 14, 6, 1)}
FLAGS.update({i: (0, 0, 0, 0, 1, 0, 1, 1, 0, 0, 0) for i in (10, 13, 5, 2)})
FLAGS.update({i: (0,) * RESULT + (1,) for i in (3, 4, 11, 12)})
FLAGS.update({i: (0,) * RESULT + (2,) for i in (15, 8, 0, 7)})


def sixteen_bands(orbitals, constants):
    def send(value, pairs):
        return lax.ppermute(value[None], "band", pairs)[0]

    kernel, left, right = constants
    own = orbitals[0]
    flags = jnp.asarray([FLAGS[i] for i in range(16)], jnp.int32)
    flags = flags[lax.axis_index("band")]
    pair = functools.partial(pair_terms, flags)
    crossed = send(own, CROSSING)
    partner = send(own, PARTNERS)
    own_copy, direct_copy = copied(flags, constants, own)
    token = crossed[:8, :LANES] + own_copy[:8, :LANES]
    direct_copy = hold(direct_copy, partner)
    direct = send(direct_copy, DIRECT)
    kernel, held_back = gate(send(token, ARRIVED), kernel, direct_copy, own_copy)
    constants = (kernel, left, right)
    beside = send(held_back, BESIDE)
    single = send(held_back, SINGLES)

    partner_sum, own_sum, crossed_sum = pair(
        0, [partner, own], crossed, constants, for_b=True
    )
    home = send(crossed_sum, HOME_ACROSS)
    partner = hold(partner, own_sum)
    turned = send(partner, TURNED)
    top, bottom = pair(1, [partner], beside, constants, sum_a=partner_sum, halves=True, then=direct)
    bottom = send(bottom, HOME_TURN)
    top = send(top, HOME_FAR)
    (own_sum,) = pair(2, [own], direct, constants, sum_a=own_sum, in_place=True)
    (own_sum,) = pair(3, [own], single, constants, sum_a=own_sum, in_place=True)
    bottom = send(hold(bottom, own_sum), HOME_TURNED)
    own_sum = settle(flags, 1, [home], own_sum)
    (own_sum,) = pair(4, [own], turned, constants, sum_a=own_sum, in_place=True)
    return settle(flags, 2, [top, bottom], own_sum)[None]


def any_bands(orbitals, constants):
    own = orbitals[0]
    flags = jnp.ones((4,), jnp.int32)
    lower = from_behind(orbitals, "band", OFFSET)[0]
    upper = from_behind(orbitals, "band", -OFFSET)[0]
    (total,) = pair_terms(flags, 0, [own], lower, constants)
    return pair_terms(flags, 1, [own], upper, constants, sum_a=total)[0][None]


def local(bands, orbitals):
    points = orbitals.shape[1]
    constants = (screened_kernel(points), *hartley_tables(points))
    if bands == 16:
        return sixteen_bands(orbitals, constants)
    return any_bands(orbitals, constants)


def solution(mesh):
    return jax.shard_map(
        functools.partial(local, mesh.shape["band"]),
        mesh=mesh,
        in_specs=(P(("groups", "band"), None, None),),
        out_specs=P(("groups", "band"), None, None),
        check_vma=False,
    )
```

```python
import functools
import math

import jax
import jax.numpy as jnp
import numpy as np
from jax import lax
from jax.experimental import pallas as pl
from jax.experimental.pallas import tpu as pltpu
from jax.sharding import PartitionSpec as P

OFFSET = 5
screening = 5.44
LANES = 128
X_STEPS = 3
SETTLE_STEPS = 6
FAR_ROWS = 32


def from_behind(value, axis, by):
    count = lax.axis_size(axis)
    return lax.ppermute(value, axis, [(i, (i + by) % count) for i in range(count)])


def screened_kernel(points):
    signed = jnp.arange(LANES, dtype=jnp.int32)
    inside = signed < points
    signed = jnp.where(signed >= points // 2, signed - points, signed)
    wavenumber = signed.astype(jnp.float32) * (2.0 * math.pi / points)
    squared = (
        wavenumber[:points, None, None] ** 2
        + wavenumber[None, :points, None] ** 2
        + wavenumber[None, None, :] ** 2
    )
    screen_rate = screening / points
    finite = jnp.where(squared > 0.0, squared, 1.0)
    screened = 4.0 * math.pi / finite * -jnp.expm1(-finite / (4.0 * screen_rate * screen_rate))
    kernel = jnp.where(squared > 0.0, screened, math.pi / (screen_rate * screen_rate))
    return jnp.where(inside, kernel / -float(points * points * points), 0.0)


def hartley_tables(points):
    counter = np.arange(points)
    angles = 2.0 * np.pi * (counter[:, None] * counter[None, :] % points) / points
    table = np.cos(angles) + np.sin(angles)
    high = table.astype(jnp.bfloat16)
    low = (table - high.astype(np.float64)).astype(jnp.bfloat16)
    left = np.zeros((2 * points, 2 * points), jnp.bfloat16)
    left[:points, :points] = high
    left[:points, points:] = high
    left[points:, :points] = low
    right = np.zeros((2 * LANES, 2 * LANES), jnp.bfloat16)
    right[:points, :points] = high
    right[:points, LANES:LANES + points] = low
    right[LANES:LANES + points, :points] = high
    return jnp.asarray(left), jnp.asarray(right)


def two_terms(value):
    high = value.astype(jnp.bfloat16)
    low = (value - high.astype(jnp.float32)).astype(jnp.bfloat16)
    return high, low


def from_left(left, value):
    half = value.shape[0]
    terms = jnp.concatenate(two_terms(value), 0)
    out = jnp.dot(left, terms, preferred_element_type=jnp.float32)
    return out[:half] + out[half:]


def from_right(value, right):
    out = jnp.dot(jnp.concatenate(two_terms(value), 1), right, preferred_element_type=jnp.float32)
    return out[:, :LANES] + out[:, LANES:]


def pair_body(points, slot, jobs, plane_steps, has, *refs):
    refs = list(refs)
    flags_ref = refs.pop(0)
    a_names = ["a%d" % job for job in range(jobs)]
    names = a_names + ["b"] + ["sum_a"] * ("sum_a" in has)
    far = {name: refs.pop(0) for name in names}
    if "then" in has:
        refs.pop(0)
    kernel_ref, left_ref, right_ref = refs.pop(0), refs.pop(0), refs.pop(0)
    outs = ["for_a%d" % job for job in range(jobs)]
    if "halves" in has:
        outs.append("low_a0")
    if "for_b" in has:
        outs.append("for_b")
    out_refs = {name: refs.pop(0) for name in outs}
    held, near, near_kernel, near_out, sems, kernel_sems, out_sems = refs
    step = pl.program_id(0)
    active = flags_ref[2 * slot] == 1
    with_sum = flags_ref[2 * slot + 1] == 1
    columns = near.shape[2] // X_STEPS
    ys = columns // points
    per_step = points // plane_steps
    late = X_STEPS + plane_steps
    steps = late + X_STEPS
    job = step // steps if jobs > 1 else 0
    at = step % steps if jobs > 1 else step

    def span_of(chunk):
        start = chunk * columns
        return pl.ds(start if isinstance(chunk, int) else pl.multiple_of(start, columns), columns)

    def fetch(name, chunk):
        place, span = names.index(name), span_of(chunk)
        return pltpu.make_async_copy(
            far[name].at[:, span], near.at[place, :, span], sems.at[place, chunk]
        )

    def fetch_kernel(part):
        span = pl.ds(part * per_step, per_step)
        return pltpu.make_async_copy(
            kernel_ref.at[span], near_kernel.at[span], kernel_sems.at[part]
        )

    def give(name, chunk):
        span = span_of(chunk)
        source = near_out.at[jobs if name == "for_b" else int(name[-1])]
        if "halves" in has and name != "for_b":
            rows = pl.ds(points - FAR_ROWS, FAR_ROWS) if name == "low_a0" else pl.ds(0, points - FAR_ROWS)
            source = source.at[rows, span]
        else:
            source = source.at[:, span]
        return pltpu.make_async_copy(
            source, out_refs[name].at[:, span], out_sems.at[outs.index(name), chunk]
        )

    def here(name, chunk):
        place = job if name == "a" else names.index(name)
        return near[place, :, span_of(chunk)]

    def when_job(number, work):
        if jobs > 1:
            pl.when(job == number)(work)
        elif number == 0:
            work()

    @pl.when(active & (step == 0))
    def start_first():
        for chunk in range(2):
            for name in ("a0", "b"):
                fetch(name, chunk).start()

    @pl.when(active & (step + 2 < X_STEPS))
    def start_next():
        for name in ("a0", "b"):
            fetch(name, step + 2).start()

    @pl.when(active & (step == 0))
    def start_kernel():
        for part in range(plane_steps):
            fetch_kernel(part).start()

    @pl.when(active & (step == X_STEPS))
    def start_rest():
        for chunk in range(X_STEPS):
            for name in a_names[1:] + ["sum_a"] * ("sum_a" in has):
                fetch(name, chunk).start()

    def lanes_apart(block):
        tail = jnp.zeros((points, LANES), jnp.float32)
        wide = jnp.concatenate([block, tail], 1)
        rows = [wide[:, q * points:q * points + LANES] for q in range(ys)]
        return jnp.swapaxes(jnp.stack(rows, 0), 0, 1)

    def lanes_together(block):
        block = jnp.swapaxes(block, 0, 1)
        return jnp.concatenate([block[q][:, :points] for q in range(ys)], 1)

    def side_by_side(block):
        return jnp.concatenate([block[i] for i in range(per_step)], 1)

    @pl.when(active & (at < X_STEPS))
    def forward_x():
        chunk = at

        def first_waits():
            fetch("a0", chunk).wait()
            fetch("b", chunk).wait()

        when_job(0, first_waits)
        for number in range(1, jobs):
            when_job(number, fetch(a_names[number], chunk).wait)
        spectrum = from_left(left_ref[...], here("a", chunk) * here("b", chunk))
        start = pl.multiple_of(chunk * ys, ys)
        held[:, pl.ds(start, ys), :] = lanes_apart(spectrum)

    @pl.when(active & (at >= X_STEPS) & (at < late))
    def planes():
        part = at - X_STEPS
        left = left_ref[...]
        right = right_ref[...]
        first = part * per_step
        when_job(0, lambda: fetch_kernel(part).wait())
        block = held[pl.ds(first, per_step)].reshape(per_step * points, LANES)
        block = from_right(block, right).reshape(per_step, points, LANES)
        wide = from_left(left, side_by_side(block))
        wide = from_left(left, wide * side_by_side(near_kernel[pl.ds(first, per_step)]))
        block = jnp.concatenate(
            [wide[:, i * LANES:(i + 1) * LANES] for i in range(per_step)], 0
        )
        block = from_right(block, right)
        held[pl.ds(first, per_step)] = block.reshape(per_step, points, LANES)

    @pl.when(active & (at >= late))
    def inverse_x():
        chunk = at - late
        start = pl.multiple_of(chunk * ys, ys)
        if "sum_a" in has:
            fetch("sum_a", chunk).wait()
        block = lanes_together(held[:, pl.ds(start, ys), :])
        potential = from_left(left_ref[...], block)
        for_a = here("b", chunk) * potential
        if "sum_a" in has:
            for_a = for_a + jnp.where(with_sum, here("sum_a", chunk), 0.0)
        near_out[job, :, span_of(chunk)] = for_a
        if "for_b" in has:
            for_b = here("a", chunk) * potential
            if jobs > 1:
                for_b = for_b + jnp.where(job > 0, near_out[jobs, :, span_of(chunk)], 0.0)
            near_out[jobs, :, span_of(chunk)] = for_b

        def give_all(number):
            for name in outs:
                if number == (jobs - 1 if name == "for_b" else int(name[-1])):
                    give(name, chunk).start()

        for number in range(jobs):
            when_job(number, functools.partial(give_all, number))

    @pl.when(active & (step == jobs * steps - 1))
    def wait_outs():
        for chunk in range(X_STEPS):
            for name in outs:
                give(name, chunk).wait()


def pair_terms(
    flags, slot, a, b, constants, sum_a=None, for_b=False, halves=False, in_place=False, then=None,
    plane_steps=2,
):
    points, plane = b.shape
    kernel, left, right = constants
    jobs = len(a)
    blocks = [*a, b] + [sum_a] * (sum_a is not None)
    waited = [] if then is None else [then]
    has = ["sum_a"] * (sum_a is not None) + ["for_b"] * for_b + ["halves"] * halves + ["then"] * len(waited)
    rows = ([points - FAR_ROWS, FAR_ROWS] if halves else [points] * jobs) + [points] * for_b
    anywhere = pl.BlockSpec(memory_space=pl.ANY)
    return pl.pallas_call(
        functools.partial(pair_body, points, slot, jobs, plane_steps, has),
        grid=(jobs * (2 * X_STEPS + plane_steps),),
        in_specs=[pl.BlockSpec(memory_space=pltpu.SMEM)]
        + [anywhere] * (len(blocks) + len(waited) + 1)
        + [pl.BlockSpec(table.shape, lambda i: (0, 0)) for table in (left, right)],
        out_specs=[anywhere] * len(rows),
        out_shape=[jax.ShapeDtypeStruct((n, plane), jnp.float32) for n in rows],
        input_output_aliases={3: 0} if in_place else {},
        scratch_shapes=[
            pltpu.VMEM((points, points, LANES), jnp.float32),
            pltpu.VMEM((len(blocks), points, plane), jnp.float32),
            pltpu.VMEM((points, points, LANES), jnp.float32),
            pltpu.VMEM((jobs + for_b, points, plane), jnp.float32),
            pltpu.SemaphoreType.DMA((len(blocks), X_STEPS)),
            pltpu.SemaphoreType.DMA((plane_steps,)),
            pltpu.SemaphoreType.DMA((len(rows), X_STEPS)),
        ],
        compiler_params=pltpu.CompilerParams(vmem_limit_bytes=63 * 2**20),
        cost_estimate=pl.CostEstimate(
            flops=100_000_000, bytes_accessed=1_000_000, transcendentals=0
        ),
        name="pair_terms",
    )(flags, *blocks, *waited, kernel, left, right)


def copy_body(flags_ref, kernel_ref, left_ref, right_ref, block_ref, first_ref, second_ref):
    del flags_ref, kernel_ref, left_ref, right_ref
    first_ref[...] = block_ref[...]
    second_ref[...] = block_ref[...]


def copied(flags, constants, block):
    points, plane = block.shape
    part = pl.BlockSpec((points, plane // X_STEPS), lambda i: (0, i))
    return pl.pallas_call(
        copy_body,
        grid=(X_STEPS,),
        in_specs=[
            pl.BlockSpec(memory_space=pltpu.SMEM),
            *[pl.BlockSpec(memory_space=pl.ANY)] * 3,
            part,
        ],
        out_specs=[part, part],
        out_shape=[jax.ShapeDtypeStruct(block.shape, block.dtype)] * 2,
        compiler_params=pltpu.CompilerParams(vmem_limit_bytes=63 * 2**20),
        name="copied",
    )(flags, *constants, block)


def gate_body(*refs):
    del refs


def gate(token, kernel, partner, block):
    anywhere = pl.BlockSpec(memory_space=pl.ANY)
    return pl.pallas_call(
        gate_body,
        in_specs=[anywhere] * 4,
        out_specs=[anywhere] * 2,
        out_shape=[
            jax.ShapeDtypeStruct(kernel.shape, kernel.dtype),
            jax.ShapeDtypeStruct(block.shape, block.dtype),
        ],
        input_output_aliases={1: 0, 3: 1},
        compiler_params=pltpu.CompilerParams(vmem_limit_bytes=63 * 2**20),
        name="gate",
    )(token, kernel, partner, block)


def hold_body(*refs):
    del refs


def hold(block, *then):
    anywhere = pl.BlockSpec(memory_space=pl.ANY)
    return pl.pallas_call(
        hold_body,
        in_specs=[anywhere] * (1 + len(then)),
        out_specs=anywhere,
        out_shape=jax.ShapeDtypeStruct(block.shape, block.dtype),
        input_output_aliases={0: 0},
        compiler_params=pltpu.CompilerParams(vmem_limit_bytes=63 * 2**20),
        name="hold",
    )(block, *then)


def settle_body(wanted, count, flags_ref, *refs):
    parts, (out_ref, near, sems) = refs[:count], refs[count + 1:]
    columns = out_ref.shape[1] // SETTLE_STEPS

    @pl.when(flags_ref[RESULT] == wanted)
    def move():
        copies = []
        for i in range(SETTLE_STEPS):
            span = pl.ds(i * columns, columns)
            start = 0
            for j, part in enumerate(parts):
                rows = pl.ds(start, part.shape[0])
                start += part.shape[0]
                copies.append((
                    pltpu.make_async_copy(part.at[:, span], near.at[rows, span], sems.at[0, j, i]),
                    pltpu.make_async_copy(near.at[rows, span], out_ref.at[rows, span], sems.at[1, j, i]),
                ))
        for inward, outward in copies:
            inward.start()
        for inward, outward in copies:
            inward.wait()
            outward.start()
        for inward, outward in copies:
            outward.wait()


def settle(flags, wanted, parts, own_sum):
    anywhere = pl.BlockSpec(memory_space=pl.ANY)
    count = len(parts)
    return pl.pallas_call(
        functools.partial(settle_body, wanted, count),
        in_specs=[pl.BlockSpec(memory_space=pltpu.SMEM)] + [anywhere] * (count + 1),
        out_specs=anywhere,
        out_shape=jax.ShapeDtypeStruct(own_sum.shape, own_sum.dtype),
        input_output_aliases={count + 1: 0},
        scratch_shapes=[
            pltpu.VMEM(own_sum.shape, own_sum.dtype),
            pltpu.SemaphoreType.DMA((2, count, SETTLE_STEPS)),
        ],
        compiler_params=pltpu.CompilerParams(vmem_limit_bytes=63 * 2**20),
        name="settle",
    )(flags, *parts, own_sum)


def both_halves(*pairs):
    return list(pairs) + [(15 - source, 15 - target) for source, target in pairs]


CROSSING = both_halves((3, 14), (4, 9))
PARTNERS = both_halves((8, 14), (15, 9), (9, 11), (14, 12))
ARRIVED = both_halves((14, 2), (9, 5))
SINGLES = both_halves((5, 10), (2, 13))
BESIDE = both_halves((13, 14), (10, 9))
DIRECT = both_halves((15, 10), (8, 13))
TURNED = both_halves((11, 14), (12, 9))
HOME_ACROSS = both_halves((9, 4), (14, 3))
HOME_FAR = both_halves((9, 15), (14, 8))
HOME_TURN = both_halves((9, 11), (14, 12))
HOME_TURNED = both_halves((11, 15), (12, 8))
RESULT = 10
FLAGS = {i: (1, 0, 1, 1, 0, 0, 0, 0, 1, 1, 0) for i in (9, 14, 6, 1)}
FLAGS.update({i: (0, 0, 0, 0, 1, 0, 1, 1, 0, 0, 0) for i in (10, 13, 5, 2)})
FLAGS.update({i: (0,) * RESULT + (1,) for i in (3, 4, 11, 12)})
FLAGS.update({i: (0,) * RESULT + (2,) for i in (15, 8, 0, 7)})


def sixteen_bands(orbitals, constants):
    def send(value, pairs):
        return lax.ppermute(value[None], "band", pairs)[0]

    kernel, left, right = constants
    own = orbitals[0]
    flags = jnp.asarray([FLAGS[i] for i in range(16)], jnp.int32)
    flags = flags[lax.axis_index("band")]
    pair = functools.partial(pair_terms, flags)
    crossed = send(own, CROSSING)
    partner = send(own, PARTNERS)
    own_copy, direct_copy = copied(flags, constants, own)
    token = crossed[:8, :LANES] + own_copy[:8, :LANES]
    direct_copy = hold(direct_copy, partner)
    direct = send(direct_copy, DIRECT)
    kernel, held_back = gate(send(token, ARRIVED), kernel, direct_copy, own_copy)
    constants = (kernel, left, right)
    beside = send(held_back, BESIDE)
    single = send(held_back, SINGLES)

    partner_sum, own_sum, crossed_sum = pair(
        0, [partner, own], crossed, constants, for_b=True, plane_steps=1
    )
    home = send(crossed_sum, HOME_ACROSS)
    partner = hold(partner, own_sum)
    turned = send(partner, TURNED)
    top, bottom = pair(1, [partner], beside, constants, sum_a=partner_sum, halves=True, then=direct, plane_steps=1)
    bottom = send(bottom, HOME_TURN)
    top = send(top, HOME_FAR)
    (own_sum,) = pair(2, [own], direct, constants, sum_a=own_sum, in_place=True)
    (own_sum,) = pair(3, [own], single, constants, sum_a=own_sum, in_place=True)
    bottom = send(hold(bottom, own_sum), HOME_TURNED)
    own_sum = settle(flags, 1, [home], own_sum)
    (own_sum,) = pair(4, [own], turned, constants, sum_a=own_sum, in_place=True)
    return settle(flags, 2, [top, bottom], own_sum)[None]


def any_bands(orbitals, constants):
    own = orbitals[0]
    flags = jnp.ones((4,), jnp.int32)
    lower = from_behind(orbitals, "band", OFFSET)[0]
    upper = from_behind(orbitals, "band", -OFFSET)[0]
    (total,) = pair_terms(flags, 0, [own], lower, constants)
    return pair_terms(flags, 1, [own], upper, constants, sum_a=total)[0][None]


def local(bands, orbitals):
    points = orbitals.shape[1]
    constants = (screened_kernel(points), *hartley_tables(points))
    if bands == 16:
        return sixteen_bands(orbitals, constants)
    return any_bands(orbitals, constants)


def solution(mesh):
    return jax.shard_map(
        functools.partial(local, mesh.shape["band"]),
        mesh=mesh,
        in_specs=(P(("groups", "band"), None, None),),
        out_specs=P(("groups", "band"), None, None),
        check_vma=False,
    )
```

```python
import functools
import math

import jax
import jax.numpy as jnp
import numpy as np
from jax import lax
from jax.experimental import pallas as pl
from jax.experimental.pallas import tpu as pltpu
from jax.sharding import PartitionSpec as P

OFFSET = 5
screening = 5.44
LANES = 128
X_STEPS = 3
SETTLE_STEPS = 6
FAR_ROWS = 32


def from_behind(value, axis, by):
    count = lax.axis_size(axis)
    return lax.ppermute(value, axis, [(i, (i + by) % count) for i in range(count)])


def screened_kernel(points):
    signed = jnp.arange(LANES, dtype=jnp.int32)
    inside = signed < points
    signed = jnp.where(signed >= points // 2, signed - points, signed)
    wavenumber = signed.astype(jnp.float32) * (2.0 * math.pi / points)
    squared = (
        wavenumber[:points, None, None] ** 2
        + wavenumber[None, :points, None] ** 2
        + wavenumber[None, None, :] ** 2
    )
    screen_rate = screening / points
    finite = jnp.where(squared > 0.0, squared, 1.0)
    screened = 4.0 * math.pi / finite * -jnp.expm1(-finite / (4.0 * screen_rate * screen_rate))
    kernel = jnp.where(squared > 0.0, screened, math.pi / (screen_rate * screen_rate))
    return jnp.where(inside, kernel / -float(points * points * points), 0.0)


def hartley_tables(points):
    counter = np.arange(points)
    angles = 2.0 * np.pi * (counter[:, None] * counter[None, :] % points) / points
    table = np.cos(angles) + np.sin(angles)
    high = table.astype(jnp.bfloat16)
    low = (table - high.astype(np.float64)).astype(jnp.bfloat16)
    left = np.zeros((2 * points, 2 * points), jnp.bfloat16)
    left[:points, :points] = high
    left[:points, points:] = high
    left[points:, :points] = low
    right = np.zeros((2 * LANES, 2 * LANES), jnp.bfloat16)
    right[:points, :points] = high
    right[:points, LANES:LANES + points] = low
    right[LANES:LANES + points, :points] = high
    return jnp.asarray(left), jnp.asarray(right)


def two_terms(value):
    high = value.astype(jnp.bfloat16)
    low = (value - high.astype(jnp.float32)).astype(jnp.bfloat16)
    return high, low


def from_left(left, value):
    half = value.shape[0]
    terms = jnp.concatenate(two_terms(value), 0)
    out = jnp.dot(left, terms, preferred_element_type=jnp.float32)
    return out[:half] + out[half:]


def from_right(value, right):
    out = jnp.dot(jnp.concatenate(two_terms(value), 1), right, preferred_element_type=jnp.float32)
    return out[:, :LANES] + out[:, LANES:]


def pair_body(points, slot, jobs, plane_steps, has, *refs):
    refs = list(refs)
    flags_ref = refs.pop(0)
    a_names = ["a%d" % job for job in range(jobs)]
    names = a_names + ["b"] + ["sum_a"] * ("sum_a" in has)
    far = {name: refs.pop(0) for name in names}
    if "then" in has:
        refs.pop(0)
    kernel_ref, left_ref, right_ref = refs.pop(0), refs.pop(0), refs.pop(0)
    outs = ["for_a%d" % job for job in range(jobs)]
    if "halves" in has:
        outs.append("low_a0")
    if "for_b" in has:
        outs.append("for_b")
    out_refs = {name: refs.pop(0) for name in outs}
    held, near, near_kernel, near_out, sems, kernel_sems, out_sems = refs
    step = pl.program_id(0)
    active = flags_ref[2 * slot] == 1
    with_sum = flags_ref[2 * slot + 1] == 1
    columns = near.shape[2] // X_STEPS
    ys = columns // points
    per_step = points // plane_steps
    late = X_STEPS + plane_steps
    steps = late + X_STEPS
    job = step // steps if jobs > 1 else 0
    at = step % steps if jobs > 1 else step

    def span_of(chunk):
        start = chunk * columns
        return pl.ds(start if isinstance(chunk, int) else pl.multiple_of(start, columns), columns)

    def fetch(name, chunk):
        place, span = names.index(name), span_of(chunk)
        return pltpu.make_async_copy(
            far[name].at[:, span], near.at[place, :, span], sems.at[place, chunk]
        )

    def fetch_kernel(part):
        span = pl.ds(part * per_step, per_step)
        return pltpu.make_async_copy(
            kernel_ref.at[span], near_kernel.at[span], kernel_sems.at[part]
        )

    def give(name, chunk):
        span = span_of(chunk)
        source = near_out.at[jobs if name == "for_b" else int(name[-1])]
        if "halves" in has and name != "for_b":
            rows = pl.ds(points - FAR_ROWS, FAR_ROWS) if name == "low_a0" else pl.ds(0, points - FAR_ROWS)
            source = source.at[rows, span]
        else:
            source = source.at[:, span]
        return pltpu.make_async_copy(
            source, out_refs[name].at[:, span], out_sems.at[outs.index(name), chunk]
        )

    def here(name, chunk):
        place = job if name == "a" else names.index(name)
        return near[place, :, span_of(chunk)]

    def when_job(number, work):
        if jobs > 1:
            pl.when(job == number)(work)
        elif number == 0:
            work()

    @pl.when(active & (step == 0))
    def start_first():
        for chunk in range(2):
            for name in ("a0", "b"):
                fetch(name, chunk).start()

    @pl.when(active & (step + 2 < X_STEPS))
    def start_next():
        for name in ("a0", "b"):
            fetch(name, step + 2).start()

    @pl.when(active & (step == 0))
    def start_kernel():
        for part in range(plane_steps):
            fetch_kernel(part).start()

    @pl.when(active & (step == X_STEPS))
    def start_rest():
        for chunk in range(X_STEPS):
            for name in a_names[1:] + ["sum_a"] * ("sum_a" in has):
                fetch(name, chunk).start()

    def put_apart(block, start):
        wide = jnp.concatenate([block, jnp.zeros((points, LANES), jnp.float32)], 1)
        for q in range(ys):
            held[pl.ds(start + q, points, stride=points), :] = wide[:, q * points:q * points + LANES]

    def get_together(start):
        return jnp.concatenate(
            [held[pl.ds(start + q, points, stride=points), :][:, :points] for q in range(ys)], 1
        )

    def side_by_side(block):
        return jnp.concatenate([block[i] for i in range(per_step)], 1)

    @pl.when(active & (at < X_STEPS))
    def forward_x():
        chunk = at

        def first_waits():
            fetch("a0", chunk).wait()
            fetch("b", chunk).wait()

        when_job(0, first_waits)
        for number in range(1, jobs):
            when_job(number, fetch(a_names[number], chunk).wait)
        spectrum = from_left(left_ref[...], here("a", chunk) * here("b", chunk))
        start = pl.multiple_of(chunk * ys, ys)
        put_apart(spectrum, start)

    @pl.when(active & (at >= X_STEPS) & (at < late))
    def planes():
        part = at - X_STEPS
        left = left_ref[...]
        right = right_ref[...]
        first = part * per_step
        when_job(0, lambda: fetch_kernel(part).wait())
        rows = pl.ds(pl.multiple_of(first * points, points), per_step * points)
        block = held[rows, :]
        block = from_right(block, right).reshape(per_step, points, LANES)
        wide = from_left(left, side_by_side(block))
        wide = from_left(left, wide * side_by_side(near_kernel[pl.ds(first, per_step)]))
        block = jnp.concatenate(
            [wide[:, i * LANES:(i + 1) * LANES] for i in range(per_step)], 0
        )
        block = from_right(block, right)
        held[rows, :] = block

    @pl.when(active & (at >= late))
    def inverse_x():
        chunk = at - late
        start = pl.multiple_of(chunk * ys, ys)
        if "sum_a" in has:
            fetch("sum_a", chunk).wait()
        block = get_together(start)
        potential = from_left(left_ref[...], block)
        for_a = here("b", chunk) * potential
        if "sum_a" in has:
            for_a = for_a + jnp.where(with_sum, here("sum_a", chunk), 0.0)
        near_out[job, :, span_of(chunk)] = for_a
        if "for_b" in has:
            for_b = here("a", chunk) * potential
            if jobs > 1:
                for_b = for_b + jnp.where(job > 0, near_out[jobs, :, span_of(chunk)], 0.0)
            near_out[jobs, :, span_of(chunk)] = for_b

        def give_all(number):
            for name in outs:
                if number == (jobs - 1 if name == "for_b" else int(name[-1])):
                    give(name, chunk).start()

        for number in range(jobs):
            when_job(number, functools.partial(give_all, number))

    @pl.when(active & (step == jobs * steps - 1))
    def wait_outs():
        for chunk in range(X_STEPS):
            for name in outs:
                give(name, chunk).wait()


def pair_terms(
    flags, slot, a, b, constants, sum_a=None, for_b=False, halves=False, in_place=False, then=None,
    plane_steps=2,
):
    points, plane = b.shape
    kernel, left, right = constants
    jobs = len(a)
    blocks = [*a, b] + [sum_a] * (sum_a is not None)
    waited = [] if then is None else [then]
    has = ["sum_a"] * (sum_a is not None) + ["for_b"] * for_b + ["halves"] * halves + ["then"] * len(waited)
    rows = ([points - FAR_ROWS, FAR_ROWS] if halves else [points] * jobs) + [points] * for_b
    anywhere = pl.BlockSpec(memory_space=pl.ANY)
    return pl.pallas_call(
        functools.partial(pair_body, points, slot, jobs, plane_steps, has),
        grid=(jobs * (2 * X_STEPS + plane_steps),),
        in_specs=[pl.BlockSpec(memory_space=pltpu.SMEM)]
        + [anywhere] * (len(blocks) + len(waited) + 1)
        + [pl.BlockSpec(table.shape, lambda i: (0, 0)) for table in (left, right)],
        out_specs=[anywhere] * len(rows),
        out_shape=[jax.ShapeDtypeStruct((n, plane), jnp.float32) for n in rows],
        input_output_aliases={3: 0} if in_place else {},
        scratch_shapes=[
            pltpu.VMEM((points * points, LANES), jnp.float32),
            pltpu.VMEM((len(blocks), points, plane), jnp.float32),
            pltpu.VMEM((points, points, LANES), jnp.float32),
            pltpu.VMEM((jobs + for_b, points, plane), jnp.float32),
            pltpu.SemaphoreType.DMA((len(blocks), X_STEPS)),
            pltpu.SemaphoreType.DMA((plane_steps,)),
            pltpu.SemaphoreType.DMA((len(rows), X_STEPS)),
        ],
        compiler_params=pltpu.CompilerParams(vmem_limit_bytes=63 * 2**20),
        cost_estimate=pl.CostEstimate(
            flops=100_000_000, bytes_accessed=1_000_000, transcendentals=0
        ),
        name="pair_terms",
    )(flags, *blocks, *waited, kernel, left, right)


def copy_body(flags_ref, kernel_ref, left_ref, right_ref, block_ref, first_ref, second_ref):
    del flags_ref, kernel_ref, left_ref, right_ref
    first_ref[...] = block_ref[...]
    second_ref[...] = block_ref[...]


def copied(flags, constants, block):
    points, plane = block.shape
    part = pl.BlockSpec((points, plane // X_STEPS), lambda i: (0, i))
    return pl.pallas_call(
        copy_body,
        grid=(X_STEPS,),
        in_specs=[
            pl.BlockSpec(memory_space=pltpu.SMEM),
            *[pl.BlockSpec(memory_space=pl.ANY)] * 3,
            part,
        ],
        out_specs=[part, part],
        out_shape=[jax.ShapeDtypeStruct(block.shape, block.dtype)] * 2,
        compiler_params=pltpu.CompilerParams(vmem_limit_bytes=63 * 2**20),
        name="copied",
    )(flags, *constants, block)


def gate_body(*refs):
    del refs


def gate(token, kernel, partner, block):
    anywhere = pl.BlockSpec(memory_space=pl.ANY)
    return pl.pallas_call(
        gate_body,
        in_specs=[anywhere] * 4,
        out_specs=[anywhere] * 2,
        out_shape=[
            jax.ShapeDtypeStruct(kernel.shape, kernel.dtype),
            jax.ShapeDtypeStruct(block.shape, block.dtype),
        ],
        input_output_aliases={1: 0, 3: 1},
        compiler_params=pltpu.CompilerParams(vmem_limit_bytes=63 * 2**20),
        name="gate",
    )(token, kernel, partner, block)


def hold_body(*refs):
    del refs


def hold(block, *then):
    anywhere = pl.BlockSpec(memory_space=pl.ANY)
    return pl.pallas_call(
        hold_body,
        in_specs=[anywhere] * (1 + len(then)),
        out_specs=anywhere,
        out_shape=jax.ShapeDtypeStruct(block.shape, block.dtype),
        input_output_aliases={0: 0},
        compiler_params=pltpu.CompilerParams(vmem_limit_bytes=63 * 2**20),
        name="hold",
    )(block, *then)


def settle_body(wanted, count, flags_ref, *refs):
    parts, (out_ref, near, sems) = refs[:count], refs[count + 1:]
    columns = out_ref.shape[1] // SETTLE_STEPS

    @pl.when(flags_ref[RESULT] == wanted)
    def move():
        copies = []
        for i in range(SETTLE_STEPS):
            span = pl.ds(i * columns, columns)
            start = 0
            for j, part in enumerate(parts):
                rows = pl.ds(start, part.shape[0])
                start += part.shape[0]
                copies.append((
                    pltpu.make_async_copy(part.at[:, span], near.at[rows, span], sems.at[0, j, i]),
                    pltpu.make_async_copy(near.at[rows, span], out_ref.at[rows, span], sems.at[1, j, i]),
                ))
        for inward, outward in copies:
            inward.start()
        for inward, outward in copies:
            inward.wait()
            outward.start()
        for inward, outward in copies:
            outward.wait()


def settle(flags, wanted, parts, own_sum):
    anywhere = pl.BlockSpec(memory_space=pl.ANY)
    count = len(parts)
    return pl.pallas_call(
        functools.partial(settle_body, wanted, count),
        in_specs=[pl.BlockSpec(memory_space=pltpu.SMEM)] + [anywhere] * (count + 1),
        out_specs=anywhere,
        out_shape=jax.ShapeDtypeStruct(own_sum.shape, own_sum.dtype),
        input_output_aliases={count + 1: 0},
        scratch_shapes=[
            pltpu.VMEM(own_sum.shape, own_sum.dtype),
            pltpu.SemaphoreType.DMA((2, count, SETTLE_STEPS)),
        ],
        compiler_params=pltpu.CompilerParams(vmem_limit_bytes=63 * 2**20),
        name="settle",
    )(flags, *parts, own_sum)


def both_halves(*pairs):
    return list(pairs) + [(15 - source, 15 - target) for source, target in pairs]


CROSSING = both_halves((3, 14), (4, 9))
PARTNERS = both_halves((8, 14), (15, 9), (9, 11), (14, 12))
ARRIVED = both_halves((14, 2), (9, 5))
SINGLES = both_halves((5, 10), (2, 13))
BESIDE = both_halves((13, 14), (10, 9))
DIRECT = both_halves((15, 10), (8, 13))
TURNED = both_halves((11, 14), (12, 9))
HOME_ACROSS = both_halves((9, 4), (14, 3))
HOME_FAR = both_halves((9, 15), (14, 8))
HOME_TURN = both_halves((9, 11), (14, 12))
HOME_TURNED = both_halves((11, 15), (12, 8))
RESULT = 10
FLAGS = {i: (1, 0, 1, 1, 0, 0, 0, 0, 1, 1, 0) for i in (9, 14, 6, 1)}
FLAGS.update({i: (0, 0, 0, 0, 1, 0, 1, 1, 0, 0, 0) for i in (10, 13, 5, 2)})
FLAGS.update({i: (0,) * RESULT + (1,) for i in (3, 4, 11, 12)})
FLAGS.update({i: (0,) * RESULT + (2,) for i in (15, 8, 0, 7)})


def sixteen_bands(orbitals, constants):
    def send(value, pairs):
        return lax.ppermute(value[None], "band", pairs)[0]

    kernel, left, right = constants
    own = orbitals[0]
    flags = jnp.asarray([FLAGS[i] for i in range(16)], jnp.int32)
    flags = flags[lax.axis_index("band")]
    pair = functools.partial(pair_terms, flags)
    crossed = send(own, CROSSING)
    partner = send(own, PARTNERS)
    own_copy, direct_copy = copied(flags, constants, own)
    token = crossed[:8, :LANES] + own_copy[:8, :LANES]
    direct_copy = hold(direct_copy, partner)
    direct = send(direct_copy, DIRECT)
    kernel, held_back = gate(send(token, ARRIVED), kernel, direct_copy, own_copy)
    constants = (kernel, left, right)
    beside = send(held_back, BESIDE)
    single = send(held_back, SINGLES)

    partner_sum, own_sum, crossed_sum = pair(
        0, [partner, own], crossed, constants, for_b=True, plane_steps=1
    )
    home = send(crossed_sum, HOME_ACROSS)
    partner = hold(partner, own_sum)
    turned = send(partner, TURNED)
    top, bottom = pair(1, [partner], beside, constants, sum_a=partner_sum, halves=True, then=direct, plane_steps=1)
    bottom = send(bottom, HOME_TURN)
    top = send(top, HOME_FAR)
    (own_sum,) = pair(2, [own], direct, constants, sum_a=own_sum, in_place=True)
    (own_sum,) = pair(3, [own], single, constants, sum_a=own_sum, in_place=True)
    bottom = send(hold(bottom, own_sum), HOME_TURNED)
    own_sum = settle(flags, 1, [home], own_sum)
    (own_sum,) = pair(4, [own], turned, constants, sum_a=own_sum, in_place=True)
    return settle(flags, 2, [top, bottom], own_sum)[None]


def any_bands(orbitals, constants):
    own = orbitals[0]
    flags = jnp.ones((4,), jnp.int32)
    lower = from_behind(orbitals, "band", OFFSET)[0]
    upper = from_behind(orbitals, "band", -OFFSET)[0]
    (total,) = pair_terms(flags, 0, [own], lower, constants)
    return pair_terms(flags, 1, [own], upper, constants, sum_a=total)[0][None]


def local(bands, orbitals):
    points = orbitals.shape[1]
    constants = (screened_kernel(points), *hartley_tables(points))
    if bands == 16:
        return sixteen_bands(orbitals, constants)
    return any_bands(orbitals, constants)


def solution(mesh):
    return jax.shard_map(
        functools.partial(local, mesh.shape["band"]),
        mesh=mesh,
        in_specs=(P(("groups", "band"), None, None),),
        out_specs=P(("groups", "band"), None, None),
        check_vma=False,
    )
```

```python
import functools
import math

import jax
import jax.numpy as jnp
import numpy as np
from jax import lax
from jax.experimental import pallas as pl
from jax.experimental.pallas import tpu as pltpu
from jax.sharding import PartitionSpec as P

OFFSET = 5
screening = 5.44
LANES = 128
X_STEPS = 3
SETTLE_STEPS = 6
FAR_ROWS = 40


def from_behind(value, axis, by):
    count = lax.axis_size(axis)
    return lax.ppermute(value, axis, [(i, (i + by) % count) for i in range(count)])


def screened_kernel(points):
    signed = jnp.arange(LANES, dtype=jnp.int32)
    inside = signed < points
    signed = jnp.where(signed >= points // 2, signed - points, signed)
    wavenumber = signed.astype(jnp.float32) * (2.0 * math.pi / points)
    squared = (
        wavenumber[:points, None, None] ** 2
        + wavenumber[None, :points, None] ** 2
        + wavenumber[None, None, :] ** 2
    )
    screen_rate = screening / points
    finite = jnp.where(squared > 0.0, squared, 1.0)
    screened = 4.0 * math.pi / finite * -jnp.expm1(-finite / (4.0 * screen_rate * screen_rate))
    kernel = jnp.where(squared > 0.0, screened, math.pi / (screen_rate * screen_rate))
    return jnp.where(inside, kernel / -float(points * points * points), 0.0)


def hartley_tables(points):
    counter = np.arange(points)
    angles = 2.0 * np.pi * (counter[:, None] * counter[None, :] % points) / points
    table = np.cos(angles) + np.sin(angles)
    high = table.astype(jnp.bfloat16)
    low = (table - high.astype(np.float64)).astype(jnp.bfloat16)
    left = np.zeros((2 * points, 2 * points), jnp.bfloat16)
    left[:points, :points] = high
    left[:points, points:] = high
    left[points:, :points] = low
    right = np.zeros((2 * LANES, 2 * LANES), jnp.bfloat16)
    right[:points, :points] = high
    right[:points, LANES:LANES + points] = low
    right[LANES:LANES + points, :points] = high
    return jnp.asarray(left), jnp.asarray(right)


def two_terms(value):
    high = value.astype(jnp.bfloat16)
    low = (value - high.astype(jnp.float32)).astype(jnp.bfloat16)
    return high, low


def from_left(left, value):
    half = value.shape[0]
    terms = jnp.concatenate(two_terms(value), 0)
    out = jnp.dot(left, terms, preferred_element_type=jnp.float32)
    return out[:half] + out[half:]


def from_right(value, right):
    out = jnp.dot(jnp.concatenate(two_terms(value), 1), right, preferred_element_type=jnp.float32)
    return out[:, :LANES] + out[:, LANES:]


def pair_body(points, slot, jobs, plane_steps, has, *refs):
    refs = list(refs)
    flags_ref = refs.pop(0)
    a_names = ["a%d" % job for job in range(jobs)]
    names = a_names + ["b"] + ["sum_a"] * ("sum_a" in has)
    far = {name: refs.pop(0) for name in names}
    if "then" in has:
        refs.pop(0)
    kernel_ref, left_ref, right_ref = refs.pop(0), refs.pop(0), refs.pop(0)
    outs = ["for_a%d" % job for job in range(jobs)]
    if "halves" in has:
        outs.append("low_a0")
    if "for_b" in has:
        outs.append("for_b")
    out_refs = {name: refs.pop(0) for name in outs}
    held, near, near_kernel, near_out, sems, kernel_sems, out_sems = refs
    step = pl.program_id(0)
    active = flags_ref[2 * slot] == 1
    with_sum = flags_ref[2 * slot + 1] == 1
    columns = near.shape[2] // X_STEPS
    ys = columns // points
    per_step = points // plane_steps
    late = X_STEPS + plane_steps
    steps = late + X_STEPS
    job = step // steps if jobs > 1 else 0
    at = step % steps if jobs > 1 else step

    def span_of(chunk):
        start = chunk * columns
        return pl.ds(start if isinstance(chunk, int) else pl.multiple_of(start, columns), columns)

    def fetch(name, chunk):
        place, span = names.index(name), span_of(chunk)
        return pltpu.make_async_copy(
            far[name].at[:, span], near.at[place, :, span], sems.at[place, chunk]
        )

    def fetch_kernel(part):
        span = pl.ds(part * per_step, per_step)
        return pltpu.make_async_copy(
            kernel_ref.at[span], near_kernel.at[span], kernel_sems.at[part]
        )

    def give(name, chunk):
        span = span_of(chunk)
        source = near_out.at[jobs if name == "for_b" else int(name[-1])]
        if "halves" in has and name != "for_b":
            rows = pl.ds(points - FAR_ROWS, FAR_ROWS) if name == "low_a0" else pl.ds(0, points - FAR_ROWS)
            source = source.at[rows, span]
        else:
            source = source.at[:, span]
        return pltpu.make_async_copy(
            source, out_refs[name].at[:, span], out_sems.at[outs.index(name), chunk]
        )

    def here(name, chunk):
        place = job if name == "a" else names.index(name)
        return near[place, :, span_of(chunk)]

    def when_job(number, work):
        if jobs > 1:
            pl.when(job == number)(work)
        elif number == 0:
            work()

    @pl.when(active & (step == 0))
    def start_first():
        for chunk in range(2):
            for name in ("a0", "b"):
                fetch(name, chunk).start()

    @pl.when(active & (step + 2 < X_STEPS))
    def start_next():
        for name in ("a0", "b"):
            fetch(name, step + 2).start()

    @pl.when(active & (step == 0))
    def start_kernel():
        for part in range(plane_steps):
            fetch_kernel(part).start()

    @pl.when(active & (step == X_STEPS))
    def start_rest():
        for chunk in range(X_STEPS):
            for name in a_names[1:] + ["sum_a"] * ("sum_a" in has):
                fetch(name, chunk).start()

    def lanes_apart(block):
        tail = jnp.zeros((points, LANES), jnp.float32)
        wide = jnp.concatenate([block, tail], 1)
        rows = [wide[:, q * points:q * points + LANES] for q in range(ys)]
        return jnp.swapaxes(jnp.stack(rows, 0), 0, 1)

    def lanes_together(block):
        block = jnp.swapaxes(block, 0, 1)
        return jnp.concatenate([block[q][:, :points] for q in range(ys)], 1)

    def side_by_side(block):
        return jnp.concatenate([block[i] for i in range(per_step)], 1)

    @pl.when(active & (at < X_STEPS))
    def forward_x():
        chunk = at

        def first_waits():
            fetch("a0", chunk).wait()
            fetch("b", chunk).wait()

        when_job(0, first_waits)
        for number in range(1, jobs):
            when_job(number, fetch(a_names[number], chunk).wait)
        spectrum = from_left(left_ref[...], here("a", chunk) * here("b", chunk))
        start = pl.multiple_of(chunk * ys, ys)
        held[:, pl.ds(start, ys), :] = lanes_apart(spectrum)

    @pl.when(active & (at >= X_STEPS) & (at < late))
    def planes():
        part = at - X_STEPS
        left = left_ref[...]
        right = right_ref[...]
        first = part * per_step
        when_job(0, lambda: fetch_kernel(part).wait())
        block = held[pl.ds(first, per_step)].reshape(per_step * points, LANES)
        block = from_right(block, right).reshape(per_step, points, LANES)
        wide = from_left(left, side_by_side(block))
        wide = from_left(left, wide * side_by_side(near_kernel[pl.ds(first, per_step)]))
        block = jnp.concatenate(
            [wide[:, i * LANES:(i + 1) * LANES] for i in range(per_step)], 0
        )
        block = from_right(block, right)
        held[pl.ds(first, per_step)] = block.reshape(per_step, points, LANES)

    @pl.when(active & (at >= late))
    def inverse_x():
        chunk = at - late
        start = pl.multiple_of(chunk * ys, ys)
        if "sum_a" in has:
            fetch("sum_a", chunk).wait()
        block = lanes_together(held[:, pl.ds(start, ys), :])
        potential = from_left(left_ref[...], block)
        for_a = here("b", chunk) * potential
        if "sum_a" in has:
            for_a = for_a + jnp.where(with_sum, here("sum_a", chunk), 0.0)
        near_out[job, :, span_of(chunk)] = for_a
        if "for_b" in has:
            for_b = here("a", chunk) * potential
            if jobs > 1:
                for_b = for_b + jnp.where(job > 0, near_out[jobs, :, span_of(chunk)], 0.0)
            near_out[jobs, :, span_of(chunk)] = for_b

        def give_all(number):
            for name in outs:
                if number == (jobs - 1 if name == "for_b" else int(name[-1])):
                    give(name, chunk).start()

        for number in range(jobs):
            when_job(number, functools.partial(give_all, number))

    @pl.when(active & (step == jobs * steps - 1))
    def wait_outs():
        for chunk in range(X_STEPS):
            for name in outs:
                give(name, chunk).wait()


def pair_terms(
    flags, slot, a, b, constants, sum_a=None, for_b=False, halves=False, in_place=False, then=None,
    plane_steps=2,
):
    points, plane = b.shape
    kernel, left, right = constants
    jobs = len(a)
    blocks = [*a, b] + [sum_a] * (sum_a is not None)
    waited = [] if then is None else [then]
    has = ["sum_a"] * (sum_a is not None) + ["for_b"] * for_b + ["halves"] * halves + ["then"] * len(waited)
    rows = ([points - FAR_ROWS, FAR_ROWS] if halves else [points] * jobs) + [points] * for_b
    anywhere = pl.BlockSpec(memory_space=pl.ANY)
    return pl.pallas_call(
        functools.partial(pair_body, points, slot, jobs, plane_steps, has),
        grid=(jobs * (2 * X_STEPS + plane_steps),),
        in_specs=[pl.BlockSpec(memory_space=pltpu.SMEM)]
        + [anywhere] * (len(blocks) + len(waited) + 1)
        + [pl.BlockSpec(table.shape, lambda i: (0, 0)) for table in (left, right)],
        out_specs=[anywhere] * len(rows),
        out_shape=[jax.ShapeDtypeStruct((n, plane), jnp.float32) for n in rows],
        input_output_aliases={3: 0} if in_place else {},
        scratch_shapes=[
            pltpu.VMEM((points, points, LANES), jnp.float32),
            pltpu.VMEM((len(blocks), points, plane), jnp.float32),
            pltpu.VMEM((points, points, LANES), jnp.float32),
            pltpu.VMEM((jobs + for_b, points, plane), jnp.float32),
            pltpu.SemaphoreType.DMA((len(blocks), X_STEPS)),
            pltpu.SemaphoreType.DMA((plane_steps,)),
            pltpu.SemaphoreType.DMA((len(rows), X_STEPS)),
        ],
        compiler_params=pltpu.CompilerParams(vmem_limit_bytes=63 * 2**20),
        cost_estimate=pl.CostEstimate(
            flops=100_000_000, bytes_accessed=1_000_000, transcendentals=0
        ),
        name="pair_terms",
    )(flags, *blocks, *waited, kernel, left, right)


def copy_body(flags_ref, kernel_ref, left_ref, right_ref, block_ref, first_ref, second_ref):
    del flags_ref, kernel_ref, left_ref, right_ref
    first_ref[...] = block_ref[...]
    second_ref[...] = block_ref[...]


def copied(flags, constants, block):
    points, plane = block.shape
    part = pl.BlockSpec((points, plane // X_STEPS), lambda i: (0, i))
    return pl.pallas_call(
        copy_body,
        grid=(X_STEPS,),
        in_specs=[
            pl.BlockSpec(memory_space=pltpu.SMEM),
            *[pl.BlockSpec(memory_space=pl.ANY)] * 3,
            part,
        ],
        out_specs=[part, part],
        out_shape=[jax.ShapeDtypeStruct(block.shape, block.dtype)] * 2,
        compiler_params=pltpu.CompilerParams(vmem_limit_bytes=63 * 2**20),
        name="copied",
    )(flags, *constants, block)


def gate_body(*refs):
    del refs


def gate(token, kernel, partner, block):
    anywhere = pl.BlockSpec(memory_space=pl.ANY)
    return pl.pallas_call(
        gate_body,
        in_specs=[anywhere] * 4,
        out_specs=[anywhere] * 2,
        out_shape=[
            jax.ShapeDtypeStruct(kernel.shape, kernel.dtype),
            jax.ShapeDtypeStruct(block.shape, block.dtype),
        ],
        input_output_aliases={1: 0, 3: 1},
        compiler_params=pltpu.CompilerParams(vmem_limit_bytes=63 * 2**20),
        name="gate",
    )(token, kernel, partner, block)


def hold_body(*refs):
    del refs


def hold(block, *then):
    anywhere = pl.BlockSpec(memory_space=pl.ANY)
    return pl.pallas_call(
        hold_body,
        in_specs=[anywhere] * (1 + len(then)),
        out_specs=anywhere,
        out_shape=jax.ShapeDtypeStruct(block.shape, block.dtype),
        input_output_aliases={0: 0},
        compiler_params=pltpu.CompilerParams(vmem_limit_bytes=63 * 2**20),
        name="hold",
    )(block, *then)


def settle_body(wanted, count, flags_ref, *refs):
    parts, (out_ref, near, sems) = refs[:count], refs[count + 1:]
    columns = out_ref.shape[1] // SETTLE_STEPS

    @pl.when(flags_ref[RESULT] == wanted)
    def move():
        copies = []
        for i in range(SETTLE_STEPS):
            span = pl.ds(i * columns, columns)
            start = 0
            for j, part in enumerate(parts):
                rows = pl.ds(start, part.shape[0])
                start += part.shape[0]
                copies.append((
                    pltpu.make_async_copy(part.at[:, span], near.at[rows, span], sems.at[0, j, i]),
                    pltpu.make_async_copy(near.at[rows, span], out_ref.at[rows, span], sems.at[1, j, i]),
                ))
        for inward, outward in copies:
            inward.start()
        for inward, outward in copies:
            inward.wait()
            outward.start()
        for inward, outward in copies:
            outward.wait()


def settle(flags, wanted, parts, own_sum):
    anywhere = pl.BlockSpec(memory_space=pl.ANY)
    count = len(parts)
    return pl.pallas_call(
        functools.partial(settle_body, wanted, count),
        in_specs=[pl.BlockSpec(memory_space=pltpu.SMEM)] + [anywhere] * (count + 1),
        out_specs=anywhere,
        out_shape=jax.ShapeDtypeStruct(own_sum.shape, own_sum.dtype),
        input_output_aliases={count + 1: 0},
        scratch_shapes=[
            pltpu.VMEM(own_sum.shape, own_sum.dtype),
            pltpu.SemaphoreType.DMA((2, count, SETTLE_STEPS)),
        ],
        compiler_params=pltpu.CompilerParams(vmem_limit_bytes=63 * 2**20),
        name="settle",
    )(flags, *parts, own_sum)


def both_halves(*pairs):
    return list(pairs) + [(15 - source, 15 - target) for source, target in pairs]


CROSSING = both_halves((3, 14), (4, 9))
PARTNERS = both_halves((8, 14), (15, 9), (9, 11), (14, 12))
ARRIVED = both_halves((14, 2), (9, 5))
SINGLES = both_halves((5, 10), (2, 13))
BESIDE = both_halves((13, 14), (10, 9))
DIRECT = both_halves((15, 10), (8, 13))
TURNED = both_halves((11, 14), (12, 9))
HOME_ACROSS = both_halves((9, 4), (14, 3))
HOME_FAR = both_halves((9, 15), (14, 8))
HOME_TURN = both_halves((9, 11), (14, 12))
HOME_TURNED = both_halves((11, 15), (12, 8))
RESULT = 10
FLAGS = {i: (1, 0, 1, 1, 0, 0, 0, 0, 1, 1, 0) for i in (9, 14, 6, 1)}
FLAGS.update({i: (0, 0, 0, 0, 1, 0, 1, 1, 0, 0, 0) for i in (10, 13, 5, 2)})
FLAGS.update({i: (0,) * RESULT + (1,) for i in (3, 4, 11, 12)})
FLAGS.update({i: (0,) * RESULT + (2,) for i in (15, 8, 0, 7)})


def sixteen_bands(orbitals, constants):
    def send(value, pairs):
        return lax.ppermute(value[None], "band", pairs)[0]

    kernel, left, right = constants
    own = orbitals[0]
    flags = jnp.asarray([FLAGS[i] for i in range(16)], jnp.int32)
    flags = flags[lax.axis_index("band")]
    pair = functools.partial(pair_terms, flags)
    crossed = send(own, CROSSING)
    partner = send(own, PARTNERS)
    own_copy, direct_copy = copied(flags, constants, own)
    token = crossed[:8, :LANES] + own_copy[:8, :LANES]
    direct_copy = hold(direct_copy, partner)
    direct = send(direct_copy, DIRECT)
    kernel, held_back = gate(send(token, ARRIVED), kernel, direct_copy, own_copy)
    constants = (kernel, left, right)
    turned = send(partner, TURNED)
    beside = send(held_back, BESIDE)
    single = send(held_back, SINGLES)

    partner_sum, own_sum, crossed_sum = pair(
        0, [partner, own], crossed, constants, for_b=True, plane_steps=1
    )
    home = send(crossed_sum, HOME_ACROSS)
    top, bottom = pair(1, [partner], beside, constants, sum_a=partner_sum, halves=True, then=direct, plane_steps=1)
    bottom = send(bottom, HOME_TURN)
    top = send(top, HOME_FAR)
    (own_sum,) = pair(2, [own], direct, constants, sum_a=own_sum, in_place=True)
    (own_sum,) = pair(4, [own], turned, constants, sum_a=own_sum, in_place=True, then=single)
    (own_sum,) = pair(3, [own], single, constants, sum_a=own_sum, in_place=True)
    bottom = send(hold(bottom, own_sum), HOME_TURNED)
    own_sum = settle(flags, 1, [home], own_sum)
    return settle(flags, 2, [top, bottom], own_sum)[None]


def any_bands(orbitals, constants):
    own = orbitals[0]
    flags = jnp.ones((4,), jnp.int32)
    lower = from_behind(orbitals, "band", OFFSET)[0]
    upper = from_behind(orbitals, "band", -OFFSET)[0]
    (total,) = pair_terms(flags, 0, [own], lower, constants)
    return pair_terms(flags, 1, [own], upper, constants, sum_a=total)[0][None]


def local(bands, orbitals):
    points = orbitals.shape[1]
    constants = (screened_kernel(points), *hartley_tables(points))
    if bands == 16:
        return sixteen_bands(orbitals, constants)
    return any_bands(orbitals, constants)


def solution(mesh):
    return jax.shard_map(
        functools.partial(local, mesh.shape["band"]),
        mesh=mesh,
        in_specs=(P(("groups", "band"), None, None),),
        out_specs=P(("groups", "band"), None, None),
        check_vma=False,
    )
```

```python
import functools
import math

import jax
import jax.numpy as jnp
import numpy as np
from jax import lax
from jax.experimental import pallas as pl
from jax.experimental.pallas import tpu as pltpu
from jax.sharding import PartitionSpec as P

OFFSET = 5
screening = 5.44
LANES = 128
X_STEPS = 3
SETTLE_STEPS = 6
FAR_ROWS = 32


def from_behind(value, axis, by):
    count = lax.axis_size(axis)
    return lax.ppermute(value, axis, [(i, (i + by) % count) for i in range(count)])


def screened_kernel(points):
    signed = jnp.arange(LANES, dtype=jnp.int32)
    inside = signed < points
    signed = jnp.where(signed >= points // 2, signed - points, signed)
    wavenumber = signed.astype(jnp.float32) * (2.0 * math.pi / points)
    squared = (
        wavenumber[:points, None, None] ** 2
        + wavenumber[None, :points, None] ** 2
        + wavenumber[None, None, :] ** 2
    )
    screen_rate = screening / points
    finite = jnp.where(squared > 0.0, squared, 1.0)
    screened = 4.0 * math.pi / finite * -jnp.expm1(-finite / (4.0 * screen_rate * screen_rate))
    kernel = jnp.where(squared > 0.0, screened, math.pi / (screen_rate * screen_rate))
    return jnp.where(inside, kernel / -float(points * points * points), 0.0)


def hartley_tables(points):
    counter = np.arange(points)
    angles = 2.0 * np.pi * (counter[:, None] * counter[None, :] % points) / points
    table = np.cos(angles) + np.sin(angles)
    high = table.astype(jnp.bfloat16)
    low = (table - high.astype(np.float64)).astype(jnp.bfloat16)
    left = np.zeros((2 * points, 2 * points), jnp.bfloat16)
    left[:points, :points] = high
    left[:points, points:] = high
    left[points:, :points] = low
    right = np.zeros((2 * LANES, 2 * LANES), jnp.bfloat16)
    right[:points, :points] = high
    right[:points, LANES:LANES + points] = low
    right[LANES:LANES + points, :points] = high
    return jnp.asarray(left), jnp.asarray(right)


def two_terms(value):
    high = value.astype(jnp.bfloat16)
    low = (value - high.astype(jnp.float32)).astype(jnp.bfloat16)
    return high, low


def from_left(left, value):
    half = value.shape[0]
    terms = jnp.concatenate(two_terms(value), 0)
    out = jnp.dot(left, terms, preferred_element_type=jnp.float32)
    return out[:half] + out[half:]


def from_right(value, right):
    out = jnp.dot(jnp.concatenate(two_terms(value), 1), right, preferred_element_type=jnp.float32)
    return out[:, :LANES] + out[:, LANES:]


def pair_body(points, slot, jobs, plane_steps, has, *refs):
    refs = list(refs)
    flags_ref = refs.pop(0)
    a_names = ["a%d" % job for job in range(jobs)]
    names = a_names + ["b"] + ["sum_a"] * ("sum_a" in has)
    far = {name: refs.pop(0) for name in names}
    if "then" in has:
        refs.pop(0)
    kernel_ref, left_ref, right_ref = refs.pop(0), refs.pop(0), refs.pop(0)
    outs = ["for_a%d" % job for job in range(jobs)]
    if "halves" in has:
        outs.append("low_a0")
    if "for_b" in has:
        outs.append("for_b")
    out_refs = {name: refs.pop(0) for name in outs}
    held, near, near_kernel, near_out, sems, kernel_sems, out_sems = refs
    step = pl.program_id(0)
    active = flags_ref[2 * slot] == 1
    with_sum = flags_ref[2 * slot + 1] == 1
    columns = near.shape[2] // X_STEPS
    ys = columns // points
    per_step = points // plane_steps
    late = X_STEPS + plane_steps
    steps = late + X_STEPS
    job = step // steps if jobs > 1 else 0
    at = step % steps if jobs > 1 else step

    def span_of(chunk):
        start = chunk * columns
        return pl.ds(start if isinstance(chunk, int) else pl.multiple_of(start, columns), columns)

    def fetch(name, chunk):
        place, span = names.index(name), span_of(chunk)
        return pltpu.make_async_copy(
            far[name].at[:, span], near.at[place, :, span], sems.at[place, chunk]
        )

    def fetch_kernel(part):
        span = pl.ds(part * per_step, per_step)
        return pltpu.make_async_copy(
            kernel_ref.at[span], near_kernel.at[span], kernel_sems.at[part]
        )

    def give(name, chunk):
        span = span_of(chunk)
        source = near_out.at[jobs if name == "for_b" else int(name[-1])]
        if "halves" in has and name != "for_b":
            rows = pl.ds(points - FAR_ROWS, FAR_ROWS) if name == "low_a0" else pl.ds(0, points - FAR_ROWS)
            source = source.at[rows, span]
        else:
            source = source.at[:, span]
        return pltpu.make_async_copy(
            source, out_refs[name].at[:, span], out_sems.at[outs.index(name), chunk]
        )

    def here(name, chunk):
        place = job if name == "a" else names.index(name)
        return near[place, :, span_of(chunk)]

    def when_job(number, work):
        if jobs > 1:
            pl.when(job == number)(work)
        elif number == 0:
            work()

    @pl.when(active & (step == 0))
    def start_first():
        for chunk in range(2):
            for name in ("a0", "b"):
                fetch(name, chunk).start()

    @pl.when(active & (step + 2 < X_STEPS))
    def start_next():
        for name in ("a0", "b"):
            fetch(name, step + 2).start()

    @pl.when(active & (step == 0))
    def start_kernel():
        for part in range(plane_steps):
            fetch_kernel(part).start()

    @pl.when(active & (step == X_STEPS))
    def start_rest():
        for chunk in range(X_STEPS):
            for name in a_names[1:] + ["sum_a"] * ("sum_a" in has):
                fetch(name, chunk).start()

    def lanes_apart(block):
        tail = jnp.zeros((points, LANES), jnp.float32)
        wide = jnp.concatenate([block, tail], 1)
        rows = [wide[:, q * points:q * points + LANES] for q in range(ys)]
        return jnp.swapaxes(jnp.stack(rows, 0), 0, 1)

    def lanes_together(block):
        block = jnp.swapaxes(block, 0, 1)
        return jnp.concatenate([block[q][:, :points] for q in range(ys)], 1)

    def side_by_side(block):
        return jnp.concatenate([block[i] for i in range(per_step)], 1)

    @pl.when(active & (at < X_STEPS))
    def forward_x():
        chunk = at

        def first_waits():
            fetch("a0", chunk).wait()
            fetch("b", chunk).wait()

        when_job(0, first_waits)
        for number in range(1, jobs):
            when_job(number, fetch(a_names[number], chunk).wait)
        spectrum = from_left(left_ref[...], here("a", chunk) * here("b", chunk))
        start = pl.multiple_of(chunk * ys, ys)
        held[:, pl.ds(start, ys), :] = lanes_apart(spectrum)

    @pl.when(active & (at >= X_STEPS) & (at < late))
    def planes():
        part = at - X_STEPS
        left = left_ref[...]
        right = right_ref[...]
        first = part * per_step
        when_job(0, lambda: fetch_kernel(part).wait())
        block = held[pl.ds(first, per_step)].reshape(per_step * points, LANES)
        block = from_right(block, right).reshape(per_step, points, LANES)
        wide = from_left(left, side_by_side(block))
        wide = from_left(left, wide * side_by_side(near_kernel[pl.ds(first, per_step)]))
        block = jnp.concatenate(
            [wide[:, i * LANES:(i + 1) * LANES] for i in range(per_step)], 0
        )
        block = from_right(block, right)
        held[pl.ds(first, per_step)] = block.reshape(per_step, points, LANES)

    @pl.when(active & (at >= late))
    def inverse_x():
        chunk = at - late
        start = pl.multiple_of(chunk * ys, ys)
        if "sum_a" in has:
            fetch("sum_a", chunk).wait()
        block = lanes_together(held[:, pl.ds(start, ys), :])
        potential = from_left(left_ref[...], block)
        for_a = here("b", chunk) * potential
        if "sum_a" in has:
            for_a = for_a + jnp.where(with_sum, here("sum_a", chunk), 0.0)
        near_out[job, :, span_of(chunk)] = for_a
        if "for_b" in has:
            for_b = here("a", chunk) * potential
            if jobs > 1:
                for_b = for_b + jnp.where(job > 0, near_out[jobs, :, span_of(chunk)], 0.0)
            near_out[jobs, :, span_of(chunk)] = for_b

        def give_all(number):
            for name in outs:
                if number == (jobs - 1 if name == "for_b" else int(name[-1])):
                    give(name, chunk).start()

        for number in range(jobs):
            when_job(number, functools.partial(give_all, number))

    @pl.when(active & (step == jobs * steps - 1))
    def wait_outs():
        for chunk in range(X_STEPS):
            for name in outs:
                give(name, chunk).wait()


def pair_terms(
    flags, slot, a, b, constants, sum_a=None, for_b=False, halves=False, in_place=False, then=None,
    plane_steps=2,
):
    points, plane = b.shape
    kernel, left, right = constants
    jobs = len(a)
    blocks = [*a, b] + [sum_a] * (sum_a is not None)
    waited = [] if then is None else [then]
    has = ["sum_a"] * (sum_a is not None) + ["for_b"] * for_b + ["halves"] * halves + ["then"] * len(waited)
    rows = ([points - FAR_ROWS, FAR_ROWS] if halves else [points] * jobs) + [points] * for_b
    anywhere = pl.BlockSpec(memory_space=pl.ANY)
    return pl.pallas_call(
        functools.partial(pair_body, points, slot, jobs, plane_steps, has),
        grid=(jobs * (2 * X_STEPS + plane_steps),),
        in_specs=[pl.BlockSpec(memory_space=pltpu.SMEM)]
        + [anywhere] * (len(blocks) + len(waited) + 1)
        + [pl.BlockSpec(table.shape, lambda i: (0, 0)) for table in (left, right)],
        out_specs=[anywhere] * len(rows),
        out_shape=[jax.ShapeDtypeStruct((n, plane), jnp.float32) for n in rows],
        input_output_aliases={3: 0} if in_place else {},
        scratch_shapes=[
            pltpu.VMEM((points, points, LANES), jnp.float32),
            pltpu.VMEM((len(blocks), points, plane), jnp.float32),
            pltpu.VMEM((points, points, LANES), jnp.float32),
            pltpu.VMEM((jobs + for_b, points, plane), jnp.float32),
            pltpu.SemaphoreType.DMA((len(blocks), X_STEPS)),
            pltpu.SemaphoreType.DMA((plane_steps,)),
            pltpu.SemaphoreType.DMA((len(rows), X_STEPS)),
        ],
        compiler_params=pltpu.CompilerParams(vmem_limit_bytes=63 * 2**20),
        cost_estimate=pl.CostEstimate(
            flops=100_000_000, bytes_accessed=1_000_000, transcendentals=0
        ),
        name="pair_terms",
    )(flags, *blocks, *waited, kernel, left, right)


def copy_body(flags_ref, kernel_ref, left_ref, right_ref, block_ref, first_ref, second_ref):
    del flags_ref, kernel_ref, left_ref, right_ref
    first_ref[...] = block_ref[...]
    second_ref[...] = block_ref[...]


def copied(flags, constants, block):
    points, plane = block.shape
    part = pl.BlockSpec((points, plane // X_STEPS), lambda i: (0, i))
    return pl.pallas_call(
        copy_body,
        grid=(X_STEPS,),
        in_specs=[
            pl.BlockSpec(memory_space=pltpu.SMEM),
            *[pl.BlockSpec(memory_space=pl.ANY)] * 3,
            part,
        ],
        out_specs=[part, part],
        out_shape=[jax.ShapeDtypeStruct(block.shape, block.dtype)] * 2,
        compiler_params=pltpu.CompilerParams(vmem_limit_bytes=63 * 2**20),
        name="copied",
    )(flags, *constants, block)


def gate_body(*refs):
    del refs


def gate(token, kernel, partner, block):
    anywhere = pl.BlockSpec(memory_space=pl.ANY)
    return pl.pallas_call(
        gate_body,
        in_specs=[anywhere] * 4,
        out_specs=[anywhere] * 2,
        out_shape=[
            jax.ShapeDtypeStruct(kernel.shape, kernel.dtype),
            jax.ShapeDtypeStruct(block.shape, block.dtype),
        ],
        input_output_aliases={1: 0, 3: 1},
        compiler_params=pltpu.CompilerParams(vmem_limit_bytes=63 * 2**20),
        name="gate",
    )(token, kernel, partner, block)


def hold_body(*refs):
    del refs


def hold(block, *then):
    anywhere = pl.BlockSpec(memory_space=pl.ANY)
    return pl.pallas_call(
        hold_body,
        in_specs=[anywhere] * (1 + len(then)),
        out_specs=anywhere,
        out_shape=jax.ShapeDtypeStruct(block.shape, block.dtype),
        input_output_aliases={0: 0},
        compiler_params=pltpu.CompilerParams(vmem_limit_bytes=63 * 2**20),
        name="hold",
    )(block, *then)


def settle_body(wanted, count, flags_ref, *refs):
    parts, (out_ref, near, sems) = refs[:count], refs[count + 1:]
    columns = out_ref.shape[1] // SETTLE_STEPS

    @pl.when(flags_ref[RESULT] == wanted)
    def move():
        copies = []
        for i in range(SETTLE_STEPS):
            span = pl.ds(i * columns, columns)
            start = 0
            for j, part in enumerate(parts):
                rows = pl.ds(start, part.shape[0])
                start += part.shape[0]
                copies.append((
                    pltpu.make_async_copy(part.at[:, span], near.at[rows, span], sems.at[0, j, i]),
                    pltpu.make_async_copy(near.at[rows, span], out_ref.at[rows, span], sems.at[1, j, i]),
                ))
        for inward, outward in copies:
            inward.start()
        for inward, outward in copies:
            inward.wait()
            outward.start()
        for inward, outward in copies:
            outward.wait()


def settle(flags, wanted, parts, own_sum):
    anywhere = pl.BlockSpec(memory_space=pl.ANY)
    count = len(parts)
    return pl.pallas_call(
        functools.partial(settle_body, wanted, count),
        in_specs=[pl.BlockSpec(memory_space=pltpu.SMEM)] + [anywhere] * (count + 1),
        out_specs=anywhere,
        out_shape=jax.ShapeDtypeStruct(own_sum.shape, own_sum.dtype),
        input_output_aliases={count + 1: 0},
        scratch_shapes=[
            pltpu.VMEM(own_sum.shape, own_sum.dtype),
            pltpu.SemaphoreType.DMA((2, count, SETTLE_STEPS)),
        ],
        compiler_params=pltpu.CompilerParams(vmem_limit_bytes=63 * 2**20),
        name="settle",
    )(flags, *parts, own_sum)


def both_halves(*pairs):
    return list(pairs) + [(15 - source, 15 - target) for source, target in pairs]


CROSSING = both_halves((3, 14), (4, 9))
PARTNERS = both_halves((8, 14), (15, 9), (9, 11), (14, 12))
ARRIVED = both_halves((14, 2), (9, 5))
SINGLES = both_halves((5, 10), (2, 13))
BESIDE = both_halves((13, 14), (10, 9))
DIRECT = both_halves((15, 10), (8, 13))
TURNED = both_halves((11, 14), (12, 9))
HOME_ACROSS = both_halves((9, 4), (14, 3))
HOME_FAR = both_halves((9, 15), (14, 8))
HOME_TURN = both_halves((9, 11), (14, 12))
HOME_TURNED = both_halves((11, 15), (12, 8))
RESULT = 10
FLAGS = {i: (1, 0, 1, 1, 0, 0, 0, 0, 1, 1, 0) for i in (9, 14, 6, 1)}
FLAGS.update({i: (0, 0, 0, 0, 1, 0, 1, 1, 0, 0, 0) for i in (10, 13, 5, 2)})
FLAGS.update({i: (0,) * RESULT + (1,) for i in (3, 4, 11, 12)})
FLAGS.update({i: (0,) * RESULT + (2,) for i in (15, 8, 0, 7)})


def sixteen_bands(orbitals, constants):
    def send(value, pairs):
        return lax.ppermute(value[None], "band", pairs)[0]

    kernel, left, right = constants
    own = orbitals[0]
    flags = jnp.asarray([FLAGS[i] for i in range(16)], jnp.int32)
    flags = flags[lax.axis_index("band")]
    pair = functools.partial(pair_terms, flags)
    crossed = send(own, CROSSING)
    partner = send(own, PARTNERS)
    own_copy, direct_copy = copied(flags, constants, own)
    token = crossed[:8, :LANES] + own_copy[:8, :LANES]
    direct = send(direct_copy, DIRECT)
    kernel, held_back = gate(send(token, ARRIVED), kernel, partner, own_copy)
    constants = (kernel, left, right)
    beside = send(held_back, BESIDE)
    single = send(held_back, SINGLES)

    partner_sum, own_sum, crossed_sum = pair(
        0, [partner, own], crossed, constants, for_b=True, then=direct, plane_steps=1
    )
    home = send(crossed_sum, HOME_ACROSS)
    partner = hold(partner, own_sum)
    turned = send(partner, TURNED)
    top, bottom = pair(1, [partner], beside, constants, sum_a=partner_sum, halves=True, plane_steps=1)
    bottom = send(bottom, HOME_TURN)
    top = send(top, HOME_FAR)
    (own_sum,) = pair(2, [own], direct, constants, sum_a=own_sum, in_place=True)
    (own_sum,) = pair(3, [own], single, constants, sum_a=own_sum, in_place=True)
    bottom = send(hold(bottom, own_sum), HOME_TURNED)
    own_sum = settle(flags, 1, [home], own_sum)
    (own_sum,) = pair(4, [own], turned, constants, sum_a=own_sum, in_place=True)
    return settle(flags, 2, [top, bottom], own_sum)[None]


def any_bands(orbitals, constants):
    own = orbitals[0]
    flags = jnp.ones((4,), jnp.int32)
    lower = from_behind(orbitals, "band", OFFSET)[0]
    upper = from_behind(orbitals, "band", -OFFSET)[0]
    (total,) = pair_terms(flags, 0, [own], lower, constants)
    return pair_terms(flags, 1, [own], upper, constants, sum_a=total)[0][None]


def local(bands, orbitals):
    points = orbitals.shape[1]
    constants = (screened_kernel(points), *hartley_tables(points))
    if bands == 16:
        return sixteen_bands(orbitals, constants)
    return any_bands(orbitals, constants)


def solution(mesh):
    return jax.shard_map(
        functools.partial(local, mesh.shape["band"]),
        mesh=mesh,
        in_specs=(P(("groups", "band"), None, None),),
        out_specs=P(("groups", "band"), None, None),
        check_vma=False,
    )
```

```python
import functools
import math

import jax
import jax.numpy as jnp
import numpy as np
from jax import lax
from jax.experimental import pallas as pl
from jax.experimental.pallas import tpu as pltpu
from jax.sharding import PartitionSpec as P

OFFSET = 5
screening = 5.44
LANES = 128
X_STEPS = 3
SETTLE_ROWS = 8
FAR_ROWS = 32


def from_behind(value, axis, by):
    count = lax.axis_size(axis)
    return lax.ppermute(value, axis, [(i, (i + by) % count) for i in range(count)])


def screened_kernel(points):
    signed = jnp.arange(LANES, dtype=jnp.int32)
    inside = signed < points
    signed = jnp.where(signed >= points // 2, signed - points, signed)
    wavenumber = signed.astype(jnp.float32) * (2.0 * math.pi / points)
    squared = (
        wavenumber[:points, None, None] ** 2
        + wavenumber[None, :points, None] ** 2
        + wavenumber[None, None, :] ** 2
    )
    screen_rate = screening / points
    finite = jnp.where(squared > 0.0, squared, 1.0)
    screened = 4.0 * math.pi / finite * -jnp.expm1(-finite / (4.0 * screen_rate * screen_rate))
    kernel = jnp.where(squared > 0.0, screened, math.pi / (screen_rate * screen_rate))
    return jnp.where(inside, kernel / -float(points * points * points), 0.0)


def hartley_tables(points):
    counter = np.arange(points)
    angles = 2.0 * np.pi * (counter[:, None] * counter[None, :] % points) / points
    table = np.cos(angles) + np.sin(angles)
    high = table.astype(jnp.bfloat16)
    low = (table - high.astype(np.float64)).astype(jnp.bfloat16)
    left = np.zeros((2 * points, 2 * points), jnp.bfloat16)
    left[:points, :points] = high
    left[:points, points:] = high
    left[points:, :points] = low
    right = np.zeros((2 * LANES, 2 * LANES), jnp.bfloat16)
    right[:points, :points] = high
    right[:points, LANES:LANES + points] = low
    right[LANES:LANES + points, :points] = high
    return jnp.asarray(left), jnp.asarray(right)


def two_terms(value):
    high = value.astype(jnp.bfloat16)
    low = (value - high.astype(jnp.float32)).astype(jnp.bfloat16)
    return high, low


def from_left(left, value):
    half = value.shape[0]
    terms = jnp.concatenate(two_terms(value), 0)
    out = jnp.dot(left, terms, preferred_element_type=jnp.float32)
    return out[:half] + out[half:]


def from_right(value, right):
    out = jnp.dot(jnp.concatenate(two_terms(value), 1), right, preferred_element_type=jnp.float32)
    return out[:, :LANES] + out[:, LANES:]


def pair_body(points, slot, jobs, plane_steps, has, *refs):
    refs = list(refs)
    flags_ref = refs.pop(0)
    a_names = ["a%d" % job for job in range(jobs)]
    names = a_names + ["b"] + ["sum_a"] * ("sum_a" in has)
    far = {name: refs.pop(0) for name in names}
    if "then" in has:
        refs.pop(0)
    kernel_ref, left_ref, right_ref = refs.pop(0), refs.pop(0), refs.pop(0)
    outs = ["for_a%d" % job for job in range(jobs)]
    if "halves" in has:
        outs.append("low_a0")
    if "for_b" in has:
        outs.append("for_b")
    out_refs = {name: refs.pop(0) for name in outs}
    held, near, near_kernel, near_out, sems, kernel_sems, out_sems = refs
    step = pl.program_id(0)
    active = flags_ref[2 * slot] == 1
    with_sum = flags_ref[2 * slot + 1] == 1
    columns = near.shape[2] // X_STEPS
    ys = columns // points
    per_step = points // plane_steps
    late = X_STEPS + plane_steps
    steps = late + X_STEPS
    job = step // steps if jobs > 1 else 0
    at = step % steps if jobs > 1 else step

    def span_of(chunk):
        start = chunk * columns
        return pl.ds(start if isinstance(chunk, int) else pl.multiple_of(start, columns), columns)

    def fetch(name, chunk):
        place, span = names.index(name), span_of(chunk)
        return pltpu.make_async_copy(
            far[name].at[:, span], near.at[place, :, span], sems.at[place, chunk]
        )

    def fetch_kernel(part):
        span = pl.ds(part * per_step, per_step)
        return pltpu.make_async_copy(
            kernel_ref.at[span], near_kernel.at[span], kernel_sems.at[part]
        )

    def give(name, chunk):
        span = span_of(chunk)
        source = near_out.at[jobs if name == "for_b" else int(name[-1])]
        if "halves" in has and name != "for_b":
            rows = pl.ds(points - FAR_ROWS, FAR_ROWS) if name == "low_a0" else pl.ds(0, points - FAR_ROWS)
            source = source.at[rows, span]
        else:
            source = source.at[:, span]
        return pltpu.make_async_copy(
            source, out_refs[name].at[:, span], out_sems.at[outs.index(name), chunk]
        )

    def here(name, chunk):
        place = job if name == "a" else names.index(name)
        return near[place, :, span_of(chunk)]

    def when_job(number, work):
        if jobs > 1:
            pl.when(job == number)(work)
        elif number == 0:
            work()

    @pl.when(active & (step == 0))
    def start_first():
        for chunk in range(2):
            for name in ("a0", "b"):
                fetch(name, chunk).start()

    @pl.when(active & (step + 2 < X_STEPS))
    def start_next():
        for name in ("a0", "b"):
            fetch(name, step + 2).start()

    @pl.when(active & (step == 0))
    def start_kernel():
        for part in range(plane_steps):
            fetch_kernel(part).start()

    @pl.when(active & (step == X_STEPS))
    def start_rest():
        for chunk in range(X_STEPS):
            for name in a_names[1:] + ["sum_a"] * ("sum_a" in has):
                fetch(name, chunk).start()

    def lanes_apart(block):
        tail = jnp.zeros((points, LANES), jnp.float32)
        wide = jnp.concatenate([block, tail], 1)
        rows = [wide[:, q * points:q * points + LANES] for q in range(ys)]
        return jnp.swapaxes(jnp.stack(rows, 0), 0, 1)

    def lanes_together(block):
        block = jnp.swapaxes(block, 0, 1)
        return jnp.concatenate([block[q][:, :points] for q in range(ys)], 1)

    def side_by_side(block):
        return jnp.concatenate([block[i] for i in range(per_step)], 1)

    @pl.when(active & (at < X_STEPS))
    def forward_x():
        chunk = at

        def first_waits():
            fetch("a0", chunk).wait()
            fetch("b", chunk).wait()

        when_job(0, first_waits)
        for number in range(1, jobs):
            when_job(number, fetch(a_names[number], chunk).wait)
        spectrum = from_left(left_ref[...], here("a", chunk) * here("b", chunk))
        start = pl.multiple_of(chunk * ys, ys)
        held[:, pl.ds(start, ys), :] = lanes_apart(spectrum)

    @pl.when(active & (at >= X_STEPS) & (at < late))
    def planes():
        part = at - X_STEPS
        left = left_ref[...]
        right = right_ref[...]
        first = part * per_step
        when_job(0, lambda: fetch_kernel(part).wait())
        block = held[pl.ds(first, per_step)].reshape(per_step * points, LANES)
        block = from_right(block, right).reshape(per_step, points, LANES)
        wide = from_left(left, side_by_side(block))
        wide = from_left(left, wide * side_by_side(near_kernel[pl.ds(first, per_step)]))
        block = jnp.concatenate(
            [wide[:, i * LANES:(i + 1) * LANES] for i in range(per_step)], 0
        )
        block = from_right(block, right)
        held[pl.ds(first, per_step)] = block.reshape(per_step, points, LANES)

    @pl.when(active & (at >= late))
    def inverse_x():
        chunk = at - late
        start = pl.multiple_of(chunk * ys, ys)
        if "sum_a" in has:
            fetch("sum_a", chunk).wait()
        block = lanes_together(held[:, pl.ds(start, ys), :])
        potential = from_left(left_ref[...], block)
        for_a = here("b", chunk) * potential
        if "sum_a" in has:
            for_a = for_a + jnp.where(with_sum, here("sum_a", chunk), 0.0)
        near_out[job, :, span_of(chunk)] = for_a
        if "for_b" in has:
            for_b = here("a", chunk) * potential
            if jobs > 1:
                for_b = for_b + jnp.where(job > 0, near_out[jobs, :, span_of(chunk)], 0.0)
            near_out[jobs, :, span_of(chunk)] = for_b

        def give_all(number):
            for name in outs:
                if number == (jobs - 1 if name == "for_b" else int(name[-1])):
                    give(name, chunk).start()

        for number in range(jobs):
            when_job(number, functools.partial(give_all, number))

    @pl.when(active & (step == jobs * steps - 1))
    def wait_outs():
        for chunk in range(X_STEPS):
            for name in outs:
                give(name, chunk).wait()


def pair_terms(
    flags, slot, a, b, constants, sum_a=None, for_b=False, halves=False, in_place=False, then=None,
    plane_steps=2,
):
    points, plane = b.shape
    kernel, left, right = constants
    jobs = len(a)
    blocks = [*a, b] + [sum_a] * (sum_a is not None)
    waited = [] if then is None else [then]
    has = ["sum_a"] * (sum_a is not None) + ["for_b"] * for_b + ["halves"] * halves + ["then"] * len(waited)
    rows = ([points - FAR_ROWS, FAR_ROWS] if halves else [points] * jobs) + [points] * for_b
    anywhere = pl.BlockSpec(memory_space=pl.ANY)
    return pl.pallas_call(
        functools.partial(pair_body, points, slot, jobs, plane_steps, has),
        grid=(jobs * (2 * X_STEPS + plane_steps),),
        in_specs=[pl.BlockSpec(memory_space=pltpu.SMEM)]
        + [anywhere] * (len(blocks) + len(waited) + 1)
        + [pl.BlockSpec(table.shape, lambda i: (0, 0)) for table in (left, right)],
        out_specs=[anywhere] * len(rows),
        out_shape=[jax.ShapeDtypeStruct((n, plane), jnp.float32) for n in rows],
        input_output_aliases={3: 0} if in_place else {},
        scratch_shapes=[
            pltpu.VMEM((points, points, LANES), jnp.float32),
            pltpu.VMEM((len(blocks), points, plane), jnp.float32),
            pltpu.VMEM((points, points, LANES), jnp.float32),
            pltpu.VMEM((jobs + for_b, points, plane), jnp.float32),
            pltpu.SemaphoreType.DMA((len(blocks), X_STEPS)),
            pltpu.SemaphoreType.DMA((plane_steps,)),
            pltpu.SemaphoreType.DMA((len(rows), X_STEPS)),
        ],
        compiler_params=pltpu.CompilerParams(vmem_limit_bytes=63 * 2**20),
        cost_estimate=pl.CostEstimate(
            flops=100_000_000, bytes_accessed=1_000_000, transcendentals=0
        ),
        name="pair_terms",
    )(flags, *blocks, *waited, kernel, left, right)


def copy_body(flags_ref, kernel_ref, left_ref, right_ref, block_ref, first_ref, second_ref):
    del flags_ref, kernel_ref, left_ref, right_ref
    first_ref[...] = block_ref[...]
    second_ref[...] = block_ref[...]


def copied(flags, constants, block):
    points, plane = block.shape
    part = pl.BlockSpec((points, plane // X_STEPS), lambda i: (0, i))
    return pl.pallas_call(
        copy_body,
        grid=(X_STEPS,),
        in_specs=[
            pl.BlockSpec(memory_space=pltpu.SMEM),
            *[pl.BlockSpec(memory_space=pl.ANY)] * 3,
            part,
        ],
        out_specs=[part, part],
        out_shape=[jax.ShapeDtypeStruct(block.shape, block.dtype)] * 2,
        compiler_params=pltpu.CompilerParams(vmem_limit_bytes=63 * 2**20),
        name="copied",
    )(flags, *constants, block)


def gate_body(*refs):
    del refs


def gate(token, kernel, partner, block):
    anywhere = pl.BlockSpec(memory_space=pl.ANY)
    return pl.pallas_call(
        gate_body,
        in_specs=[anywhere] * 4,
        out_specs=[anywhere] * 2,
        out_shape=[
            jax.ShapeDtypeStruct(kernel.shape, kernel.dtype),
            jax.ShapeDtypeStruct(block.shape, block.dtype),
        ],
        input_output_aliases={1: 0, 3: 1},
        compiler_params=pltpu.CompilerParams(vmem_limit_bytes=63 * 2**20),
        name="gate",
    )(token, kernel, partner, block)


def hold_body(*refs):
    del refs


def hold(block, *then):
    anywhere = pl.BlockSpec(memory_space=pl.ANY)
    return pl.pallas_call(
        hold_body,
        in_specs=[anywhere] * (1 + len(then)),
        out_specs=anywhere,
        out_shape=jax.ShapeDtypeStruct(block.shape, block.dtype),
        input_output_aliases={0: 0},
        compiler_params=pltpu.CompilerParams(vmem_limit_bytes=63 * 2**20),
        name="hold",
    )(block, *then)


def settle_body(wanted, count, flags_ref, *refs):
    parts, (out_ref, near, sems) = refs[:count], refs[count + 1:]

    @pl.when(flags_ref[RESULT] == wanted)
    def move():
        copies = []
        start = 0
        for part in parts:
            for row in range(0, part.shape[0], SETTLE_ROWS):
                rows = pl.ds(start + row, SETTLE_ROWS)
                place = (start + row) // SETTLE_ROWS
                source = part.at[pl.ds(row, SETTLE_ROWS), :]
                copies.append((
                    pltpu.make_async_copy(source, near.at[rows, :], sems.at[0, place]),
                    pltpu.make_async_copy(near.at[rows, :], out_ref.at[rows, :], sems.at[1, place]),
                ))
            start += part.shape[0]
        for inward, outward in copies:
            inward.start()
        for inward, outward in copies:
            inward.wait()
            outward.start()
        for inward, outward in copies:
            outward.wait()


def settle(flags, wanted, parts, own_sum):
    anywhere = pl.BlockSpec(memory_space=pl.ANY)
    count = len(parts)
    return pl.pallas_call(
        functools.partial(settle_body, wanted, count),
        in_specs=[pl.BlockSpec(memory_space=pltpu.SMEM)] + [anywhere] * (count + 1),
        out_specs=anywhere,
        out_shape=jax.ShapeDtypeStruct(own_sum.shape, own_sum.dtype),
        input_output_aliases={count + 1: 0},
        scratch_shapes=[
            pltpu.VMEM(own_sum.shape, own_sum.dtype),
            pltpu.SemaphoreType.DMA((2, own_sum.shape[0] // SETTLE_ROWS)),
        ],
        compiler_params=pltpu.CompilerParams(vmem_limit_bytes=63 * 2**20),
        name="settle",
    )(flags, *parts, own_sum)


def both_halves(*pairs):
    return list(pairs) + [(15 - source, 15 - target) for source, target in pairs]


CROSSING = both_halves((3, 14), (4, 9))
PARTNERS = both_halves((8, 14), (15, 9), (9, 11), (14, 12))
ARRIVED = both_halves((14, 2), (9, 5))
SINGLES = both_halves((5, 10), (2, 13))
BESIDE = both_halves((13, 14), (10, 9))
DIRECT = both_halves((15, 10), (8, 13))
TURNED = both_halves((11, 14), (12, 9))
HOME_ACROSS = both_halves((9, 4), (14, 3))
HOME_FAR = both_halves((9, 15), (14, 8))
HOME_TURN = both_halves((9, 11), (14, 12))
HOME_TURNED = both_halves((11, 15), (12, 8))
RESULT = 10
FLAGS = {i: (1, 0, 1, 1, 0, 0, 0, 0, 1, 1, 0) for i in (9, 14, 6, 1)}
FLAGS.update({i: (0, 0, 0, 0, 1, 0, 1, 1, 0, 0, 0) for i in (10, 13, 5, 2)})
FLAGS.update({i: (0,) * RESULT + (1,) for i in (3, 4, 11, 12)})
FLAGS.update({i: (0,) * RESULT + (2,) for i in (15, 8, 0, 7)})


def sixteen_bands(orbitals, constants):
    def send(value, pairs):
        return lax.ppermute(value[None], "band", pairs)[0]

    kernel, left, right = constants
    own = orbitals[0]
    flags = jnp.asarray([FLAGS[i] for i in range(16)], jnp.int32)
    flags = flags[lax.axis_index("band")]
    pair = functools.partial(pair_terms, flags)
    crossed = send(own, CROSSING)
    partner = send(own, PARTNERS)
    own_copy, direct_copy = copied(flags, constants, own)
    token = crossed[:8, :LANES] + own_copy[:8, :LANES]
    direct = send(direct_copy, DIRECT)
    kernel, held_back = gate(send(token, ARRIVED), kernel, partner, own_copy)
    constants = (kernel, left, right)
    beside = send(held_back, BESIDE)
    single = send(held_back, SINGLES)

    partner_sum, own_sum, crossed_sum = pair(
        0, [partner, own], crossed, constants, for_b=True, then=direct, plane_steps=1
    )
    home = send(crossed_sum, HOME_ACROSS)
    partner = hold(partner, own_sum)
    turned = send(partner, TURNED)
    top, bottom = pair(1, [partner], beside, constants, sum_a=partner_sum, halves=True, plane_steps=1)
    bottom = send(bottom, HOME_TURN)
    top = send(top, HOME_FAR)
    (own_sum,) = pair(2, [own], direct, constants, sum_a=own_sum, in_place=True)
    (own_sum,) = pair(3, [own], single, constants, sum_a=own_sum, in_place=True)
    bottom = send(hold(bottom, own_sum), HOME_TURNED)
    own_sum = settle(flags, 1, [home], own_sum)
    (own_sum,) = pair(4, [own], turned, constants, sum_a=own_sum, in_place=True)
    return settle(flags, 2, [top, bottom], own_sum)[None]


def any_bands(orbitals, constants):
    own = orbitals[0]
    flags = jnp.ones((4,), jnp.int32)
    lower = from_behind(orbitals, "band", OFFSET)[0]
    upper = from_behind(orbitals, "band", -OFFSET)[0]
    (total,) = pair_terms(flags, 0, [own], lower, constants)
    return pair_terms(flags, 1, [own], upper, constants, sum_a=total)[0][None]


def local(bands, orbitals):
    points = orbitals.shape[1]
    constants = (screened_kernel(points), *hartley_tables(points))
    if bands == 16:
        return sixteen_bands(orbitals, constants)
    return any_bands(orbitals, constants)


def solution(mesh):
    return jax.shard_map(
        functools.partial(local, mesh.shape["band"]),
        mesh=mesh,
        in_specs=(P(("groups", "band"), None, None),),
        out_specs=P(("groups", "band"), None, None),
        check_vma=False,
    )
```

```python
import functools
import math

import jax
import jax.numpy as jnp
import numpy as np
from jax import lax
from jax.experimental import pallas as pl
from jax.experimental.pallas import tpu as pltpu
from jax.sharding import PartitionSpec as P

OFFSET = 5
screening = 5.44
LANES = 128
X_STEPS = 3
SETTLE_STEPS = 6
FAR_ROWS = 32


def from_behind(value, axis, by):
    count = lax.axis_size(axis)
    return lax.ppermute(value, axis, [(i, (i + by) % count) for i in range(count)])


def screened_kernel(points):
    signed = jnp.arange(LANES, dtype=jnp.int32)
    inside = signed < points
    signed = jnp.where(signed >= points // 2, signed - points, signed)
    wavenumber = signed.astype(jnp.float32) * (2.0 * math.pi / points)
    squared = (
        wavenumber[:points, None, None] ** 2
        + wavenumber[None, :points, None] ** 2
        + wavenumber[None, None, :] ** 2
    )
    screen_rate = screening / points
    finite = jnp.where(squared > 0.0, squared, 1.0)
    screened = 4.0 * math.pi / finite * -jnp.expm1(-finite / (4.0 * screen_rate * screen_rate))
    kernel = jnp.where(squared > 0.0, screened, math.pi / (screen_rate * screen_rate))
    return jnp.where(inside, kernel / -float(points * points * points), 0.0)


def hartley_tables(points):
    counter = np.arange(points)
    angles = 2.0 * np.pi * (counter[:, None] * counter[None, :] % points) / points
    table = np.cos(angles) + np.sin(angles)
    high = table.astype(jnp.bfloat16)
    low = (table - high.astype(np.float64)).astype(jnp.bfloat16)
    left = np.zeros((2 * points, 2 * points), jnp.bfloat16)
    left[:points, :points] = high
    left[:points, points:] = high
    left[points:, :points] = low
    right = np.zeros((2 * LANES, 2 * LANES), jnp.bfloat16)
    right[:points, :points] = high
    right[:points, LANES:LANES + points] = low
    right[LANES:LANES + points, :points] = high
    return jnp.asarray(left), jnp.asarray(right)


def two_terms(value):
    high = value.astype(jnp.bfloat16)
    low = (value - high.astype(jnp.float32)).astype(jnp.bfloat16)
    return high, low


def from_left(left, value):
    half = value.shape[0]
    terms = jnp.concatenate(two_terms(value), 0)
    out = jnp.dot(left, terms, preferred_element_type=jnp.float32)
    return out[:half] + out[half:]


def from_right(value, right):
    out = jnp.dot(jnp.concatenate(two_terms(value), 1), right, preferred_element_type=jnp.float32)
    return out[:, :LANES] + out[:, LANES:]


def pair_body(points, slot, jobs, plane_steps, has, *refs):
    refs = list(refs)
    flags_ref = refs.pop(0)
    a_names = ["a%d" % job for job in range(jobs)]
    names = a_names + ["b"] + ["sum_a"] * ("sum_a" in has)
    far = {name: refs.pop(0) for name in names}
    if "then" in has:
        refs.pop(0)
    kernel_ref, left_ref, right_ref = refs.pop(0), refs.pop(0), refs.pop(0)
    outs = ["for_a%d" % job for job in range(jobs)]
    if "halves" in has:
        outs.append("low_a0")
    if "for_b" in has:
        outs.append("for_b")
    out_refs = {name: refs.pop(0) for name in outs}
    held, near, near_kernel, near_out, sems, kernel_sems, out_sems = refs
    step = pl.program_id(0)
    active = flags_ref[2 * slot] == 1
    with_sum = flags_ref[2 * slot + 1] == 1
    columns = near.shape[2] // X_STEPS
    ys = columns // points
    per_step = points // plane_steps
    late = X_STEPS + plane_steps
    steps = late + X_STEPS
    job = step // steps if jobs > 1 else 0
    at = step % steps if jobs > 1 else step

    def span_of(chunk):
        start = chunk * columns
        return pl.ds(start if isinstance(chunk, int) else pl.multiple_of(start, columns), columns)

    def fetch(name, chunk):
        place, span = names.index(name), span_of(chunk)
        return pltpu.make_async_copy(
            far[name].at[:, span], near.at[place, :, span], sems.at[place, chunk]
        )

    def fetch_kernel(part):
        span = pl.ds(part * per_step, per_step)
        return pltpu.make_async_copy(
            kernel_ref.at[span], near_kernel.at[span], kernel_sems.at[part]
        )

    def give(name, chunk):
        span = span_of(chunk)
        source = near_out.at[jobs if name == "for_b" else int(name[-1])]
        if "halves" in has and name != "for_b":
            rows = pl.ds(points - FAR_ROWS, FAR_ROWS) if name == "low_a0" else pl.ds(0, points - FAR_ROWS)
            source = source.at[rows, span]
        else:
            source = source.at[:, span]
        return pltpu.make_async_copy(
            source, out_refs[name].at[:, span], out_sems.at[outs.index(name), chunk]
        )

    def here(name, chunk):
        place = job if name == "a" else names.index(name)
        return near[place, :, span_of(chunk)]

    def when_job(number, work):
        if jobs > 1:
            pl.when(job == number)(work)
        elif number == 0:
            work()

    @pl.when(active & (step == 0))
    def start_first():
        for chunk in range(2):
            for name in ("a0", "b"):
                fetch(name, chunk).start()

    @pl.when(active & (step + 2 < X_STEPS))
    def start_next():
        for name in ("a0", "b"):
            fetch(name, step + 2).start()

    @pl.when(active & (step == 0))
    def start_kernel():
        for part in range(plane_steps):
            fetch_kernel(part).start()

    @pl.when(active & (step == X_STEPS))
    def start_rest():
        for chunk in range(X_STEPS):
            for name in a_names[1:] + ["sum_a"] * ("sum_a" in has):
                fetch(name, chunk).start()

    def lanes_apart(block):
        tail = jnp.zeros((points, LANES), jnp.float32)
        wide = jnp.concatenate([block, tail], 1)
        rows = [wide[:, q * points:q * points + LANES] for q in range(ys)]
        return jnp.swapaxes(jnp.stack(rows, 0), 0, 1)

    def lanes_together(block):
        block = jnp.swapaxes(block, 0, 1)
        return jnp.concatenate([block[q][:, :points] for q in range(ys)], 1)

    def side_by_side(block):
        return jnp.concatenate([block[i] for i in range(per_step)], 1)

    @pl.when(active & (at < X_STEPS))
    def forward_x():
        chunk = at

        def first_waits():
            fetch("a0", chunk).wait()
            fetch("b", chunk).wait()

        when_job(0, first_waits)
        for number in range(1, jobs):
            when_job(number, fetch(a_names[number], chunk).wait)
        spectrum = from_left(left_ref[...], here("a", chunk) * here("b", chunk))
        start = pl.multiple_of(chunk * ys, ys)
        held[:, pl.ds(start, ys), :] = lanes_apart(spectrum)

    @pl.when(active & (at >= X_STEPS) & (at < late))
    def planes():
        part = at - X_STEPS
        left = left_ref[...]
        right = right_ref[...]
        first = part * per_step
        when_job(0, lambda: fetch_kernel(part).wait())
        block = held[pl.ds(first, per_step)].reshape(per_step * points, LANES)
        block = from_right(block, right).reshape(per_step, points, LANES)
        wide = from_left(left, side_by_side(block))
        wide = from_left(left, wide * side_by_side(near_kernel[pl.ds(first, per_step)]))
        block = jnp.concatenate(
            [wide[:, i * LANES:(i + 1) * LANES] for i in range(per_step)], 0
        )
        block = from_right(block, right)
        held[pl.ds(first, per_step)] = block.reshape(per_step, points, LANES)

    @pl.when(active & (at >= late))
    def inverse_x():
        chunk = at - late
        start = pl.multiple_of(chunk * ys, ys)
        if "sum_a" in has:
            fetch("sum_a", chunk).wait()
        block = lanes_together(held[:, pl.ds(start, ys), :])
        potential = from_left(left_ref[...], block)
        for_a = here("b", chunk) * potential
        if "sum_a" in has:
            for_a = for_a + jnp.where(with_sum, here("sum_a", chunk), 0.0)
        near_out[job, :, span_of(chunk)] = for_a
        if "for_b" in has:
            for_b = here("a", chunk) * potential
            if jobs > 1:
                for_b = for_b + jnp.where(job > 0, near_out[jobs, :, span_of(chunk)], 0.0)
            near_out[jobs, :, span_of(chunk)] = for_b

        def give_all(number):
            for name in outs:
                if number == (jobs - 1 if name == "for_b" else int(name[-1])):
                    give(name, chunk).start()

        for number in range(jobs):
            when_job(number, functools.partial(give_all, number))

    @pl.when(active & (step == jobs * steps - 1))
    def wait_outs():
        for chunk in range(X_STEPS):
            for name in outs:
                give(name, chunk).wait()


def pair_terms(
    flags, slot, a, b, constants, sum_a=None, for_b=False, halves=False, in_place=False, then=None,
    plane_steps=2,
):
    points, plane = b.shape
    kernel, left, right = constants
    jobs = len(a)
    blocks = [*a, b] + [sum_a] * (sum_a is not None)
    waited = [] if then is None else [then]
    has = ["sum_a"] * (sum_a is not None) + ["for_b"] * for_b + ["halves"] * halves + ["then"] * len(waited)
    rows = ([points - FAR_ROWS, FAR_ROWS] if halves else [points] * jobs) + [points] * for_b
    anywhere = pl.BlockSpec(memory_space=pl.ANY)
    return pl.pallas_call(
        functools.partial(pair_body, points, slot, jobs, plane_steps, has),
        grid=(jobs * (2 * X_STEPS + plane_steps),),
        in_specs=[pl.BlockSpec(memory_space=pltpu.SMEM)]
        + [anywhere] * (len(blocks) + len(waited) + 1)
        + [pl.BlockSpec(table.shape, lambda i: (0, 0)) for table in (left, right)],
        out_specs=[anywhere] * len(rows),
        out_shape=[jax.ShapeDtypeStruct((n, plane), jnp.float32) for n in rows],
        input_output_aliases={3: 0} if in_place else {},
        scratch_shapes=[
            pltpu.VMEM((points, points, LANES), jnp.float32),
            pltpu.VMEM((len(blocks), points, plane), jnp.float32),
            pltpu.VMEM((points, points, LANES), jnp.float32),
            pltpu.VMEM((jobs + for_b, points, plane), jnp.float32),
            pltpu.SemaphoreType.DMA((len(blocks), X_STEPS)),
            pltpu.SemaphoreType.DMA((plane_steps,)),
            pltpu.SemaphoreType.DMA((len(rows), X_STEPS)),
        ],
        compiler_params=pltpu.CompilerParams(vmem_limit_bytes=63 * 2**20),
        cost_estimate=pl.CostEstimate(
            flops=100_000_000, bytes_accessed=1_000_000, transcendentals=0
        ),
        name="pair_terms",
    )(flags, *blocks, *waited, kernel, left, right)


def copy_body(flags_ref, kernel_ref, left_ref, right_ref, block_ref, first_ref, second_ref):
    del flags_ref, kernel_ref, left_ref, right_ref
    first_ref[...] = block_ref[...]
    second_ref[...] = block_ref[...]


def copied(flags, constants, block):
    points, plane = block.shape
    part = pl.BlockSpec((points, plane // X_STEPS), lambda i: (0, i))
    return pl.pallas_call(
        copy_body,
        grid=(X_STEPS,),
        in_specs=[
            pl.BlockSpec(memory_space=pltpu.SMEM),
            *[pl.BlockSpec(memory_space=pl.ANY)] * 3,
            part,
        ],
        out_specs=[part, part],
        out_shape=[jax.ShapeDtypeStruct(block.shape, block.dtype)] * 2,
        compiler_params=pltpu.CompilerParams(vmem_limit_bytes=63 * 2**20),
        name="copied",
    )(flags, *constants, block)


def gate_body(*refs):
    del refs


def gate(token, kernel, partner, block):
    anywhere = pl.BlockSpec(memory_space=pl.ANY)
    return pl.pallas_call(
        gate_body,
        in_specs=[anywhere] * 4,
        out_specs=[anywhere] * 2,
        out_shape=[
            jax.ShapeDtypeStruct(kernel.shape, kernel.dtype),
            jax.ShapeDtypeStruct(block.shape, block.dtype),
        ],
        input_output_aliases={1: 0, 3: 1},
        compiler_params=pltpu.CompilerParams(vmem_limit_bytes=63 * 2**20),
        name="gate",
    )(token, kernel, partner, block)


def hold_body(*refs):
    del refs


def hold(block, *then):
    anywhere = pl.BlockSpec(memory_space=pl.ANY)
    return pl.pallas_call(
        hold_body,
        in_specs=[anywhere] * (1 + len(then)),
        out_specs=anywhere,
        out_shape=jax.ShapeDtypeStruct(block.shape, block.dtype),
        input_output_aliases={0: 0},
        compiler_params=pltpu.CompilerParams(vmem_limit_bytes=63 * 2**20),
        name="hold",
    )(block, *then)


def settle_body(wanted, count, flags_ref, *refs):
    parts, (out_ref, near, sems) = refs[:count], refs[count + 1:]
    columns = out_ref.shape[1] // SETTLE_STEPS

    @pl.when(flags_ref[RESULT] == wanted)
    def move():
        copies = []
        for i in range(SETTLE_STEPS):
            span = pl.ds(i * columns, columns)
            start = 0
            for j, part in enumerate(parts):
                rows = pl.ds(start, part.shape[0])
                start += part.shape[0]
                copies.append((
                    pltpu.make_async_copy(part.at[:, span], near.at[rows, span], sems.at[0, j, i]),
                    pltpu.make_async_copy(near.at[rows, span], out_ref.at[rows, span], sems.at[1, j, i]),
                ))
        for inward, outward in copies:
            inward.start()
        for inward, outward in copies:
            inward.wait()
            outward.start()
        for inward, outward in copies:
            outward.wait()


def settle(flags, wanted, parts, own_sum):
    anywhere = pl.BlockSpec(memory_space=pl.ANY)
    count = len(parts)
    return pl.pallas_call(
        functools.partial(settle_body, wanted, count),
        in_specs=[pl.BlockSpec(memory_space=pltpu.SMEM)] + [anywhere] * (count + 1),
        out_specs=anywhere,
        out_shape=jax.ShapeDtypeStruct(own_sum.shape, own_sum.dtype),
        input_output_aliases={count + 1: 0},
        scratch_shapes=[
            pltpu.VMEM(own_sum.shape, own_sum.dtype),
            pltpu.SemaphoreType.DMA((2, count, SETTLE_STEPS)),
        ],
        compiler_params=pltpu.CompilerParams(vmem_limit_bytes=63 * 2**20),
        name="settle",
    )(flags, *parts, own_sum)


def both_halves(*pairs):
    return list(pairs) + [(15 - source, 15 - target) for source, target in pairs]


CROSSING = both_halves((3, 14), (4, 9))
PARTNERS = both_halves((8, 14), (15, 9), (9, 11), (14, 12))
ARRIVED = both_halves((14, 2), (9, 5))
SINGLES = both_halves((5, 10), (2, 13))
BESIDE = both_halves((13, 14), (10, 9))
DIRECT = both_halves((15, 10), (8, 13))
TURNED = both_halves((11, 14), (12, 9))
HOME_ACROSS = both_halves((9, 4), (14, 3))
HOME_FAR = both_halves((9, 15), (14, 8))
HOME_TURN = both_halves((9, 11), (14, 12))
HOME_TURNED = both_halves((11, 15), (12, 8))
RESULT = 10
FLAGS = {i: (1, 0, 1, 1, 0, 0, 0, 0, 1, 1, 0) for i in (9, 14, 6, 1)}
FLAGS.update({i: (0, 0, 0, 0, 1, 0, 1, 1, 0, 0, 0) for i in (10, 13, 5, 2)})
FLAGS.update({i: (0,) * RESULT + (1,) for i in (3, 4, 11, 12)})
FLAGS.update({i: (0,) * RESULT + (2,) for i in (15, 8, 0, 7)})


def sixteen_bands(orbitals, constants):
    def send(value, pairs):
        return lax.ppermute(value[None], "band", pairs)[0]

    kernel, left, right = constants
    own = orbitals[0]
    flags = jnp.asarray([FLAGS[i] for i in range(16)], jnp.int32)
    flags = flags[lax.axis_index("band")]
    pair = functools.partial(pair_terms, flags)
    crossed = send(own, CROSSING)
    partner = send(own, PARTNERS)
    own_copy, direct_copy = copied(flags, constants, own)
    token = hold(own_copy[:8, :LANES], crossed)
    direct = send(direct_copy, DIRECT)
    kernel, held_back = gate(send(token, ARRIVED), kernel, partner, own_copy)
    constants = (kernel, left, right)
    beside = send(held_back, BESIDE)
    single = send(held_back, SINGLES)

    partner_sum, own_sum, crossed_sum = pair(
        0, [partner, own], crossed, constants, for_b=True, then=direct, plane_steps=1
    )
    home = send(crossed_sum, HOME_ACROSS)
    partner = hold(partner, own_sum)
    turned = send(partner, TURNED)
    top, bottom = pair(1, [partner], beside, constants, sum_a=partner_sum, halves=True, plane_steps=1)
    bottom = send(bottom, HOME_TURN)
    top = send(top, HOME_FAR)
    (own_sum,) = pair(2, [own], direct, constants, sum_a=own_sum, in_place=True)
    (own_sum,) = pair(3, [own], single, constants, sum_a=own_sum, in_place=True)
    bottom = send(hold(bottom, own_sum), HOME_TURNED)
    own_sum = settle(flags, 1, [home], own_sum)
    (own_sum,) = pair(4, [own], turned, constants, sum_a=own_sum, in_place=True)
    return settle(flags, 2, [top, bottom], own_sum)[None]


def any_bands(orbitals, constants):
    own = orbitals[0]
    flags = jnp.ones((4,), jnp.int32)
    lower = from_behind(orbitals, "band", OFFSET)[0]
    upper = from_behind(orbitals, "band", -OFFSET)[0]
    (total,) = pair_terms(flags, 0, [own], lower, constants)
    return pair_terms(flags, 1, [own], upper, constants, sum_a=total)[0][None]


def local(bands, orbitals):
    points = orbitals.shape[1]
    constants = (screened_kernel(points), *hartley_tables(points))
    if bands == 16:
        return sixteen_bands(orbitals, constants)
    return any_bands(orbitals, constants)


def solution(mesh):
    return jax.shard_map(
        functools.partial(local, mesh.shape["band"]),
        mesh=mesh,
        in_specs=(P(("groups", "band"), None, None),),
        out_specs=P(("groups", "band"), None, None),
        check_vma=False,
    )
```

```python
import functools
import math

import jax
import jax.numpy as jnp
import numpy as np
from jax import lax
from jax.experimental import pallas as pl
from jax.experimental.pallas import tpu as pltpu
from jax.sharding import PartitionSpec as P

OFFSET = 5
screening = 5.44
LANES = 128
X_STEPS = 3
SETTLE_STEPS = 6
FAR_ROWS = 32


def from_behind(value, axis, by):
    count = lax.axis_size(axis)
    return lax.ppermute(value, axis, [(i, (i + by) % count) for i in range(count)])


def screened_kernel(points):
    signed = jnp.arange(LANES, dtype=jnp.int32)
    inside = signed < points
    signed = jnp.where(signed >= points // 2, signed - points, signed)
    wavenumber = signed.astype(jnp.float32) * (2.0 * math.pi / points)
    squared = (
        wavenumber[:points, None, None] ** 2
        + wavenumber[None, :points, None] ** 2
        + wavenumber[None, None, :] ** 2
    )
    screen_rate = screening / points
    finite = jnp.where(squared > 0.0, squared, 1.0)
    screened = 4.0 * math.pi / finite * -jnp.expm1(-finite / (4.0 * screen_rate * screen_rate))
    kernel = jnp.where(squared > 0.0, screened, math.pi / (screen_rate * screen_rate))
    return jnp.where(inside, kernel / -float(points * points * points), 0.0)


def hartley_tables(points):
    counter = np.arange(points)
    angles = 2.0 * np.pi * (counter[:, None] * counter[None, :] % points) / points
    table = np.cos(angles) + np.sin(angles)
    high = table.astype(jnp.bfloat16)
    low = (table - high.astype(np.float64)).astype(jnp.bfloat16)
    left = np.zeros((2 * points, 2 * points), jnp.bfloat16)
    left[:points, :points] = high
    left[:points, points:] = high
    left[points:, :points] = low
    right = np.zeros((2 * LANES, 2 * LANES), jnp.bfloat16)
    right[:points, :points] = high
    right[:points, LANES:LANES + points] = low
    right[LANES:LANES + points, :points] = high
    return jnp.asarray(left), jnp.asarray(right)


def two_terms(value):
    high = value.astype(jnp.bfloat16)
    low = (value - high.astype(jnp.float32)).astype(jnp.bfloat16)
    return high, low


def from_left(left, value):
    half = value.shape[0]
    terms = jnp.concatenate(two_terms(value), 0)
    out = jnp.dot(left, terms, preferred_element_type=jnp.float32)
    return out[:half] + out[half:]


def from_right(value, right):
    out = jnp.dot(jnp.concatenate(two_terms(value), 1), right, preferred_element_type=jnp.float32)
    return out[:, :LANES] + out[:, LANES:]


def pair_body(points, slot, jobs, plane_steps, has, *refs):
    refs = list(refs)
    flags_ref = refs.pop(0)
    a_names = ["a%d" % job for job in range(jobs)]
    names = a_names + ["b"] + ["sum_a"] * ("sum_a" in has)
    far = {name: refs.pop(0) for name in names}
    if "then" in has:
        refs.pop(0)
    kernel_ref, left_ref, right_ref = refs.pop(0), refs.pop(0), refs.pop(0)
    outs = ["for_a%d" % job for job in range(jobs)]
    if "halves" in has:
        outs.append("low_a0")
    if "for_b" in has:
        outs.append("for_b")
    out_refs = {name: refs.pop(0) for name in outs}
    held, near, near_kernel, near_out, sems, kernel_sems, out_sems = refs
    step = pl.program_id(0)
    active = flags_ref[2 * slot] == 1
    with_sum = flags_ref[2 * slot + 1] == 1
    columns = near.shape[2] // X_STEPS
    ys = columns // points
    per_step = points // plane_steps
    late = X_STEPS + plane_steps
    steps = late + X_STEPS
    job = step // steps if jobs > 1 else 0
    at = step % steps if jobs > 1 else step

    def span_of(chunk):
        start = chunk * columns
        return pl.ds(start if isinstance(chunk, int) else pl.multiple_of(start, columns), columns)

    def fetch(name, chunk):
        place, span = names.index(name), span_of(chunk)
        return pltpu.make_async_copy(
            far[name].at[:, span], near.at[place, :, span], sems.at[place, chunk]
        )

    def fetch_kernel(part):
        span = pl.ds(part * per_step, per_step)
        return pltpu.make_async_copy(
            kernel_ref.at[span], near_kernel.at[span], kernel_sems.at[part]
        )

    def give(name, chunk):
        span = span_of(chunk)
        source = near_out.at[jobs if name == "for_b" else int(name[-1])]
        if "halves" in has and name != "for_b":
            rows = pl.ds(points - FAR_ROWS, FAR_ROWS) if name == "low_a0" else pl.ds(0, points - FAR_ROWS)
            source = source.at[rows, span]
        else:
            source = source.at[:, span]
        return pltpu.make_async_copy(
            source, out_refs[name].at[:, span], out_sems.at[outs.index(name), chunk]
        )

    def here(name, chunk):
        place = job if name == "a" else names.index(name)
        return near[place, :, span_of(chunk)]

    def when_job(number, work):
        if jobs > 1:
            pl.when(job == number)(work)
        elif number == 0:
            work()

    @pl.when(active & (step == 0))
    def start_first():
        for chunk in range(2):
            for name in ("a0", "b"):
                fetch(name, chunk).start()

    @pl.when(active & (step + 2 < X_STEPS))
    def start_next():
        for name in ("a0", "b"):
            fetch(name, step + 2).start()

    @pl.when(active & (step == 0))
    def start_kernel():
        for part in range(plane_steps):
            fetch_kernel(part).start()

    @pl.when(active & (step == X_STEPS))
    def start_rest():
        for chunk in range(X_STEPS):
            for name in a_names[1:] + ["sum_a"] * ("sum_a" in has):
                fetch(name, chunk).start()

    def lanes_apart(block):
        tail = jnp.zeros((points, LANES), jnp.float32)
        wide = jnp.concatenate([block, tail], 1)
        rows = [wide[:, q * points:q * points + LANES] for q in range(ys)]
        return jnp.swapaxes(jnp.stack(rows, 0), 0, 1)

    def lanes_together(block):
        block = jnp.swapaxes(block, 0, 1)
        return jnp.concatenate([block[q][:, :points] for q in range(ys)], 1)

    def side_by_side(block):
        return jnp.concatenate([block[i] for i in range(per_step)], 1)

    @pl.when(active & (at < X_STEPS))
    def forward_x():
        chunk = at

        def first_waits():
            fetch("a0", chunk).wait()
            fetch("b", chunk).wait()

        when_job(0, first_waits)
        for number in range(1, jobs):
            when_job(number, fetch(a_names[number], chunk).wait)
        spectrum = from_left(left_ref[...], here("a", chunk) * here("b", chunk))
        start = pl.multiple_of(chunk * ys, ys)
        held[:, pl.ds(start, ys), :] = lanes_apart(spectrum)

    @pl.when(active & (at >= X_STEPS) & (at < late))
    def planes():
        part = at - X_STEPS
        left = left_ref[...]
        right = right_ref[...]
        first = part * per_step
        when_job(0, lambda: fetch_kernel(part).wait())
        block = held[pl.ds(first, per_step)].reshape(per_step * points, LANES)
        block = from_right(block, right).reshape(per_step, points, LANES)
        wide = from_left(left, side_by_side(block))
        wide = from_left(left, wide * side_by_side(near_kernel[pl.ds(first, per_step)]))
        block = jnp.concatenate(
            [wide[:, i * LANES:(i + 1) * LANES] for i in range(per_step)], 0
        )
        block = from_right(block, right)
        held[pl.ds(first, per_step)] = block.reshape(per_step, points, LANES)

    @pl.when(active & (at >= late))
    def inverse_x():
        chunk = at - late
        start = pl.multiple_of(chunk * ys, ys)
        if "sum_a" in has:
            fetch("sum_a", chunk).wait()
        block = lanes_together(held[:, pl.ds(start, ys), :])
        potential = from_left(left_ref[...], block)
        for_a = here("b", chunk) * potential
        if "sum_a" in has:
            for_a = for_a + jnp.where(with_sum, here("sum_a", chunk), 0.0)
        near_out[job, :, span_of(chunk)] = for_a
        if "for_b" in has:
            for_b = here("a", chunk) * potential
            if jobs > 1:
                for_b = for_b + jnp.where(job > 0, near_out[jobs, :, span_of(chunk)], 0.0)
            near_out[jobs, :, span_of(chunk)] = for_b

        def give_all(number):
            for name in outs:
                if number == (jobs - 1 if name == "for_b" else int(name[-1])):
                    give(name, chunk).start()

        for number in range(jobs):
            when_job(number, functools.partial(give_all, number))

    @pl.when(active & (step == jobs * steps - 1))
    def wait_outs():
        for chunk in range(X_STEPS):
            for name in outs:
                give(name, chunk).wait()


def pair_terms(
    flags, slot, a, b, constants, sum_a=None, for_b=False, halves=False, in_place=False, then=None,
    plane_steps=2,
):
    points, plane = b.shape
    kernel, left, right = constants
    jobs = len(a)
    blocks = [*a, b] + [sum_a] * (sum_a is not None)
    waited = [] if then is None else [then]
    has = ["sum_a"] * (sum_a is not None) + ["for_b"] * for_b + ["halves"] * halves + ["then"] * len(waited)
    rows = ([points - FAR_ROWS, FAR_ROWS] if halves else [points] * jobs) + [points] * for_b
    anywhere = pl.BlockSpec(memory_space=pl.ANY)
    return pl.pallas_call(
        functools.partial(pair_body, points, slot, jobs, plane_steps, has),
        grid=(jobs * (2 * X_STEPS + plane_steps),),
        in_specs=[pl.BlockSpec(memory_space=pltpu.SMEM)]
        + [anywhere] * (len(blocks) + len(waited) + 1)
        + [pl.BlockSpec(table.shape, lambda i: (0, 0)) for table in (left, right)],
        out_specs=[anywhere] * len(rows),
        out_shape=[jax.ShapeDtypeStruct((n, plane), jnp.float32) for n in rows],
        input_output_aliases={3: 0} if in_place else {},
        scratch_shapes=[
            pltpu.VMEM((points, points, LANES), jnp.float32),
            pltpu.VMEM((len(blocks), points, plane), jnp.float32),
            pltpu.VMEM((points, points, LANES), jnp.float32),
            pltpu.VMEM((jobs + for_b, points, plane), jnp.float32),
            pltpu.SemaphoreType.DMA((len(blocks), X_STEPS)),
            pltpu.SemaphoreType.DMA((plane_steps,)),
            pltpu.SemaphoreType.DMA((len(rows), X_STEPS)),
        ],
        compiler_params=pltpu.CompilerParams(vmem_limit_bytes=63 * 2**20),
        cost_estimate=pl.CostEstimate(
            flops=100_000_000, bytes_accessed=1_000_000, transcendentals=0
        ),
        name="pair_terms",
    )(flags, *blocks, *waited, kernel, left, right)


def copy_body(flags_ref, kernel_ref, left_ref, right_ref, block_ref, first_ref, second_ref):
    del flags_ref, kernel_ref, left_ref, right_ref
    first_ref[...] = block_ref[...]
    second_ref[...] = block_ref[...]


def copied(flags, constants, block):
    points, plane = block.shape
    part = pl.BlockSpec((points, plane // X_STEPS), lambda i: (0, i))
    return pl.pallas_call(
        copy_body,
        grid=(X_STEPS,),
        in_specs=[
            pl.BlockSpec(memory_space=pltpu.SMEM),
            *[pl.BlockSpec(memory_space=pl.ANY)] * 3,
            part,
        ],
        out_specs=[part, part],
        out_shape=[jax.ShapeDtypeStruct(block.shape, block.dtype)] * 2,
        compiler_params=pltpu.CompilerParams(vmem_limit_bytes=63 * 2**20),
        name="copied",
    )(flags, *constants, block)


def gate_body(*refs):
    del refs


def gate(token, kernel, partner, block):
    anywhere = pl.BlockSpec(memory_space=pl.ANY)
    return pl.pallas_call(
        gate_body,
        in_specs=[anywhere] * 4,
        out_specs=[anywhere] * 2,
        out_shape=[
            jax.ShapeDtypeStruct(kernel.shape, kernel.dtype),
            jax.ShapeDtypeStruct(block.shape, block.dtype),
        ],
        input_output_aliases={1: 0, 3: 1},
        compiler_params=pltpu.CompilerParams(vmem_limit_bytes=63 * 2**20),
        name="gate",
    )(token, kernel, partner, block)


def hold_body(*refs):
    del refs


def hold(block, *then):
    anywhere = pl.BlockSpec(memory_space=pl.ANY)
    return pl.pallas_call(
        hold_body,
        in_specs=[anywhere] * (1 + len(then)),
        out_specs=anywhere,
        out_shape=jax.ShapeDtypeStruct(block.shape, block.dtype),
        input_output_aliases={0: 0},
        compiler_params=pltpu.CompilerParams(vmem_limit_bytes=63 * 2**20),
        name="hold",
    )(block, *then)


def settle_body(wanted, count, flags_ref, *refs):
    parts, (out_ref, near, sems) = refs[:count], refs[count + 1:]
    columns = out_ref.shape[1] // SETTLE_STEPS

    @pl.when(flags_ref[RESULT] == wanted)
    def move():
        copies = []
        for i in range(SETTLE_STEPS):
            span = pl.ds(i * columns, columns)
            start = 0
            for j, part in enumerate(parts):
                rows = pl.ds(start, part.shape[0])
                start += part.shape[0]
                copies.append((
                    pltpu.make_async_copy(part.at[:, span], near.at[rows, span], sems.at[0, j, i]),
                    pltpu.make_async_copy(near.at[rows, span], out_ref.at[rows, span], sems.at[1, j, i]),
                ))
        for inward, outward in copies:
            inward.start()
        for inward, outward in copies:
            inward.wait()
            outward.start()
        for inward, outward in copies:
            outward.wait()


def settle(flags, wanted, parts, own_sum):
    anywhere = pl.BlockSpec(memory_space=pl.ANY)
    count = len(parts)
    return pl.pallas_call(
        functools.partial(settle_body, wanted, count),
        in_specs=[pl.BlockSpec(memory_space=pltpu.SMEM)] + [anywhere] * (count + 1),
        out_specs=anywhere,
        out_shape=jax.ShapeDtypeStruct(own_sum.shape, own_sum.dtype),
        input_output_aliases={count + 1: 0},
        scratch_shapes=[
            pltpu.VMEM(own_sum.shape, own_sum.dtype),
            pltpu.SemaphoreType.DMA((2, count, SETTLE_STEPS)),
        ],
        compiler_params=pltpu.CompilerParams(vmem_limit_bytes=63 * 2**20),
        name="settle",
    )(flags, *parts, own_sum)


def both_halves(*pairs):
    return list(pairs) + [(15 - source, 15 - target) for source, target in pairs]


CROSSING = both_halves((3, 14), (4, 9))
PARTNERS = both_halves((8, 14), (15, 9), (9, 11), (14, 12))
ARRIVED = both_halves((14, 2), (9, 5))
SINGLES = both_halves((5, 10), (2, 13))
BESIDE = both_halves((13, 14), (10, 9))
DIRECT = both_halves((15, 10), (8, 13))
TURNED = both_halves((11, 14), (12, 9))
HOME_ACROSS = both_halves((9, 4), (14, 3))
HOME_FAR = both_halves((9, 15), (14, 8))
HOME_TURN = both_halves((9, 11), (14, 12))
HOME_TURNED = both_halves((11, 15), (12, 8))
RESULT = 10
FLAGS = {i: (1, 0, 1, 1, 0, 0, 0, 0, 1, 1, 0) for i in (9, 14, 6, 1)}
FLAGS.update({i: (0, 0, 0, 0, 1, 0, 1, 1, 0, 0, 0) for i in (10, 13, 5, 2)})
FLAGS.update({i: (0,) * RESULT + (1,) for i in (3, 4, 11, 12)})
FLAGS.update({i: (0,) * RESULT + (2,) for i in (15, 8, 0, 7)})


def sixteen_bands(orbitals, constants):
    def send(value, pairs):
        return lax.ppermute(value[None], "band", pairs)[0]

    kernel, left, right = constants
    own = orbitals[0]
    flags = jnp.asarray([FLAGS[i] for i in range(16)], jnp.int32)
    flags = flags[lax.axis_index("band")]
    pair = functools.partial(pair_terms, flags)
    crossed = send(own, CROSSING)
    partner = send(own, PARTNERS)
    own_copy, direct_copy = copied(flags, constants, own)
    token = hold(own_copy[:8, :LANES], crossed)
    direct = send(direct_copy, DIRECT)
    kernel, held_back = gate(send(token, ARRIVED), kernel, partner, own_copy)
    constants = (kernel, left, right)
    beside = send(held_back, BESIDE)
    single = send(held_back, SINGLES)

    partner_sum, own_sum, crossed_sum = pair(
        0, [partner, own], crossed, constants, for_b=True, then=direct, plane_steps=1
    )
    home = send(crossed_sum, HOME_ACROSS)
    partner = hold(partner, own_sum)
    turned = send(partner, TURNED)
    top, bottom = pair(1, [partner], beside, constants, sum_a=partner_sum, halves=True, plane_steps=1)
    bottom = send(bottom, HOME_TURN)
    top = send(top, HOME_FAR)
    (own_sum,) = pair(2, [own], direct, constants, sum_a=own_sum, in_place=True)
    (own_sum,) = pair(3, [own], single, constants, sum_a=own_sum, in_place=True)
    bottom = send(hold(bottom, own_sum), HOME_TURNED)
    own_sum = settle(flags, 1, [home], own_sum)
    (own_sum,) = pair(4, [own], turned, constants, sum_a=own_sum, in_place=True, plane_steps=1)
    return settle(flags, 2, [top, bottom], own_sum)[None]


def any_bands(orbitals, constants):
    own = orbitals[0]
    flags = jnp.ones((4,), jnp.int32)
    lower = from_behind(orbitals, "band", OFFSET)[0]
    upper = from_behind(orbitals, "band", -OFFSET)[0]
    (total,) = pair_terms(flags, 0, [own], lower, constants)
    return pair_terms(flags, 1, [own], upper, constants, sum_a=total)[0][None]


def local(bands, orbitals):
    points = orbitals.shape[1]
    constants = (screened_kernel(points), *hartley_tables(points))
    if bands == 16:
        return sixteen_bands(orbitals, constants)
    return any_bands(orbitals, constants)


def solution(mesh):
    return jax.shard_map(
        functools.partial(local, mesh.shape["band"]),
        mesh=mesh,
        in_specs=(P(("groups", "band"), None, None),),
        out_specs=P(("groups", "band"), None, None),
        check_vma=False,
    )
```
